32 devices in a mesh: pix: 16 (over z, x, core), col: 2 (over y).
Axes of the slice: x: 2, y: 2, z: 4, core: 2. Of those that a mesh axis runs over, the one named last changes fastest.
Arguments:
- observed: float32 [4096, 4096], P('pix', 'col'), may hold values from -40 to 40
- valid_mask: int32 [4096, 512], P('pix', 'col'), may hold values 0 or 1
- pix_factor: float32 [4096, 256], P('pix'), may hold values from -6 to 6
- col_factor: float32 [4096, 256], P('col'), may hold values from -0.375 to 0.375
Outputs:
- pix_next: float32 [4096, 256], P('pix')
- col_next: float32 [4096, 256], P('col')
- cloud: float32 [4096, 4096], P('pix', 'col')
The draws below stay inside these ranges and needn't reach their ends.
All inputs are finite; a program needn't handle non-finite values. No bound on the sum of `valid_mask` on one device may be relied on, other than what follows from the above.
Results may differ from the reference program's by a relative error of at most 0.0003.
Values sent between devices are 32-bit elements; how exact they have to be, the bound alone decides.
No kernel may reach another device: no remote copies, remote signals or barrier semaphores. Data moves between devices by JAX's collectives and lax.ppermute only.
A program may use at most 64 MiB of HBM per device.

```python
import jax
import jax.numpy as jnp
from jax import lax

C = 4096
R = 256
BANDS = 8
WIDTH = 256
ITERS = 2
PASSES = 2
P_SIZE = 4096
DATES = 512


def draw_observed(key, part):
    key_rows, key_cols, key_noise = jax.random.split(jax.random.fold_in(key, 11), 3)
    row_scale = jnp.exp(jax.random.uniform(key_rows, (P_SIZE, 1), jnp.float32, jnp.log(0.2), jnp.log(2.0)))
    ramp = 3.0 ** (jnp.arange(P_SIZE, dtype=jnp.float32) / (P_SIZE - 1))
    col_scale = jnp.exp(jax.random.uniform(key_cols, (1, C), jnp.float32, jnp.log(0.2), jnp.log(2.0)))
    noise = jnp.clip(jax.random.normal(key_noise, (P_SIZE, C), jnp.float32), -3.3, 3.3)
    values = 0.5 * row_scale * ramp[:, None] * col_scale * noise
    return jnp.clip(values, -40.0, 40.0).astype(jnp.float32)


def plant(entries, key, low, high):
    shape = entries.shape
    place = [jax.random.randint(jax.random.fold_in(key, axis), (), 0, shape[axis]) for axis in range(len(shape))]
    entries = entries.at[tuple(place)].set(low)
    longest = shape.index(max(shape))
    place[longest] = (place[longest] + 1) % shape[longest]
    return entries.at[tuple(place)].set(high)


def shard_levels(rng, shape, shards, least, largest):
    def one(dim, blocks):
        heights = jax.random.uniform(jax.random.fold_in(jax.random.fold_in(rng, 6), dim), (blocks,), jnp.float32, least / len(shards), largest / len(shards))
        return jnp.repeat(jnp.exp(heights), shape[dim] // blocks).reshape((-1,) + (1,) * (len(shape) - dim - 1))

    loudness = one(*shards[0])
    for cut in shards[1:]:
        loudness = loudness * one(*cut)
    return loudness


def scatter_about(key, shape, deviation, limit, pieces=(), kind=jnp.bfloat16):
    array = deviation * jax.random.normal(key, shape, jnp.float32)
    if pieces:
        array = array * shard_levels(key, shape, pieces, -0.22, 0.18)
    return jnp.clip(array, -limit, limit).astype(kind)


def setup_inputs(seed: int = 0) -> dict:
    arg_keys = jax.random.split(jax.random.key(seed), 5)
    observed = draw_observed(jax.random.fold_in(arg_keys[4], 71), 0)
    valid_mask = plant((jax.random.randint(arg_keys[1], (P_SIZE, DATES), 0, 10) < 7).astype(jnp.int32), jax.random.fold_in(arg_keys[1], 1), 0, 1)
    pix_factor = scatter_about(arg_keys[2], (P_SIZE, R), 1.0, 6.0, ((0, 16),), jnp.float32)
    col_factor = scatter_about(arg_keys[3], (C, R), R ** -0.5, 0.375, ((0, 2),), jnp.float32)
    return {"observed": observed, "valid_mask": valid_mask, "pix_factor": pix_factor, "col_factor": col_factor}


highest = lax.Precision.HIGHEST
threshold_scale = 1.0
diffusion = 0.2

def soft_cut(values, level):
    return jnp.sign(values) * jnp.maximum(jnp.abs(values) - level, 0.0)

def flux_of(diff, level):
    return diff / (1.0 + (diff / level) ** 2)

def level_of(residual, weight, total):
    return threshold_scale * jnp.sqrt(jnp.sum(weight * residual * residual) / total + 1e-06)

def reference(observed, valid_mask, pix_factor, col_factor):
    weight = jnp.repeat(valid_mask.astype(jnp.float32), BANDS, axis=1)
    total = float(observed.shape[0] * observed.shape[1])
    pix_fac = pix_factor
    col_fac = col_factor
    low_rank = jnp.dot(pix_fac, col_fac.T, precision=highest)
    for iteration in range(ITERS):
        residual = observed - low_rank
        level = level_of(residual, weight, total)
        sparse = weight * soft_cut(residual, level)
        misfit = weight * (sparse - residual)
        pix_grad = jnp.dot(misfit, col_fac, precision=highest)
        change = jnp.dot(pix_grad, col_fac.T, precision=highest)
        step_pix = jnp.sum(pix_grad * pix_grad) / jnp.sum(weight * change * change)
        pix_fac = pix_fac - step_pix * pix_grad
        low_rank = low_rank - step_pix * change
        misfit = weight * (sparse - (observed - low_rank))
        col_grad = jnp.dot(misfit.T, pix_fac, precision=highest)
        shifted = jnp.dot(pix_fac, col_grad.T, precision=highest)
        step_col = jnp.sum(col_grad * col_grad) / jnp.sum(weight * shifted * shifted)
        col_fac = col_fac - step_col * col_grad
        low_rank = low_rank - step_col * shifted
    residual = observed - low_rank
    level = level_of(residual, weight, total)
    layer = weight * soft_cut(residual, level)
    grid = layer.reshape(observed.shape[0] // WIDTH, WIDTH, -1)
    for sweep_index in range(PASSES):
        padded = jnp.pad(grid, ((1, 1), (1, 1), (0, 0)), mode='edge')
        summed = flux_of(padded[:-2, 1:-1] - grid, level) + flux_of(padded[2:, 1:-1] - grid, level)
        summed = summed + flux_of(padded[1:-1, :-2] - grid, level) + flux_of(padded[1:-1, 2:] - grid, level)
        grid = grid + diffusion * summed
    cloud = grid.reshape(layer.shape)
    return (pix_fac, col_fac, cloud)
```

```python
import functools

import jax
import jax.numpy as jnp
from jax import lax
from jax.experimental import pallas as pl
from jax.experimental.pallas import tpu as pltpu
from jax.sharding import PartitionSpec as P

BANDS = 8
WIDTH = 256
ITERS = 2
PASSES = 2
LANES = 128
GROUP = 8

threshold_scale = 1.0
diffusion = 0.2
f32 = jnp.float32
bf16 = jnp.bfloat16


def along_pix(block, distance):
    count = lax.axis_size("pix")
    return lax.ppermute(block, "pix", [(i, i ^ distance) for i in range(count)])


def to_chip(block, distance, crossed):
    count = lax.axis_size("pix")
    route = [(i, (i ^ crossed) + 2 * distance) for i in range(count)]
    route = [(a, b) for a, b in route if 0 <= b < count]
    return lax.ppermute(block, "pix", route)


def summed_over_col(block):
    count = lax.axis_size("col")
    step = 1
    while step < count:
        block = block + lax.ppermute(block, "col", [(i, i ^ step) for i in range(count)])
        step *= 2
    return block


def everywhere(rows):
    return lax.all_to_all(rows, ("pix", "col"), 0, 0, tiled=True)


def halves(x):
    high = x.astype(bf16)
    return high, (x - high.astype(f32)).astype(bf16)


def product(a, b, dims=((1,), (0,))):
    def part(x, y):
        return lax.dot_general(x, y, (dims, ((), ())), preferred_element_type=f32)

    return part(a[0], b[0]) + (part(a[0], b[1]) + part(a[1], b[0]))


def rows_folded(x):
    return jnp.sum(x.reshape(x.shape[0] // 8, 8, x.shape[1]), axis=0)


def whole_sum(x):
    return jnp.sum(jnp.sum(x, axis=0, keepdims=True), axis=1, keepdims=True)


def packed_sums(shape, sums):
    lane = lax.broadcasted_iota(jnp.int32, shape, 1)
    packed = jnp.zeros(shape, f32)
    for place, value in enumerate(sums):
        packed = packed + jnp.where(lane == place, value, 0.0)
    return packed


def read_sums(ref, count):
    total = jnp.sum(ref[...], axis=0, keepdims=True)
    return [total[:, k : k + 1] for k in range(count)]


def spread_mask(mask, chunk):
    dates = mask.shape[1]
    date = lax.broadcasted_iota(jnp.int32, (dates, LANES), 0)
    lane = lax.broadcasted_iota(jnp.int32, (dates, LANES), 1)
    pick = (date == chunk * (LANES // BANDS) + lane // BANDS).astype(bf16)
    return jnp.dot(mask.astype(bf16), pick, preferred_element_type=f32)


def call(kernel, grid, in_specs, out_specs, out_shape, scratch, place, *args):
    return pl.pallas_call(
        kernel,
        grid_spec=pltpu.PrefetchScalarGridSpec(
            num_scalar_prefetch=1,
            grid=grid,
            in_specs=in_specs,
            out_specs=out_specs,
            scratch_shapes=scratch,
        ),
        out_shape=out_shape,
        compiler_params=pltpu.CompilerParams(vmem_limit_bytes=48 * 2**20),
    )(place, *args)


def whole(shape):
    return pl.BlockSpec(shape, lambda t, s: (0,) * len(shape))


def tile(rows, cols):
    return pl.BlockSpec((rows, cols), lambda t, s: (0, t))


def shaped(*shape):
    return jax.ShapeDtypeStruct(shape, f32)


def start_kernel(place, own_obs, own_mask, other_obs, other_mask, own_u, other_u, v_ref,
                 res_ref, weight_ref, vt_ref, sums_ref, u_high, u_low, acc):
    step = pl.program_id(0)
    chunk = place[1] ^ step
    pixels = own_u.shape[0]

    @pl.when(step == 0)
    def _():
        for part, ref in enumerate((own_u, other_u)):
            high, low = halves(ref[...])
            u_high[part * pixels : (part + 1) * pixels] = high
            u_low[part * pixels : (part + 1) * pixels] = low
        acc[...] = jnp.zeros_like(acc)

    vt = v_ref[...].T
    vt_ref[...] = vt
    low_rank = product((u_high[...], u_low[...]), halves(vt))
    for part, (obs, mask) in enumerate(((own_obs, own_mask), (other_obs, other_mask))):
        rows = slice(part * pixels, (part + 1) * pixels)
        weight = spread_mask(mask[...], chunk)
        res = weight * (obs[...] - low_rank[rows])
        weight_ref[rows] = weight
        res_ref[rows] = res
        acc[...] += rows_folded(res * res)

    @pl.when(step == pl.num_programs(0) - 1)
    def _():
        sums_ref[...] = packed_sums(sums_ref.shape, [whole_sum(acc[...])])


def level_from(spread, total):
    return threshold_scale * jnp.sqrt(jnp.maximum(spread, 0.0) / total + 1e-06)


def first_grad_kernel(total, place, sums_ref, res_ref, vt_ref, grad_ref):
    step = pl.program_id(0)
    (spread,) = read_sums(sums_ref, 1)
    level = level_from(spread, total)
    misfit = -jnp.clip(res_ref[...], -level, level)
    part = product(halves(misfit), halves(vt_ref[...]), ((1,), (1,)))

    @pl.when(step == 0)
    def _():
        grad_ref[...] = part

    @pl.when(step > 0)
    def _():
        grad_ref[...] += part


def column_sums(sums):
    top, curve, cross, before = sums
    step = top / curve
    return step, before + 2.0 * step * cross + step * step * curve


def next_grad_kernel(total, place, sums_ref, res_ref, shift_ref, vt_ref, even_ref, odd_ref,
                     res_out, vt_out, grad_ref):
    step = pl.program_id(0)
    size, spread = column_sums(read_sums(sums_ref, 4))
    level = level_from(spread, total)
    grad = jnp.concatenate([even_ref[0], odd_ref[0]], axis=1)
    vt = vt_ref[...] - size * grad
    vt_out[...] = vt
    res = res_ref[...] + size * shift_ref[...]
    res_out[...] = res
    misfit = -jnp.clip(res, -level, level)
    part = product(halves(misfit), halves(vt), ((1,), (1,)))

    @pl.when(step == 0)
    def _():
        grad_ref[...] = part

    @pl.when(step > 0)
    def _():
        grad_ref[...] += part


def change_kernel(col_count, place, own_grad, other_grad, vt_ref, weight_ref,
                  change_ref, sums_ref, g_high, g_low, acc):
    step = pl.program_id(0)
    pixels = own_grad.shape[0]

    @pl.when(step == 0)
    def _():
        for part, ref in enumerate((own_grad, other_grad)):
            high, low = halves(ref[...])
            g_high[part * pixels : (part + 1) * pixels] = high
            g_low[part * pixels : (part + 1) * pixels] = low
        acc[...] = jnp.zeros_like(acc)

    change = weight_ref[...] * product((g_high[...], g_low[...]), halves(vt_ref[...]))
    change_ref[...] = change
    acc[...] += rows_folded(change * change)

    @pl.when(step == pl.num_programs(0) - 1)
    def _():
        top = whole_sum(own_grad[...] * own_grad[...]) / col_count
        sums_ref[...] = packed_sums(sums_ref.shape, [top, whole_sum(acc[...])])


def pix_step_kernel(total, first, place, level_sums, sums_ref, u_ref, own_grad, other_grad, res_ref,
                    change_ref, u_out, res_out, even_ref, odd_ref, u_high, u_low):
    step = pl.program_id(0)
    pixels = own_grad.shape[0]
    top, curve = read_sums(sums_ref, 2)
    size = top / curve
    if first:
        (spread,) = read_sums(level_sums, 1)
    else:
        _, spread = column_sums(read_sums(level_sums, 4))
    level = level_from(spread, total)

    @pl.when(step == 0)
    def _():
        for part, ref in enumerate((own_grad, other_grad)):
            rows = slice(part * pixels, (part + 1) * pixels)
            u = u_ref[rows] - size * ref[...]
            u_out[rows] = u
            high, low = halves(u)
            u_high[rows] = high
            u_low[rows] = low

    res = res_ref[...]
    moved = size * change_ref[...]
    res_out[...] = res + moved
    misfit = -(jnp.clip(res, -level, level) + moved)
    grad = product((u_high[...], u_low[...]), halves(misfit), ((0,), (0,)))
    even_ref[0] = grad[:, :LANES]
    odd_ref[0] = grad[:, LANES:]


def shift_kernel(chips, place, u_ref, even_ref, odd_ref, weight_ref, res_ref,
                 shift_ref, sums_ref, u_high, u_low, acc, acc_top):
    step = pl.program_id(0)

    @pl.when(step == 0)
    def _():
        high, low = halves(u_ref[...])
        u_high[...] = high
        u_low[...] = low
        acc[...] = jnp.zeros_like(acc)
        acc_top[...] = jnp.zeros_like(acc_top)

    grad = jnp.concatenate([even_ref[0], odd_ref[0]], axis=1)
    acc_top[...] += rows_folded(grad * grad)
    shift = weight_ref[...] * product((u_high[...], u_low[...]), halves(grad))
    shift_ref[...] = shift
    res = res_ref[...]
    acc[0] += rows_folded(shift * shift)
    acc[1] += rows_folded(shift * res)
    acc[2] += rows_folded(res * res)

    @pl.when(step == pl.num_programs(0) - 1)
    def _():
        sums = [whole_sum(acc_top[...]) / chips] + [whole_sum(acc[k]) for k in range(3)]
        sums_ref[...] = packed_sums(sums_ref.shape, sums)


def rim_kernel(place, *refs):
    obs = refs[0:4]
    mask = refs[4:8]
    u_north, u_south, vt_ref, res_ref, weight_ref, u_high, u_low = refs[8:]
    step = pl.program_id(0)
    chunk = place[1] ^ step
    pixels = obs[0].shape[0]

    @pl.when(step == 0)
    def _():
        for part, ref in enumerate((u_north, u_south)):
            rows = slice(2 * part * pixels, 2 * (part + 1) * pixels)
            high, low = halves(ref[...])
            u_high[rows] = high
            u_low[rows] = low

    low_rank = product((u_high[...], u_low[...]), halves(vt_ref[...]))
    for part in range(4):
        weight = spread_mask(mask[part][...], chunk)
        weight_ref[part] = weight
        res_ref[part] = weight * (obs[part][...] - low_rank[part * pixels : (part + 1) * pixels])


def flux_of(diff, inverse):
    ratio = diff * inverse
    return diff / (1.0 + ratio * ratio)


def smooth_kernel(total, chips, place, sums_ref, res_ref, shift_ref, rim_ref, rim_weight, u_north, u_south,
                  grad_ref, own_ref, other_ref, u_high, u_low):
    step = pl.program_id(0)
    core, chip = place[0], place[2]
    pixels = own_ref.shape[0]

    @pl.when(step == 0)
    def _():
        for part, ref in enumerate((u_north, u_south)):
            rows = slice(2 * part * pixels, 2 * (part + 1) * pixels)
            high, low = halves(ref[...])
            u_high[rows] = high
            u_low[rows] = low

    size, spread = column_sums(read_sums(sums_ref, 4))
    level = level_from(spread, total)
    inverse = 1.0 / level
    rim_shift = product((u_high[...], u_low[...]), halves(grad_ref[0]))
    shifts = rim_shift.reshape(4, pixels, LANES)

    def cut(res):
        return res - jnp.clip(res, -level, level)

    own = [cut(res_ref[k] + size * shift_ref[k]) for k in range(2)]
    rim = [cut(rim_ref[k] + size * (rim_weight[k] * shifts[k])) for k in range(4)]

    def ordered(pair):
        return [jnp.where(core == 0, pair[0], pair[1]), jnp.where(core == 0, pair[1], pair[0])]

    rows = ordered(rim[0:2]) + ordered(own) + ordered(rim[2:4])
    keep_north = jnp.where(chip > 0, 1.0, 0.0).astype(f32)
    keep_south = jnp.where(chip < chips - 1, 1.0, 0.0).astype(f32)
    last = lax.broadcasted_iota(jnp.int32, (pixels, LANES), 0) % WIDTH == WIDTH - 1
    scaled = diffusion

    def smoothed(rows, north_edge, south_edge):
        count = len(rows)
        cross = []
        for k in range(count - 1):
            flux = flux_of(rows[k + 1] - rows[k], inverse)
            if k == north_edge:
                flux = flux * keep_north
            if k == south_edge:
                flux = flux * keep_south
            cross.append(flux)
        out = []
        for k in range(1, count - 1):
            east = jnp.where(last, 0.0, flux_of(pltpu.roll(rows[k], pixels - 1, 0) - rows[k], inverse))
            along = east - pltpu.roll(east, 1, 0)
            out.append(rows[k] + scaled * ((cross[k] - cross[k - 1]) + along))
        return out

    rows = smoothed(rows, 1, 3)
    rows = smoothed(rows, 0, 2)
    even, odd = rows
    own_ref[...] = jnp.where(core == 0, even, odd)
    other_ref[...] = jnp.where(core == 0, odd, even)


def factor_kernel(place, sums_ref, vt_ref, grad_ref, out_ref):
    size, _ = column_sums(read_sums(sums_ref, 4))
    out_ref[...] = (vt_ref[...] - size * grad_ref[0]).T


def grad_over_chips(even, odd):
    chips = lax.axis_size("pix") // 2
    kept = even + along_pix(odd, 2)
    mine = kept[0]
    for part in [along_pix(kept[k], 4 * k) for k in (1, 2, 3)]:
        mine = mine + part
    distance = GROUP
    while distance < chips:
        mine = mine + along_pix(mine, 2 * distance)
        distance *= 2
    even = jnp.stack([mine] + [along_pix(mine, 4 * k) for k in (1, 2, 3)])
    return even, along_pix(even, 2)


def per_device(observed, valid_mask, pix_factor, col_factor):
    pix_count = lax.axis_size("pix")
    col_count = lax.axis_size("col")
    devices = pix_count * col_count
    chips = pix_count // 2
    pixels, columns = observed.shape
    rank = pix_factor.shape[1]
    half = columns // 2
    dates = valid_mask.shape[1] // 2
    total = float(pixels * columns * pix_count * col_count)
    assert pixels == WIDTH and half == GROUP * LANES and chips % GROUP == 0 and PASSES == 2
    index = lax.axis_index("pix")
    core = index % 2
    chip = index // 2
    place = jnp.stack([core, chip % GROUP, chip]).astype(jnp.int32)

    def half_of(which):
        obs = lax.dynamic_slice(observed, (0, which * half), (pixels, half))
        mask = lax.dynamic_slice(valid_mask, (0, which * dates), (pixels, dates))
        return jnp.concatenate([obs, mask.astype(f32)], axis=1)

    other_half = half_of(1 - core)
    own_half = half_of(core)
    received = along_pix(other_half, 1)
    other_factor = along_pix(pix_factor, 1)
    rims = [
        to_chip(own_half, 1, 0), to_chip(other_half, 1, 1),
        to_chip(own_half, -1, 0), to_chip(other_half, -1, 1),
    ]

    both = 2 * pixels
    wide = 2 * LANES
    steps = half // wide
    chunk_in = pl.BlockSpec((pixels, LANES), lambda t, s: (0, s[1] ^ t))
    mask_in = pl.BlockSpec((pixels, dates), lambda t, s: (0, half // dates))
    sums_shape = (devices, LANES)
    pix_block = whole((pixels, rank))
    both_block = whole((both, rank))
    sums_block = whole(sums_shape)
    tile_block = tile(both, wide)
    vt_block = tile(rank, wide)
    grad_block = pl.BlockSpec((1, rank, LANES), lambda t, s: (t, 0, 0))
    local = shaped(both, half)
    factor_scratch = [pltpu.VMEM((both, rank), bf16)] * 2

    residual, weight, vt, sums = call(
        start_kernel, (GROUP,),
        [chunk_in, mask_in, chunk_in, mask_in, pix_block, pix_block,
         pl.BlockSpec((LANES, rank), lambda t, s: (s[0] * GROUP + (s[1] ^ t), 0))],
        [tile(both, LANES), tile(both, LANES), tile(rank, LANES), sums_block],
        [local, local, shaped(rank, half), shaped(*sums_shape)],
        factor_scratch + [pltpu.VMEM((8, LANES), f32)],
        place, own_half, own_half, received, received, pix_factor, other_factor, col_factor,
    )
    level_sums = everywhere(sums)
    u = jnp.concatenate([pix_factor, other_factor], axis=0)

    for iteration in range(ITERS):
        if iteration == 0:
            partial = call(
                functools.partial(first_grad_kernel, total), (steps,),
                [sums_block, tile_block, vt_block], both_block, shaped(both, rank), [],
                place, level_sums, residual, vt,
            )
        else:
            residual, vt, partial = call(
                functools.partial(next_grad_kernel, total), (steps,),
                [sums_block, tile_block, tile_block, vt_block, grad_block, grad_block],
                [tile_block, vt_block, both_block],
                [local, shaped(rank, half), shaped(both, rank)], [],
                place, level_sums, residual, shift, vt, even, odd,
            )
        own_grad = summed_over_col(partial[:pixels] + along_pix(partial[pixels:], 1))
        other_grad = along_pix(own_grad, 1)
        change, sums = call(
            functools.partial(change_kernel, col_count), (steps,),
            [pix_block, pix_block, vt_block, tile_block], [tile_block, sums_block],
            [local, shaped(*sums_shape)], factor_scratch + [pltpu.VMEM((8, wide), f32)],
            place, own_grad, other_grad, vt, weight,
        )
        pix_sums = everywhere(sums)
        u, residual, even, odd = call(
            functools.partial(pix_step_kernel, total, iteration == 0), (steps,),
            [sums_block, sums_block, both_block, pix_block, pix_block, tile_block, tile_block],
            [both_block, tile_block, grad_block, grad_block],
            [shaped(both, rank), local, shaped(steps, rank, LANES), shaped(steps, rank, LANES)],
            factor_scratch,
            place, level_sums, pix_sums, u, own_grad, other_grad, residual, change,
        )
        even, odd = grad_over_chips(even, odd)
        shift, sums = call(
            functools.partial(shift_kernel, chips), (steps,),
            [both_block, grad_block, grad_block, tile_block, tile_block], [tile_block, sums_block],
            [local, shaped(*sums_shape)],
            factor_scratch + [pltpu.VMEM((3, 8, wide), f32), pltpu.VMEM((8, wide), f32)],
            place, u, even, odd, weight, residual,
        )
        level_sums = everywhere(sums)

    u_north = to_chip(u, 1, 0)
    u_south = to_chip(u, -1, 0)
    rim_block = pl.BlockSpec((4, pixels, LANES), lambda t, s: (0, 0, t))
    rim_scratch = [pltpu.VMEM((2 * both, rank), bf16)] * 2
    rim_res, rim_weight = call(
        rim_kernel, (GROUP,),
        [chunk_in] * 4 + [mask_in] * 4 + [both_block, both_block, tile(rank, LANES)],
        [rim_block, rim_block], [shaped(4, pixels, half)] * 2, rim_scratch,
        place, *rims, *rims, u_north, u_south, vt,
    )
    grad = jnp.stack([even, odd], axis=1).reshape(GROUP, rank, LANES)
    pair_block = pl.BlockSpec((2, pixels, LANES), lambda t, s: (0, 0, t))
    own_cloud, other_cloud = call(
        functools.partial(smooth_kernel, total, chips), (GROUP,),
        [sums_block, pair_block, pair_block, rim_block, rim_block, both_block, both_block, grad_block],
        [chunk_in, chunk_in], [shaped(pixels, half)] * 2, rim_scratch,
        place, level_sums, residual.reshape(2, pixels, half), shift.reshape(2, pixels, half),
        rim_res, rim_weight, u_north, u_south, grad,
    )
    own_v = call(
        factor_kernel, (GROUP,),
        [sums_block, tile(rank, LANES), grad_block],
        pl.BlockSpec((LANES, rank), lambda t, s: (s[1] ^ t, 0)), shaped(half, rank), [],
        place, level_sums, vt, grad,
    )
    other_v = along_pix(own_v, 1)
    from_other = along_pix(other_cloud, 1)

    def joined(own, other, axis):
        pair = [jnp.where(core == 0, own, other), jnp.where(core == 0, other, own)]
        return jnp.concatenate(pair, axis=axis)

    return u[:pixels], joined(own_v, other_v, 0), joined(own_cloud, from_other, 1)


def solution(mesh):
    in_specs = (P("pix", "col"), P("pix", "col"), P("pix", None), P("col", None))
    out_specs = (P("pix", None), P("col", None), P("pix", "col"))
    return jax.shard_map(
        per_device, mesh=mesh, in_specs=in_specs, out_specs=out_specs, check_vma=False
    )
```

```python
import functools

import jax
import jax.numpy as jnp
from jax import lax
from jax.experimental import pallas as pl
from jax.experimental.pallas import tpu as pltpu
from jax.sharding import PartitionSpec as P

BANDS = 8
WIDTH = 256
ITERS = 2
PASSES = 2
LANES = 128
GROUP = 8

threshold_scale = 1.0
diffusion = 0.2
f32 = jnp.float32
bf16 = jnp.bfloat16


def along_pix(block, distance):
    count = lax.axis_size("pix")
    return lax.ppermute(block, "pix", [(i, i ^ distance) for i in range(count)])


def to_odd_or_even(block, far, crossed):
    count = lax.axis_size("pix")
    route = []
    for i in range(count):
        chip = i // 2
        target = ((chip + 1) ^ 1) - 1 if far else chip ^ 1
        if 0 <= target < count // 2:
            route.append((i, 2 * target + (i % 2 ^ crossed)))
    return lax.ppermute(block, "pix", route)


def summed_over_col(block):
    count = lax.axis_size("col")
    step = 1
    while step < count:
        block = block + lax.ppermute(block, "col", [(i, i ^ step) for i in range(count)])
        step *= 2
    return block


def everywhere(rows):
    return lax.all_to_all(rows, ("pix", "col"), 0, 0, tiled=True)


def halves(x):
    high = x.astype(bf16)
    return high, (x - high.astype(f32)).astype(bf16)


def product(a, b, dims=((1,), (0,))):
    def part(x, y):
        return lax.dot_general(x, y, (dims, ((), ())), preferred_element_type=f32)

    return part(a[0], b[0]) + (part(a[0], b[1]) + part(a[1], b[0]))


def rows_folded(x):
    return jnp.sum(x.reshape(x.shape[0] // 8, 8, x.shape[1]), axis=0)


def whole_sum(x):
    return jnp.sum(jnp.sum(x, axis=0, keepdims=True), axis=1, keepdims=True)


def packed_sums(shape, sums):
    lane = lax.broadcasted_iota(jnp.int32, shape, 1)
    packed = jnp.zeros(shape, f32)
    for place, value in enumerate(sums):
        packed = packed + jnp.where(lane == place, value, 0.0)
    return packed


def read_sums(ref, count):
    total = jnp.sum(ref[...], axis=0, keepdims=True)
    return [total[:, k : k + 1] for k in range(count)]


def spread_mask(mask, chunk):
    dates = mask.shape[1]
    date = lax.broadcasted_iota(jnp.int32, (dates, LANES), 0)
    lane = lax.broadcasted_iota(jnp.int32, (dates, LANES), 1)
    pick = (date == chunk * (LANES // BANDS) + lane // BANDS).astype(bf16)
    return jnp.dot(mask.astype(bf16), pick, preferred_element_type=f32)


def call(kernel, grid, in_specs, out_specs, out_shape, scratch, place, *args, after=(), through=()):
    single = not isinstance(out_shape, (list, tuple))
    if single:
        out_specs, out_shape = [out_specs], [out_shape]
    extra_in, extra_out = len(after) + len(through), len(through)
    inputs, outputs = len(in_specs), len(out_specs)
    anywhere = pl.BlockSpec(memory_space=pl.ANY)

    def body(place_ref, *refs):
        first = inputs + extra_in
        kernel(place_ref, *refs[:inputs], *refs[first : first + outputs], *refs[first + outputs + extra_out :])

    results = pl.pallas_call(
        body,
        grid_spec=pltpu.PrefetchScalarGridSpec(
            num_scalar_prefetch=1,
            grid=grid,
            in_specs=list(in_specs) + [anywhere] * extra_in,
            out_specs=list(out_specs) + [anywhere] * extra_out,
            scratch_shapes=scratch,
        ),
        out_shape=list(out_shape) + [jax.ShapeDtypeStruct(x.shape, x.dtype) for x in through],
        input_output_aliases={1 + inputs + len(after) + k: outputs + k for k in range(extra_out)},
        compiler_params=pltpu.CompilerParams(vmem_limit_bytes=48 * 2**20),
    )(place, *args, *after, *through)
    if through:
        return results[:outputs], results[outputs:]
    return results[0] if single else results


def held_until(array, *after):
    def body(*refs):
        pass

    anywhere = pl.BlockSpec(memory_space=pl.ANY)
    return pl.pallas_call(
        body,
        in_specs=[anywhere] * (1 + len(after)),
        out_specs=anywhere,
        out_shape=jax.ShapeDtypeStruct(array.shape, array.dtype),
        input_output_aliases={0: 0},
    )(array, *after)


def whole(shape):
    return pl.BlockSpec(shape, lambda t, s: (0,) * len(shape))


def tile(rows, cols):
    return pl.BlockSpec((rows, cols), lambda t, s: (0, t))


def shaped(*shape):
    return jax.ShapeDtypeStruct(shape, f32)


def start_kernel(place, own_obs, own_mask, other_obs, other_mask, own_u, other_u, v_ref,
                 res_ref, weight_ref, vt_ref, sums_ref, u_high, u_low, acc):
    step = pl.program_id(0)
    chunk = place[1] ^ step
    pixels = own_u.shape[0]

    @pl.when(step == 0)
    def _():
        for part, ref in enumerate((own_u, other_u)):
            high, low = halves(ref[...])
            u_high[part * pixels : (part + 1) * pixels] = high
            u_low[part * pixels : (part + 1) * pixels] = low
        acc[...] = jnp.zeros_like(acc)

    vt = v_ref[...].T
    vt_ref[...] = vt
    low_rank = product((u_high[...], u_low[...]), halves(vt))
    for part, (obs, mask) in enumerate(((own_obs, own_mask), (other_obs, other_mask))):
        rows = slice(part * pixels, (part + 1) * pixels)
        weight = spread_mask(mask[...], chunk)
        res = weight * (obs[...] - low_rank[rows])
        weight_ref[rows] = weight
        res_ref[rows] = res
        acc[...] += rows_folded(res * res)

    @pl.when(step == pl.num_programs(0) - 1)
    def _():
        sums_ref[...] = packed_sums(sums_ref.shape, [whole_sum(acc[...])])


def level_from(spread, total):
    return threshold_scale * jnp.sqrt(jnp.maximum(spread, 0.0) / total + 1e-06)


def first_grad_kernel(total, place, sums_ref, res_ref, vt_ref, grad_ref):
    step = pl.program_id(0)
    (spread,) = read_sums(sums_ref, 1)
    level = level_from(spread, total)
    misfit = -jnp.clip(res_ref[...], -level, level)
    part = product(halves(misfit), halves(vt_ref[...]), ((1,), (1,)))

    @pl.when(step == 0)
    def _():
        grad_ref[...] = part

    @pl.when(step > 0)
    def _():
        grad_ref[...] += part


def column_sums(sums):
    top, curve, cross, before = sums
    step = top / curve
    return step, before + 2.0 * step * cross + step * step * curve


def next_grad_kernel(total, place, sums_ref, res_ref, shift_ref, vt_ref, even_ref, odd_ref,
                     res_out, vt_out, grad_ref):
    step = pl.program_id(0)
    size, spread = column_sums(read_sums(sums_ref, 4))
    level = level_from(spread, total)
    grad = jnp.concatenate([even_ref[0], odd_ref[0]], axis=1)
    vt = vt_ref[...] - size * grad
    vt_out[...] = vt
    res = res_ref[...] + size * shift_ref[...]
    res_out[...] = res
    misfit = -jnp.clip(res, -level, level)
    part = product(halves(misfit), halves(vt), ((1,), (1,)))

    @pl.when(step == 0)
    def _():
        grad_ref[...] = part

    @pl.when(step > 0)
    def _():
        grad_ref[...] += part


def change_kernel(col_count, place, own_grad, other_grad, vt_ref, weight_ref,
                  change_ref, sums_ref, g_high, g_low, acc):
    step = pl.program_id(0)
    pixels = own_grad.shape[0]

    @pl.when(step == 0)
    def _():
        for part, ref in enumerate((own_grad, other_grad)):
            high, low = halves(ref[...])
            g_high[part * pixels : (part + 1) * pixels] = high
            g_low[part * pixels : (part + 1) * pixels] = low
        acc[...] = jnp.zeros_like(acc)

    change = weight_ref[...] * product((g_high[...], g_low[...]), halves(vt_ref[...]))
    change_ref[...] = change
    acc[...] += rows_folded(change * change)

    @pl.when(step == pl.num_programs(0) - 1)
    def _():
        top = whole_sum(own_grad[...] * own_grad[...]) / col_count
        sums_ref[...] = packed_sums(sums_ref.shape, [top, whole_sum(acc[...])])


def pix_step_kernel(total, first, place, level_sums, sums_ref, u_ref, own_grad, other_grad, res_ref,
                    change_ref, u_out, res_out, even_ref, odd_ref, u_high, u_low):
    step = pl.program_id(0)
    pixels = own_grad.shape[0]
    top, curve = read_sums(sums_ref, 2)
    size = top / curve
    if first:
        (spread,) = read_sums(level_sums, 1)
    else:
        _, spread = column_sums(read_sums(level_sums, 4))
    level = level_from(spread, total)

    @pl.when(step == 0)
    def _():
        for part, ref in enumerate((own_grad, other_grad)):
            rows = slice(part * pixels, (part + 1) * pixels)
            u = u_ref[rows] - size * ref[...]
            u_out[rows] = u
            high, low = halves(u)
            u_high[rows] = high
            u_low[rows] = low

    res = res_ref[...]
    moved = size * change_ref[...]
    res_out[...] = res + moved
    misfit = -(jnp.clip(res, -level, level) + moved)
    grad = product((u_high[...], u_low[...]), halves(misfit), ((0,), (0,)))
    even_ref[0] = grad[:, :LANES]
    odd_ref[0] = grad[:, LANES:]


def shift_kernel(chips, place, u_ref, even_ref, odd_ref, weight_ref, res_ref,
                 shift_ref, sums_ref, u_high, u_low, acc, acc_top):
    step = pl.program_id(0)

    @pl.when(step == 0)
    def _():
        high, low = halves(u_ref[...])
        u_high[...] = high
        u_low[...] = low
        acc[...] = jnp.zeros_like(acc)
        acc_top[...] = jnp.zeros_like(acc_top)

    grad = jnp.concatenate([even_ref[0], odd_ref[0]], axis=1)
    acc_top[...] += rows_folded(grad * grad)
    shift = weight_ref[...] * product((u_high[...], u_low[...]), halves(grad))
    shift_ref[...] = shift
    res = res_ref[...]
    acc[0] += rows_folded(shift * shift)
    acc[1] += rows_folded(shift * res)
    acc[2] += rows_folded(res * res)

    @pl.when(step == pl.num_programs(0) - 1)
    def _():
        sums = [whole_sum(acc_top[...]) / chips] + [whole_sum(acc[k]) for k in range(3)]
        sums_ref[...] = packed_sums(sums_ref.shape, sums)


def rim_kernel(place, *refs):
    obs = refs[0:4]
    mask = refs[4:8]
    factors = refs[8:12]
    vt_ref, res_ref, weight_ref, u_high, u_low = refs[12:]
    step = pl.program_id(0)
    chunk = place[1] ^ step
    pixels = obs[0].shape[0]

    @pl.when(step == 0)
    def _():
        for part, ref in enumerate(factors):
            rows = slice(part * pixels, (part + 1) * pixels)
            high, low = halves(ref[...])
            u_high[rows] = high
            u_low[rows] = low

    low_rank = product((u_high[...], u_low[...]), halves(vt_ref[...]))
    for part in range(4):
        weight = spread_mask(mask[part][...], chunk)
        weight_ref[part] = weight
        res_ref[part] = weight * (obs[part][...] - low_rank[part * pixels : (part + 1) * pixels])


def flux_of(diff, inverse):
    ratio = diff * inverse
    return diff / (1.0 + ratio * ratio)


def smooth_kernel(total, chips, place, sums_ref, res_ref, shift_ref, rim_ref, rim_weight, *refs):
    factors = refs[:4]
    grad_ref, own_ref, other_ref, u_high, u_low, rim_shift = refs[4:]
    step = pl.program_id(0)
    core, chip = place[0], place[2]
    pixels = own_ref.shape[0]

    @pl.when(step == 0)
    def _():
        for part, ref in enumerate(factors):
            rows = slice(part * pixels, (part + 1) * pixels)
            high, low = halves(ref[...])
            u_high[rows] = high
            u_low[rows] = low

    size, spread = column_sums(read_sums(sums_ref, 4))
    level = level_from(spread, total)
    inverse = 1.0 / level
    moved = product((u_high[...], u_low[...]), halves(grad_ref[0]))
    rim_shift[...] = moved.reshape(rim_shift.shape)

    def cut(res):
        return res - jnp.clip(res, -level, level)

    def own(k):
        return cut(res_ref[k] + size * shift_ref[k])

    def rim(k):
        return cut(rim_ref[k] + size * (rim_weight[k] * rim_shift[k]))

    south = 2 * (chip % 2)
    north = 2 - south
    rows = [rim(north + core), rim(north + 1 - core), own(core), own(1 - core),
            rim(south + core), rim(south + 1 - core)]
    keep_north = jnp.where(chip > 0, 1.0, 0.0).astype(f32)
    keep_south = jnp.where(chip < chips - 1, 1.0, 0.0).astype(f32)
    last = lax.broadcasted_iota(jnp.int32, (pixels, LANES), 0) % WIDTH == WIDTH - 1
    scaled = diffusion

    def smoothed(rows, north_edge, south_edge):
        count = len(rows)
        cross = []
        for k in range(count - 1):
            flux = flux_of(rows[k + 1] - rows[k], inverse)
            if k == north_edge:
                flux = flux * keep_north
            if k == south_edge:
                flux = flux * keep_south
            cross.append(flux)
        out = []
        for k in range(1, count - 1):
            east = jnp.where(last, 0.0, flux_of(pltpu.roll(rows[k], pixels - 1, 0) - rows[k], inverse))
            along = east - pltpu.roll(east, 1, 0)
            out.append(rows[k] + scaled * ((cross[k] - cross[k - 1]) + along))
        return out

    rows = smoothed(rows, 1, 3)
    rows = smoothed(rows, 0, 2)
    even, odd = rows
    own_ref[...] = jnp.where(core == 0, even, odd)
    other_ref[...] = jnp.where(core == 0, odd, even)


def factor_kernel(place, sums_ref, vt_ref, grad_ref, out_ref):
    size, _ = column_sums(read_sums(sums_ref, 4))
    out_ref[...] = (vt_ref[...] - size * grad_ref[0]).T


def grad_over_chips(even, odd, half):
    chips = lax.axis_size("pix") // 2
    from_odd = along_pix(odd, 2)
    kept = even + from_odd
    half = held_until(half, from_odd)
    mine = kept[0]
    for part in [along_pix(kept[k], 4 * k) for k in (1, 2, 3)]:
        mine = mine + part
    distance = GROUP
    while distance < chips:
        mine = mine + along_pix(mine, 2 * distance)
        distance *= 2
    even = jnp.stack([mine] + [along_pix(mine, 4 * k) for k in (1, 2, 3)])
    return even, half


def per_device(observed, valid_mask, pix_factor, col_factor):
    pix_count = lax.axis_size("pix")
    col_count = lax.axis_size("col")
    devices = pix_count * col_count
    chips = pix_count // 2
    pixels, columns = observed.shape
    rank = pix_factor.shape[1]
    half = columns // 2
    dates = valid_mask.shape[1] // 2
    total = float(pixels * columns * pix_count * col_count)
    assert pixels == WIDTH and half == GROUP * LANES and chips % GROUP == 0 and PASSES == 2
    index = lax.axis_index("pix")
    core = index % 2
    chip = index // 2
    place = jnp.stack([core, chip % GROUP, chip]).astype(jnp.int32)

    def half_of(which):
        obs = lax.dynamic_slice(observed, (0, which * half), (pixels, half))
        mask = lax.dynamic_slice(valid_mask, (0, which * dates), (pixels, dates))
        return jnp.concatenate([obs, mask.astype(f32)], axis=1)

    other_half = half_of(1 - core)
    own_half = half_of(core)
    received = along_pix(other_half, 1)
    other_factor = along_pix(pix_factor, 1)
    sent = [own_half, other_half]
    rims = []

    both = 2 * pixels
    wide = 2 * LANES
    steps = half // wide
    chunk_in = pl.BlockSpec((pixels, LANES), lambda t, s: (0, s[1] ^ t))
    mask_in = pl.BlockSpec((pixels, dates), lambda t, s: (0, half // dates))
    sums_shape = (devices, LANES)
    pix_block = whole((pixels, rank))
    both_block = whole((both, rank))
    sums_block = whole(sums_shape)
    tile_block = tile(both, wide)
    vt_block = tile(rank, wide)
    grad_block = pl.BlockSpec((1, rank, LANES), lambda t, s: (t, 0, 0))
    local = pltpu.HBM((both, half), f32)
    factor_scratch = [pltpu.VMEM((both, rank), bf16)] * 2

    residual, weight, vt, sums = call(
        start_kernel, (GROUP,),
        [chunk_in, mask_in, chunk_in, mask_in, pix_block, pix_block,
         pl.BlockSpec((LANES, rank), lambda t, s: (s[0] * GROUP + (s[1] ^ t), 0))],
        [tile(both, LANES), tile(both, LANES), tile(rank, LANES), sums_block],
        [local, local, shaped(rank, half), shaped(*sums_shape)],
        factor_scratch + [pltpu.VMEM((8, LANES), f32)],
        place, own_half, own_half, received, received, pix_factor, other_factor, col_factor,
    )
    level_sums = everywhere(sums)
    u = jnp.concatenate([pix_factor, other_factor], axis=0)

    for iteration in range(ITERS):
        sent[iteration] = held_until(sent[iteration], level_sums)
        rims.append(to_odd_or_even(sent[iteration], True, iteration))
        if iteration == 0:
            partial = call(
                functools.partial(first_grad_kernel, total), (steps,),
                [sums_block, tile_block, vt_block], both_block, shaped(both, rank), [],
                place, level_sums, residual, vt,
            )
        else:
            residual, vt, partial = call(
                functools.partial(next_grad_kernel, total), (steps,),
                [sums_block, tile_block, tile_block, vt_block, grad_block, grad_block],
                [tile_block, vt_block, both_block],
                [local, shaped(rank, half), shaped(both, rank)], [],
                place, level_sums, residual, shift, vt, even, odd,
            )
        own_grad = summed_over_col(partial[:pixels] + along_pix(partial[pixels:], 1))
        other_grad = along_pix(own_grad, 1)
        change, sums = call(
            functools.partial(change_kernel, col_count), (steps,),
            [pix_block, pix_block, vt_block, tile_block], [tile_block, sums_block],
            [local, shaped(*sums_shape)], factor_scratch + [pltpu.VMEM((8, wide), f32)],
            place, own_grad, other_grad, vt, weight,
        )
        pix_sums = everywhere(sums)
        u, residual, even, odd = call(
            functools.partial(pix_step_kernel, total, iteration == 0), (steps,),
            [sums_block, sums_block, both_block, pix_block, pix_block, tile_block, tile_block],
            [both_block, tile_block, grad_block, grad_block],
            [shaped(both, rank), local, shaped(steps, rank, LANES), shaped(steps, rank, LANES)],
            factor_scratch,
            place, level_sums, pix_sums, u, own_grad, other_grad, residual, change, after=rims[-1:],
        )
        if iteration == ITERS - 1:
            u_own = u[:pixels]
            u_near = to_odd_or_even(u_own, False, 0)
            u_far = to_odd_or_even(u_own, True, 0)
            factors = [u_near, along_pix(u_near, 1), u_far, along_pix(u_far, 1)]
        even, sent[iteration] = grad_over_chips(even, odd, sent[iteration])
        rims.append(to_odd_or_even(sent[iteration], False, iteration))
        even = held_until(even, rims[-1])
        odd = along_pix(even, 2)
        shift, sums = call(
            functools.partial(shift_kernel, chips), (steps,),
            [both_block, grad_block, grad_block, tile_block, tile_block], [tile_block, sums_block],
            [local, shaped(*sums_shape)],
            factor_scratch + [pltpu.VMEM((3, 8, wide), f32), pltpu.VMEM((8, wide), f32)],
            place, u, even, odd, weight, residual,
        )
        level_sums = everywhere(sums)

    rims = [rims[1], rims[3], rims[0], rims[2]]
    rim_block = pl.BlockSpec((4, pixels, LANES), lambda t, s: (0, 0, t))
    rim_scratch = [pltpu.VMEM((2 * both, rank), bf16)] * 2
    rim_res, rim_weight = call(
        rim_kernel, (GROUP,),
        [chunk_in] * 4 + [mask_in] * 4 + [pix_block] * 4 + [tile(rank, LANES)],
        [rim_block, rim_block], [shaped(4, pixels, half)] * 2, rim_scratch,
        place, *rims, *rims, *factors, vt,
    )
    grad = jnp.stack([even, odd], axis=1).reshape(GROUP, rank, LANES)
    pair_block = pl.BlockSpec((2, pixels, LANES), lambda t, s: (0, 0, t))
    own_cloud, other_cloud = call(
        functools.partial(smooth_kernel, total, chips), (GROUP,),
        [sums_block, pair_block, pair_block, rim_block, rim_block] + [pix_block] * 4 + [grad_block],
        [chunk_in, chunk_in], [shaped(pixels, half)] * 2,
        rim_scratch + [pltpu.VMEM((4, pixels, LANES), f32)],
        place, level_sums, residual.reshape(2, pixels, half), shift.reshape(2, pixels, half),
        rim_res, rim_weight, *factors, grad,
    )
    own_v = call(
        factor_kernel, (GROUP,),
        [sums_block, tile(rank, LANES), grad_block],
        pl.BlockSpec((LANES, rank), lambda t, s: (s[1] ^ t, 0)), shaped(half, rank), [],
        place, level_sums, vt, grad,
    )
    other_v = along_pix(own_v, 1)
    from_other = along_pix(other_cloud, 1)

    def joined(own, other, axis):
        pair = [jnp.where(core == 0, own, other), jnp.where(core == 0, other, own)]
        return jnp.concatenate(pair, axis=axis)

    return u_own, joined(own_v, other_v, 0), joined(own_cloud, from_other, 1)


def solution(mesh):
    in_specs = (P("pix", "col"), P("pix", "col"), P("pix", None), P("col", None))
    out_specs = (P("pix", None), P("col", None), P("pix", "col"))
    return jax.shard_map(
        per_device, mesh=mesh, in_specs=in_specs, out_specs=out_specs, check_vma=False
    )
```

```python
import functools

import jax
import jax.numpy as jnp
from jax import lax
from jax.experimental import pallas as pl
from jax.experimental.pallas import tpu as pltpu
from jax.sharding import PartitionSpec as P

BANDS = 8
WIDTH = 256
ITERS = 2
PASSES = 2
LANES = 128
GROUP = 8

threshold_scale = 1.0
diffusion = 0.2
f32 = jnp.float32
bf16 = jnp.bfloat16


def along_pix(block, distance):
    count = lax.axis_size("pix")
    return lax.ppermute(block, "pix", [(i, i ^ distance) for i in range(count)])


def to_odd_or_even(block, far, crossed):
    count = lax.axis_size("pix")
    route = []
    for i in range(count):
        chip = i // 2
        target = ((chip + 1) ^ 1) - 1 if far else chip ^ 1
        if 0 <= target < count // 2:
            route.append((i, 2 * target + (i % 2 ^ crossed)))
    return lax.ppermute(block, "pix", route)


def summed_over_col(block):
    count = lax.axis_size("col")
    step = 1
    while step < count:
        block = block + lax.ppermute(block, "col", [(i, i ^ step) for i in range(count)])
        step *= 2
    return block


def everywhere(rows):
    return lax.all_to_all(rows, ("pix", "col"), 0, 0, tiled=True)


def halves(x):
    high = x.astype(bf16)
    return high, (x - high.astype(f32)).astype(bf16)


def product(a, b, dims=((1,), (0,))):
    def part(x, y):
        return lax.dot_general(x, y, (dims, ((), ())), preferred_element_type=f32)

    return part(a[0], b[0]) + (part(a[0], b[1]) + part(a[1], b[0]))


def rows_folded(x):
    return jnp.sum(x.reshape(x.shape[0] // 8, 8, x.shape[1]), axis=0)


def whole_sum(x):
    return jnp.sum(jnp.sum(x, axis=0, keepdims=True), axis=1, keepdims=True)


def packed_sums(shape, sums):
    lane = lax.broadcasted_iota(jnp.int32, shape, 1)
    packed = jnp.zeros(shape, f32)
    for place, value in enumerate(sums):
        packed = packed + jnp.where(lane == place, value, 0.0)
    return packed


def read_sums(ref, count):
    total = jnp.sum(ref[...], axis=0, keepdims=True)
    return [total[:, k : k + 1] for k in range(count)]


def spread_mask(mask, chip, step):
    dates = mask.shape[1]
    date = lax.broadcasted_iota(jnp.int32, (dates, 2 * LANES), 0)
    lane = lax.broadcasted_iota(jnp.int32, (dates, 2 * LANES), 1)
    chunk = chip ^ (2 * step + lane // LANES)
    pick = (date == chunk * (LANES // BANDS) + lane % LANES // BANDS).astype(bf16)
    return jnp.dot(mask.astype(bf16), pick, preferred_element_type=f32)


def call(kernel, grid, in_specs, out_specs, out_shape, scratch, *args, place=None, after=()):
    single = not isinstance(out_shape, (list, tuple))
    if single:
        out_specs, out_shape = [out_specs], [out_shape]
    inputs = len(in_specs)
    lead = 0 if place is None else 1

    def body(*refs):
        used = lead + inputs
        kernel(*refs[:used], *refs[used + len(after) :])

    results = pl.pallas_call(
        body,
        grid_spec=pltpu.PrefetchScalarGridSpec(
            num_scalar_prefetch=lead,
            grid=grid,
            in_specs=list(in_specs) + [pl.BlockSpec(memory_space=pl.ANY)] * len(after),
            out_specs=list(out_specs),
            scratch_shapes=scratch,
        ),
        out_shape=list(out_shape),
        compiler_params=pltpu.CompilerParams(vmem_limit_bytes=24 * 2**20),
    )(*([place] if lead else []), *args, *after)
    return results[0] if single else results


def in_hbm(array):
    return pltpu.with_memory_space_constraint(array, pltpu.HBM)


def held_until(array, *after):
    def body(*refs):
        pass

    anywhere = pl.BlockSpec(memory_space=pl.ANY)
    return pl.pallas_call(
        body,
        in_specs=[anywhere] * (1 + len(after)),
        out_specs=anywhere,
        out_shape=jax.ShapeDtypeStruct(array.shape, array.dtype),
        input_output_aliases={0: 0},
    )(array, *after)


def whole(shape):
    return pl.BlockSpec(shape, lambda t, *s: (0,) * len(shape))


def tile(rows, cols):
    return pl.BlockSpec((rows, cols), lambda t, *s: (0, t))


def shaped(*shape):
    return jax.ShapeDtypeStruct(shape, f32)


def split_factor(refs, high_ref, low_ref):
    pixels = refs[0].shape[0]
    for part, ref in enumerate(refs):
        rows = slice(part * pixels, (part + 1) * pixels)
        high_ref[rows], low_ref[rows] = halves(ref[...])


def start_kernel(place, own_0, own_1, own_mask, other_0, other_1, other_mask, own_u, other_u, v_0, v_1,
                 res_ref, weight_ref, vt_ref, sums_ref, u_high, u_low, acc):
    step = pl.program_id(0)
    pixels = own_u.shape[0]

    @pl.when(step == 0)
    def _():
        split_factor((own_u, other_u), u_high, u_low)
        acc[...] = jnp.zeros_like(acc)

    vt = jnp.concatenate([v_0[...].T, v_1[...].T], axis=1)
    vt_ref[...] = vt
    low_rank = product((u_high[...], u_low[...]), halves(vt))
    strips = ((own_0, own_1, own_mask), (other_0, other_1, other_mask))
    for part, (left, right, mask) in enumerate(strips):
        rows = slice(part * pixels, (part + 1) * pixels)
        weight = spread_mask(mask[...], place[1], step)
        obs = jnp.concatenate([left[...], right[...]], axis=1)
        res = weight * (obs - low_rank[rows])
        weight_ref[rows] = weight
        res_ref[rows] = res
        acc[...] += rows_folded(res * res)

    @pl.when(step == pl.num_programs(0) - 1)
    def _():
        sums_ref[...] = packed_sums(sums_ref.shape, [whole_sum(acc[...])])


def level_from(spread, total):
    return threshold_scale * jnp.sqrt(jnp.maximum(spread, 0.0) / total + 1e-06)


def add_parts(step, part, own_ref, other_ref):
    pixels = own_ref.shape[0]

    @pl.when(step == 0)
    def _():
        own_ref[...] = part[:pixels]
        other_ref[...] = part[pixels:]

    @pl.when(step > 0)
    def _():
        own_ref[...] += part[:pixels]
        other_ref[...] += part[pixels:]


def first_grad_kernel(total, sums_ref, res_ref, vt_ref, own_ref, other_ref):
    (spread,) = read_sums(sums_ref, 1)
    level = level_from(spread, total)
    misfit = -jnp.clip(res_ref[...], -level, level)
    part = product(halves(misfit), halves(vt_ref[...]), ((1,), (1,)))
    add_parts(pl.program_id(0), part, own_ref, other_ref)


def column_sums(sums):
    top, curve, cross, before = sums
    step = top / curve
    return step, before + 2.0 * step * cross + step * step * curve


def next_grad_kernel(total, sums_ref, res_ref, shift_ref, vt_ref, even_ref, odd_ref,
                     res_out, vt_out, own_ref, other_ref):
    size, spread = column_sums(read_sums(sums_ref, 4))
    level = level_from(spread, total)
    grad = jnp.concatenate([even_ref[0], odd_ref[0]], axis=1)
    vt = vt_ref[...] - size * grad
    vt_out[...] = vt
    res = res_ref[...] + size * shift_ref[...]
    res_out[...] = res
    misfit = -jnp.clip(res, -level, level)
    part = product(halves(misfit), halves(vt), ((1,), (1,)))
    add_parts(pl.program_id(0), part, own_ref, other_ref)


def change_kernel(col_count, own_grad, other_grad, vt_ref, weight_ref,
                  change_ref, sums_ref, g_high, g_low, acc):
    step = pl.program_id(0)

    @pl.when(step == 0)
    def _():
        split_factor((own_grad, other_grad), g_high, g_low)
        acc[...] = jnp.zeros_like(acc)

    change = weight_ref[...] * product((g_high[...], g_low[...]), halves(vt_ref[...]))
    change_ref[...] = change
    acc[...] += rows_folded(change * change)

    @pl.when(step == pl.num_programs(0) - 1)
    def _():
        top = whole_sum(own_grad[...] * own_grad[...]) / col_count
        sums_ref[...] = packed_sums(sums_ref.shape, [top, whole_sum(acc[...])])


def pix_step_kernel(total, first, level_sums, sums_ref, own_u, other_u, own_grad, other_grad, res_ref,
                    change_ref, own_out, other_out, res_out, even_ref, odd_ref, ut_high, ut_low):
    step = pl.program_id(0)
    pixels = own_grad.shape[0]
    top, curve = read_sums(sums_ref, 2)
    size = top / curve
    if first:
        (spread,) = read_sums(level_sums, 1)
    else:
        _, spread = column_sums(read_sums(level_sums, 4))
    level = level_from(spread, total)

    @pl.when(step == 0)
    def _():
        strips = ((own_u, own_grad, own_out), (other_u, other_grad, other_out))
        for part, (old, grad, out) in enumerate(strips):
            u = old[...] - size * grad[...]
            out[...] = u
            cols = slice(part * pixels, (part + 1) * pixels)
            ut_high[:, cols], ut_low[:, cols] = halves(u.T)

    res = res_ref[...]
    moved = size * change_ref[...]
    res_out[...] = res + moved
    misfit = -(jnp.clip(res, -level, level) + moved)
    grad = product((ut_high[...], ut_low[...]), halves(misfit))
    even_ref[0] = grad[:, :LANES]
    odd_ref[0] = grad[:, LANES:]


def shift_kernel(chips, own_u, other_u, even_ref, odd_ref, weight_ref, res_ref,
                 shift_ref, sums_ref, u_high, u_low, acc, acc_top):
    step = pl.program_id(0)

    @pl.when(step == 0)
    def _():
        split_factor((own_u, other_u), u_high, u_low)
        acc[...] = jnp.zeros_like(acc)
        acc_top[...] = jnp.zeros_like(acc_top)

    grad = jnp.concatenate([even_ref[0], odd_ref[0]], axis=1)
    acc_top[...] += rows_folded(grad * grad)
    shift = weight_ref[...] * product((u_high[...], u_low[...]), halves(grad))
    shift_ref[...] = shift
    res = res_ref[...]
    acc[0] += rows_folded(shift * shift)
    acc[1] += rows_folded(shift * res)
    acc[2] += rows_folded(res * res)

    @pl.when(step == pl.num_programs(0) - 1)
    def _():
        sums = [whole_sum(acc_top[...]) / chips] + [whole_sum(acc[k]) for k in range(3)]
        sums_ref[...] = packed_sums(sums_ref.shape, sums)


def rim_kernel(place, *refs):
    obs = refs[0:8]
    mask = refs[8:12]
    factors = refs[12:16]
    vt_ref, res_ref, weight_ref, u_high, u_low = refs[16:]
    step = pl.program_id(0)
    pixels = factors[0].shape[0]

    @pl.when(step == 0)
    def _():
        split_factor(factors, u_high, u_low)

    low_rank = product((u_high[...], u_low[...]), halves(vt_ref[...]))
    for part in range(4):
        weight = spread_mask(mask[part][...], place[1], step)
        weight_ref[part] = weight
        rows = jnp.concatenate([obs[2 * part][...], obs[2 * part + 1][...]], axis=1)
        res_ref[part] = weight * (rows - low_rank[part * pixels : (part + 1) * pixels])


def add_kernel(kept_ref, from_ref, *out_refs):
    for k, ref in enumerate(out_refs):
        ref[...] = kept_ref[k] + from_ref[k]


def stack_kernel(*refs):
    for k, ref in enumerate(refs[:-1]):
        refs[-1][k] = ref[...]


def flux_of(diff, inverse):
    ratio = diff * inverse
    below = 1.0 + ratio * ratio
    guess = pl.reciprocal(below, approx=True)
    return diff * (guess * (2.0 - below * guess))


def smooth_kernel(total, chips, place, sums_ref, res_ref, shift_ref, rim_ref, rim_weight, *refs):
    factors = refs[:4]
    own_vt, other_vt, own_grad, other_grad, own_ref, other_ref, v_ref, u_high, u_low, rim_shift = refs[4:]
    step = pl.program_id(0)
    core, chip = place[0], place[2]
    pixels = own_ref.shape[0]

    @pl.when(step == 0)
    def _():
        split_factor(factors, u_high, u_low)

    size, spread = column_sums(read_sums(sums_ref, 4))
    level = level_from(spread, total)
    inverse = 1.0 / level
    v_ref[core] = (own_vt[...] - size * own_grad[0]).T
    v_ref[1 - core] = (other_vt[...] - size * other_grad[0]).T
    moved = product((u_high[...], u_low[...]), halves(own_grad[0]))
    rim_shift[...] = moved.reshape(rim_shift.shape)

    def cut(res):
        return res - jnp.clip(res, -level, level)

    def own(k):
        return cut(res_ref[k] + size * shift_ref[k])

    def rim(k):
        return cut(rim_ref[k] + size * (rim_weight[k] * rim_shift[k]))

    south = 2 * (chip % 2)
    north = 2 - south
    rows = [rim(north + core), rim(north + 1 - core), own(core), own(1 - core),
            rim(south + core), rim(south + 1 - core)]
    keep_north = jnp.where(chip > 0, 1.0, 0.0).astype(f32)
    keep_south = jnp.where(chip < chips - 1, 1.0, 0.0).astype(f32)
    last = lax.broadcasted_iota(jnp.int32, (pixels, LANES), 0) % WIDTH == WIDTH - 1
    scaled = diffusion

    def smoothed(rows, north_edge, south_edge):
        count = len(rows)
        cross = []
        for k in range(count - 1):
            flux = flux_of(rows[k + 1] - rows[k], inverse)
            if k == north_edge:
                flux = flux * keep_north
            if k == south_edge:
                flux = flux * keep_south
            cross.append(flux)
        out = []
        for k in range(1, count - 1):
            east = jnp.where(last, 0.0, flux_of(pltpu.roll(rows[k], pixels - 1, 0) - rows[k], inverse))
            along = east - pltpu.roll(east, 1, 0)
            out.append(rows[k] + scaled * ((cross[k] - cross[k - 1]) + along))
        return out

    rows = smoothed(rows, 1, 3)
    rows = smoothed(rows, 0, 2)
    even, odd = rows
    own_ref[...] = jnp.where(core == 0, even, odd)
    other_ref[...] = jnp.where(core == 0, odd, even)


def grad_over_chips(even, odd, half):
    chips = lax.axis_size("pix") // 2
    count, rank, lanes = even.shape
    block = whole((rank, lanes))
    blocks = whole(even.shape)
    from_odd = along_pix(odd, 2)
    half = held_until(half, from_odd)
    kept = call(add_kernel, (1,), [blocks] * 2, [block] * count, [shaped(rank, lanes)] * count, [], even, from_odd)
    mine = kept[0]
    for part in [along_pix(kept[k], 4 * k) for k in (1, 2, 3)]:
        mine = mine + part
    distance = GROUP
    while distance < chips:
        mine = mine + along_pix(mine, 2 * distance)
        distance *= 2
    parts = [mine] + [along_pix(mine, 4 * k) for k in (1, 2, 3)]
    return parts, half


def per_device(observed, valid_mask, pix_factor, col_factor):
    pix_count = lax.axis_size("pix")
    col_count = lax.axis_size("col")
    devices = pix_count * col_count
    chips = pix_count // 2
    pixels, columns = observed.shape
    rank = pix_factor.shape[1]
    half = columns // 2
    dates = valid_mask.shape[1] // 2
    total = float(pixels * columns * pix_count * col_count)
    assert pixels == WIDTH and half == GROUP * LANES and chips % GROUP == 0 and PASSES == 2
    index = lax.axis_index("pix")
    core = index % 2
    chip = index // 2
    place = jnp.stack([core, chip % GROUP, chip]).astype(jnp.int32)

    def half_of(which):
        obs = lax.dynamic_slice(observed, (0, which * half), (pixels, half))
        mask = lax.dynamic_slice(valid_mask, (0, which * dates), (pixels, dates))
        return in_hbm(jnp.concatenate([obs, mask.astype(f32)], axis=1))

    other_half = half_of(1 - core)
    received = in_hbm(along_pix(other_half, 1))
    own_half = half_of(core)
    other_u = along_pix(pix_factor, 1)
    own_u = pix_factor
    sent = [own_half, other_half]
    rims = []

    both = 2 * pixels
    wide = 2 * LANES
    steps = half // wide
    chunk_in = [
        pl.BlockSpec((pixels, LANES), lambda t, s: (0, s[1] ^ (2 * t))),
        pl.BlockSpec((pixels, LANES), lambda t, s: (0, s[1] ^ (2 * t + 1))),
    ]
    mask_in = pl.BlockSpec((pixels, dates), lambda t, s: (0, half // dates))
    sums_shape = pltpu.HBM((devices, LANES), f32)
    pix_block = whole((pixels, rank))
    pix_shape = shaped(pixels, rank)
    sums_block = whole((devices, LANES))
    tile_block = tile(both, wide)
    vt_block = tile(rank, wide)
    grad_block = pl.BlockSpec((1, rank, LANES), lambda t: (t, 0, 0))
    grad_shape = shaped(steps, rank, LANES)
    local = pltpu.HBM((both, half), f32)
    factor_scratch = [pltpu.VMEM((both, rank), bf16)] * 2
    v_in = [
        pl.BlockSpec((LANES, rank), lambda t, s: (s[0] * GROUP + (s[1] ^ (2 * t)), 0)),
        pl.BlockSpec((LANES, rank), lambda t, s: (s[0] * GROUP + (s[1] ^ (2 * t + 1)), 0)),
    ]
    v = in_hbm(col_factor)

    residual, weight, vt, sums = call(
        start_kernel, (steps,),
        chunk_in + [mask_in] + chunk_in + [mask_in, pix_block, pix_block] + v_in,
        [tile_block, tile_block, vt_block, sums_block],
        [local, local, shaped(rank, half), sums_shape],
        factor_scratch + [pltpu.VMEM((8, wide), f32)],
        own_half, own_half, own_half, received, received, received, own_u, other_u, v, v, place=place,
    )
    weight = in_hbm(weight)
    level_sums = everywhere(sums)

    for iteration in range(ITERS):
        sent[iteration] = held_until(sent[iteration], level_sums)
        rims.append(in_hbm(to_odd_or_even(sent[iteration], True, iteration)))
        if iteration == 0:
            residual = in_hbm(residual)
            own_part, other_part = call(
                functools.partial(first_grad_kernel, total), (steps,),
                [sums_block, tile_block, vt_block], [pix_block] * 2, [pix_shape] * 2, [],
                level_sums, residual, vt,
            )
        else:
            residual, vt, own_part, other_part = call(
                functools.partial(next_grad_kernel, total), (steps,),
                [sums_block, tile_block, tile_block, vt_block, grad_block, grad_block],
                [tile_block, vt_block, pix_block, pix_block],
                [local, shaped(rank, half), pix_shape, pix_shape], [],
                level_sums, in_hbm(residual), in_hbm(shift), vt, even, odd,
            )
        own_grad = summed_over_col(own_part + along_pix(other_part, 1))
        other_grad = along_pix(own_grad, 1)
        change, sums = call(
            functools.partial(change_kernel, col_count), (steps,),
            [pix_block, pix_block, vt_block, tile_block], [tile_block, sums_block],
            [local, sums_shape], factor_scratch + [pltpu.VMEM((8, wide), f32)],
            own_grad, other_grad, vt, weight,
        )
        pix_sums = everywhere(sums)
        own_u, other_u, residual, even, odd = call(
            functools.partial(pix_step_kernel, total, iteration == 0), (steps,),
            [sums_block, sums_block] + [pix_block] * 4 + [tile_block, tile_block],
            [pix_block, pix_block, tile_block, grad_block, grad_block],
            [pix_shape, pix_shape, local, grad_shape, grad_shape],
            [pltpu.VMEM((rank, both), bf16)] * 2,
            level_sums, pix_sums, own_u, other_u, own_grad, other_grad, in_hbm(residual), in_hbm(change),
            after=rims[-1:],
        )
        if iteration == ITERS - 1:
            u_near = to_odd_or_even(own_u, False, 0)
            u_far = to_odd_or_even(own_u, True, 0)
            factors = [u_near, along_pix(u_near, 1), u_far, along_pix(u_far, 1)]
            other_vt = along_pix(vt, 1)
        parts, sent[iteration] = grad_over_chips(even, odd, sent[iteration])
        rims.append(in_hbm(to_odd_or_even(sent[iteration], False, iteration)))
        even = call(
            stack_kernel, (1,), [whole((rank, LANES))] * steps, whole((steps, rank, LANES)), grad_shape, [],
            *parts, after=rims[-1:],
        )
        odd = along_pix(even, 2)
        shift, sums = call(
            functools.partial(shift_kernel, chips), (steps,),
            [pix_block, pix_block, grad_block, grad_block, tile_block, tile_block], [tile_block, sums_block],
            [local, sums_shape],
            factor_scratch + [pltpu.VMEM((3, 8, wide), f32), pltpu.VMEM((8, wide), f32)],
            own_u, other_u, even, odd, weight, in_hbm(residual),
        )
        level_sums = everywhere(sums)

    rims = [rims[1], rims[3], rims[0], rims[2]]
    rim_scratch = [pltpu.VMEM((2 * both, rank), bf16)] * 2
    rim_block = pl.BlockSpec((4, pixels, wide), lambda t, s: (0, 0, t))
    rim_shape = pltpu.HBM((4, pixels, half), f32)
    rim_res, rim_weight = call(
        rim_kernel, (steps,),
        chunk_in * 4 + [mask_in] * 4 + [pix_block] * 4 + [vt_block],
        [rim_block] * 2, [rim_shape] * 2, rim_scratch,
        *[rim for rim in rims for _ in range(2)], *rims, *factors, vt, place=place, after=[sums],
    )

    def all_chunks(even, odd):
        return jnp.stack([even, odd], axis=1).reshape(GROUP, rank, LANES)

    own_chunks = all_chunks(even, odd)
    other_chunks = along_pix(own_chunks, 1)
    pair_block = pl.BlockSpec((2, pixels, LANES), lambda t, s: (0, 0, t))
    rim_block = pl.BlockSpec((4, pixels, LANES), lambda t, s: (0, 0, t))
    chunk_block = pl.BlockSpec((1, rank, LANES), lambda t, s: (t, 0, 0))
    own_cloud, other_cloud, v = call(
        functools.partial(smooth_kernel, total, chips), (GROUP,),
        [sums_block, pair_block, pair_block, rim_block, rim_block] + [pix_block] * 4
        + [tile(rank, LANES)] * 2 + [chunk_block] * 2,
        [
            pl.BlockSpec((pixels, LANES), lambda t, s: (0, s[0] * GROUP + (s[1] ^ t))),
            pl.BlockSpec((pixels, LANES), lambda t, s: (0, s[1] ^ t)),
            pl.BlockSpec((2, LANES, rank), lambda t, s: (0, s[1] ^ t, 0)),
        ],
        [shaped(pixels, columns), shaped(pixels, half), shaped(2, half, rank)],
        rim_scratch + [pltpu.VMEM((4, pixels, LANES), f32)],
        level_sums, in_hbm(residual.reshape(2, pixels, half)), in_hbm(shift.reshape(2, pixels, half)),
        in_hbm(rim_res), in_hbm(rim_weight), *factors, vt, other_vt, own_chunks, other_chunks, place=place,
    )
    from_other = along_pix(other_cloud, 1)
    cloud = lax.dynamic_update_slice(own_cloud, from_other, (0, (1 - core) * half))
    return own_u, v.reshape(columns, rank), cloud


def solution(mesh):
    in_specs = (P("pix", "col"), P("pix", "col"), P("pix", None), P("col", None))
    out_specs = (P("pix", None), P("col", None), P("pix", "col"))
    return jax.shard_map(
        per_device, mesh=mesh, in_specs=in_specs, out_specs=out_specs, check_vma=False
    )
```

```python
import functools

import jax
import jax.numpy as jnp
from jax import lax
from jax.experimental import pallas as pl
from jax.experimental.pallas import tpu as pltpu
from jax.sharding import PartitionSpec as P

BANDS = 8
WIDTH = 256
ITERS = 2
PASSES = 2
LANES = 128
GROUP = 8

threshold_scale = 1.0
diffusion = 0.2
f32 = jnp.float32
bf16 = jnp.bfloat16


def along_pix(block, distance):
    count = lax.axis_size("pix")
    return lax.ppermute(block, "pix", [(i, i ^ distance) for i in range(count)])


def to_near(block, crossed):
    count = lax.axis_size("pix")
    return lax.ppermute(block, "pix", [(i, i ^ 2 ^ crossed) for i in range(count)])


def to_far(block):
    count = lax.axis_size("pix")
    route = [(i, i + (4 if i // 2 % 2 == 0 else -4)) for i in range(count)]
    return lax.ppermute(block, "pix", [(a, b) for a, b in route if 0 <= b < count])


def summed_over_col(block):
    count = lax.axis_size("col")
    step = 1
    while step < count:
        block = plus(block, lax.ppermute(block, "col", [(i, i ^ step) for i in range(count)]))
        step *= 2
    return block


def everywhere(sums):
    count = lax.axis_size("col")
    devices = lax.axis_size("pix") * count
    bits = [count << k for k in range(1, (devices // count).bit_length() - 1)]
    bits = [bits[0]] + [1 << k for k in range(count.bit_length() - 1)] + bits[1:]
    stages = [[count]] + [bits[k : k + 2] for k in range(0, len(bits), 2)]
    for stage in stages:
        moves = [0]
        for bit in stage:
            moves += [move ^ bit for move in moves]
        parts = [
            lax.ppermute(sums, ("pix", "col"), [(i, i ^ move) for i in range(devices)]) for move in moves[1:]
        ]
        sums = plus(sums, *parts)
    return sums


def halves(x):
    high = x.astype(bf16)
    return high, (x - high.astype(f32)).astype(bf16)


def left_parts(x, axis):
    high, low = halves(x)
    return jnp.concatenate([high, high, low], axis=axis)


def right_parts(x, axis):
    high, low = halves(x)
    return jnp.concatenate([high, low, high], axis=axis)


def product(a, b, summed=0):
    return lax.dot_general(a, b, (((1,), (summed,)), ((), ())), preferred_element_type=f32)


def rows_folded(x):
    return jnp.sum(x.reshape(x.shape[0] // 8, 8, x.shape[1]), axis=0)


def whole_sum(x):
    return jnp.sum(jnp.sum(x, axis=0, keepdims=True), axis=1, keepdims=True)


def packed_sums(shape, sums):
    lane = lax.broadcasted_iota(jnp.int32, shape, 1)
    row = lax.broadcasted_iota(jnp.int32, shape, 0)
    packed = jnp.zeros(shape, f32)
    for place, value in enumerate(sums):
        packed = packed + jnp.where((lane == place) & (row == 0), value, 0.0)
    return packed


def read_sums(ref, count):
    total = jnp.sum(ref[...], axis=0, keepdims=True)
    return [total[:, k : k + 1] for k in range(count)]


def spread_mask(mask, chip, step):
    dates = mask.shape[1]
    date = lax.broadcasted_iota(jnp.int32, (dates, 2 * LANES), 0)
    lane = lax.broadcasted_iota(jnp.int32, (dates, 2 * LANES), 1)
    chunk = chip ^ (2 * step + lane // LANES)
    pick = (date == chunk * (LANES // BANDS) + lane % LANES // BANDS).astype(bf16)
    return jnp.dot(mask.astype(f32).astype(bf16), pick, preferred_element_type=f32)


SMEM = pl.BlockSpec(memory_space=pltpu.SMEM)
VMEM = pl.BlockSpec(memory_space=pltpu.VMEM)
ANY = pl.BlockSpec(memory_space=pl.ANY)


def call(kernel, in_specs, out_specs, out_shape, scratch, *args, grid=(), place=None, after=(), beside=()):
    inputs = len(in_specs)
    lead = 0 if place is None else 1

    def body(*refs):
        used = lead + inputs
        kernel(*refs[:used], *refs[used + len(after) + len(beside) :])

    results = pl.pallas_call(
        body,
        grid_spec=pltpu.PrefetchScalarGridSpec(
            num_scalar_prefetch=lead,
            grid=grid,
            in_specs=list(in_specs) + [ANY] * len(after) + [VMEM] * len(beside),
            out_specs=list(out_specs),
            scratch_shapes=scratch,
        ),
        out_shape=list(out_shape),
        compiler_params=pltpu.CompilerParams(vmem_limit_bytes=16 * 2**20),
    )(*([place] if lead else []), *args, *after, *[in_vmem(x) for x in beside])
    return list(results)


def plus_kernel(*refs):
    total = refs[0][...]
    for ref in refs[1:-1]:
        total = total + ref[...]
    refs[-1][...] = total


def plus(*arrays):
    (total,) = call(plus_kernel, [VMEM] * len(arrays), [VMEM], [shaped(*arrays[0].shape)], [], *arrays)
    return total


def in_vmem(array):
    return pltpu.with_memory_space_constraint(array, pltpu.VMEM)


def in_hbm(array):
    return pltpu.with_memory_space_constraint(array, pltpu.HBM)


def held_until(array, *after):
    def body(*refs):
        pass

    return pl.pallas_call(
        body,
        in_specs=[ANY] * (1 + len(after)),
        out_specs=ANY,
        out_shape=jax.ShapeDtypeStruct(array.shape, array.dtype),
        input_output_aliases={0: 0},
        compiler_params=pltpu.CompilerParams(vmem_limit_bytes=2**20),
    )(array, *after)


def shaped(*shape):
    return jax.ShapeDtypeStruct(shape, f32)


def tiles(ref):
    return [slice(start, start + 2 * LANES) for start in range(0, ref.shape[-1], 2 * LANES)]


def pack_strip(obs_ref, mask_ref, out_refs):
    columns = obs_ref.shape[1]
    start = 0
    for ref in out_refs:
        rows = slice(start, start + ref.shape[0])
        ref[:, :columns] = obs_ref[rows]
        ref[:, columns:] = mask_ref[rows].astype(f32)
        start += ref.shape[0]


def pack_kernel(which, obs_ref, mask_ref, *out_refs):
    pack_strip(obs_ref, mask_ref, out_refs)


def split_factor(refs, parts_ref):
    pixels = refs[0].shape[0]
    for part, ref in enumerate(refs):
        parts_ref[part * pixels : (part + 1) * pixels] = left_parts(ref[...], 1)


def chunk_starts(chip, step):
    return [pl.multiple_of((chip ^ (2 * step + b)) * LANES, LANES) for b in range(2)]


def own_kernel(place, obs_ref, mask_ref, v_ref, u_ref, low_ref, high_ref, vt_ref, res_ref, weight_ref, sum_ref):
    pack_strip(obs_ref, mask_ref, (low_ref, high_ref))
    u = left_parts(u_ref[...], 1)
    spread = 0.0
    for step, cols in enumerate(tiles(vt_ref)):
        starts = chunk_starts(place[1], step)
        vt = jnp.concatenate([v_ref[pl.ds(start, LANES)].T for start in starts], axis=1)
        vt_ref[:, cols] = vt
        weight = spread_mask(mask_ref[...], place[1], step)
        obs = jnp.concatenate([obs_ref[:, pl.ds(start, LANES)] for start in starts], axis=1)
        res = weight * (obs - product(u, right_parts(vt, 0)))
        weight_ref[:, cols] = weight
        res_ref[:, cols] = res
        spread = spread + rows_folded(res * res)
    sum_ref[...] = spread


def residual_of_pieces(pieces, chip, step, low_rank):
    half = pieces[0].shape[1] // (BANDS + 1) * BANDS
    start = 0
    for piece in pieces:
        rows = slice(start, start + piece.shape[0])
        weight = spread_mask(piece[:, half:], chip, step)
        obs = jnp.concatenate([piece[:, pl.ds(first, LANES)] for first in chunk_starts(chip, step)], axis=1)
        yield rows, weight * (obs - low_rank[rows]), weight
        start += piece.shape[0]


def other_kernel(place, low_piece, high_piece, u_ref, vt_ref, own_res, own_weight, own_sum,
                 res_ref, weight_ref, sums_ref):
    pixels = own_res.shape[0]
    res_ref[:pixels] = own_res[...]
    weight_ref[:pixels] = own_weight[...]
    u = left_parts(u_ref[...], 1)
    spread = own_sum[...]
    for step, cols in enumerate(tiles(vt_ref)):
        low_rank = product(u, right_parts(vt_ref[:, cols], 0))
        for rows, res, weight in residual_of_pieces((low_piece, high_piece), place[1], step, low_rank):
            below = slice(pixels + rows.start, pixels + rows.stop)
            weight_ref[below, cols] = weight
            res_ref[below, cols] = res
            spread = spread + rows_folded(res * res)
    sums_ref[...] = packed_sums(sums_ref.shape, [whole_sum(spread)])


def level_from(spread, total):
    return threshold_scale * jnp.sqrt(jnp.maximum(spread, 0.0) / total + 1e-06)


def store_parts(grad, own_ref, other_ref):
    pixels = own_ref.shape[0]
    own_ref[...] = grad[:pixels]
    other_ref[...] = grad[pixels:]


def first_grad_kernel(total, sums_ref, res_ref, vt_ref, own_ref, other_ref):
    (spread,) = read_sums(sums_ref, 1)
    level = level_from(spread, total)
    grad = None
    for cols in tiles(res_ref):
        misfit = -jnp.clip(res_ref[:, cols], -level, level)
        part = product(left_parts(misfit, 1), right_parts(vt_ref[:, cols], 1), 1)
        grad = part if grad is None else grad + part
    store_parts(grad, own_ref, other_ref)


def column_sums(sums):
    top, curve, cross, before = sums
    step = top / curve
    return step, before + 2.0 * step * cross + step * step * curve


def next_grad_kernel(total, sums_ref, res_ref, shift_ref, vt_ref, even_ref, odd_ref,
                     res_out, vt_out, own_ref, other_ref):
    size, spread = column_sums(read_sums(sums_ref, 4))
    level = level_from(spread, total)
    grad = None
    for k, cols in enumerate(tiles(res_ref)):
        vt = vt_ref[:, cols] - size * jnp.concatenate([even_ref[k], odd_ref[k]], axis=1)
        vt_out[:, cols] = vt
        res = res_ref[:, cols] + size * shift_ref[:, cols]
        res_out[:, cols] = res
        misfit = -jnp.clip(res, -level, level)
        part = product(left_parts(misfit, 1), right_parts(vt, 1), 1)
        grad = part if grad is None else grad + part
    store_parts(grad, own_ref, other_ref)


def change_kernel(col_count, own_grad, other_grad, vt_ref, weight_ref, change_ref, sums_ref, g_parts):
    split_factor((own_grad, other_grad), g_parts)
    curve = 0.0
    for cols in tiles(vt_ref):
        change = weight_ref[:, cols] * product(g_parts[...], right_parts(vt_ref[:, cols], 0))
        change_ref[:, cols] = change
        curve = curve + rows_folded(change * change)
    top = whole_sum(own_grad[...] * own_grad[...]) / col_count
    sums_ref[...] = packed_sums(sums_ref.shape, [top, whole_sum(curve)])


def pix_step_kernel(total, first, level_sums, sums_ref, own_u, other_u, own_grad, other_grad, res_ref,
                    change_ref, own_out, other_out, res_out, even_ref, odd_ref, ut_parts):
    pixels = own_grad.shape[0]
    top, curve = read_sums(sums_ref, 2)
    size = top / curve
    if first:
        (spread,) = read_sums(level_sums, 1)
    else:
        _, spread = column_sums(read_sums(level_sums, 4))
    level = level_from(spread, total)
    strips = ((own_u, own_grad, own_out), (other_u, other_grad, other_out))
    for part, (old, grad, out) in enumerate(strips):
        u = old[...] - size * grad[...]
        out[...] = u
        high, low = halves(u.T)
        for k, value in enumerate((high, high, low)):
            first_col = (2 * k + part) * pixels
            ut_parts[:, first_col : first_col + pixels] = value
    for k, cols in enumerate(tiles(res_ref)):
        res = res_ref[:, cols]
        moved = size * change_ref[:, cols]
        res_out[:, cols] = res + moved
        misfit = -(jnp.clip(res, -level, level) + moved)
        grad = product(ut_parts[...], right_parts(misfit, 0))
        even_ref[k] = grad[:, :LANES]
        odd_ref[k] = grad[:, LANES:]


def shift_kernel(chips, own_u, other_u, even_ref, odd_ref, weight_ref, res_ref, shift_ref, sums_ref, u_parts):
    split_factor((own_u, other_u), u_parts)
    top = curve = cross = spread = 0.0
    for k, cols in enumerate(tiles(res_ref)):
        grad = jnp.concatenate([even_ref[k], odd_ref[k]], axis=1)
        top = top + rows_folded(grad * grad)
        shift = weight_ref[:, cols] * product(u_parts[...], right_parts(grad, 0))
        shift_ref[:, cols] = shift
        res = res_ref[:, cols]
        curve = curve + rows_folded(shift * shift)
        cross = cross + rows_folded(shift * res)
        spread = spread + rows_folded(res * res)
    sums = [whole_sum(top) / chips, whole_sum(curve), whole_sum(cross), whole_sum(spread)]
    sums_ref[...] = packed_sums(sums_ref.shape, sums)


def rim_kernel(place, *refs):
    packs = [refs[2 * k : 2 * k + 2] for k in range(4)]
    factors = refs[8:12]
    vt_ref, res_ref, weight_ref, u_parts = refs[12:]
    pixels = factors[0].shape[0]
    split_factor(factors, u_parts)
    for step, cols in enumerate(tiles(vt_ref)):
        low_rank = product(u_parts[...], right_parts(vt_ref[:, cols], 0))
        for part, pieces in enumerate(packs):
            strip = low_rank[part * pixels : (part + 1) * pixels]
            for rows, res, weight in residual_of_pieces(pieces, place[1], step, strip):
                weight_ref[part, rows, cols] = weight
                res_ref[part, rows, cols] = res


def add_kernel(kept_ref, from_ref, *refs):
    count = kept_ref.shape[0]
    held = (len(refs) - count) // 2
    for k, ref in enumerate(refs[held : held + count]):
        ref[...] = kept_ref[k] + from_ref[k]
    for source, target in zip(refs[:held], refs[held + count :]):
        target[...] = source[...]


def stack_kernel(*refs):
    for k, ref in enumerate(refs[:-1]):
        refs[-1][k] = ref[...]


def flux_of(diff, inverse):
    ratio = diff * inverse
    below = 1.0 + ratio * ratio
    guess = pl.reciprocal(below, approx=True)
    return diff * (guess * (2.0 - below * guess))


PAD = 8
SPAN = 64


def smooth_rows(source, target, inverse, keep_north, keep_south, north_edge, south_edge):
    count = source.shape[0]
    for start in range(0, WIDTH, SPAN):
        row = lax.broadcasted_iota(jnp.int32, (SPAN + 2 * PAD, LANES), 0) + (start - PAD)
        inside = (row >= 0) & (row < WIDTH - 1)
        around = slice(start, start + SPAN + 2 * PAD)
        middle = slice(PAD, PAD + SPAN)
        before = None
        here = source[0, around]
        for k in range(count - 1):
            after = source[k + 1, around]
            cross = flux_of(after[middle] - here[middle], inverse)
            if k == north_edge:
                cross = cross * keep_north
            if k == south_edge:
                cross = cross * keep_south
            if k > 0:
                east = flux_of(pltpu.roll(here, SPAN + 2 * PAD - 1, 0) - here, inverse)
                east = jnp.where(inside, east, 0.0)
                west = pltpu.roll(east, 1, 0)
                along = east[middle] - west[middle]
                target(k - 1, start, here[middle] + diffusion * ((cross - before) + along))
            before = cross
            here = after


def smooth_kernel(total, chips, place, sums_ref, res_ref, shift_ref, rim_ref, rim_weight, *refs):
    factors = refs[:4]
    own_vt, other_vt, own_even, own_odd, other_even, other_odd = refs[4:10]
    own_ref, other_ref, v_ref, u_parts, rim_shift, layer, once = refs[10:]
    step = pl.program_id(0)
    core, chip = place[0], place[2]
    pixels = own_ref.shape[0]

    @pl.when(step == 0)
    def _():
        split_factor(factors, u_parts)

    size, spread = column_sums(read_sums(sums_ref, 4))
    level = level_from(spread, total)
    inverse = 1.0 / level
    grad = jnp.concatenate([own_even[step], own_odd[step]], axis=1)
    moved = product(u_parts[...], right_parts(grad, 0))
    rim_shift[...] = moved.reshape(rim_shift.shape)

    def cut(res):
        return res - jnp.clip(res, -level, level)

    south = 2 * (chip % 2)
    beyond_own = jnp.where(core == 0, 2 - south, south)
    beyond_other = 2 - beyond_own
    keep_north = jnp.where(chip > 0, 1.0, 0.0).astype(f32)
    keep_south = jnp.where(chip < chips - 1, 1.0, 0.0).astype(f32)
    keep_own = jnp.where(core == 0, keep_north, keep_south)
    keep_other = jnp.where(core == 0, keep_south, keep_north)
    inner = slice(PAD, PAD + pixels)
    pair = ((own_even, other_even), (own_odd, other_odd))
    for b in range(2):
        cols = pl.ds(pl.multiple_of((2 * step + b) * LANES, LANES), LANES)
        here = slice(b * LANES, (b + 1) * LANES)
        there = pl.ds(pl.multiple_of((chip % 2 ^ b) * LANES, LANES), LANES)
        v_ref[core, there] = (own_vt[:, cols] - size * pair[b][0][step]).T
        v_ref[1 - core, there] = (other_vt[:, cols] - size * pair[b][1][step]).T
        for k in range(2):
            layer[2 + k, inner] = cut(res_ref[k, :, cols] + size * shift_ref[k, :, cols])
            for first, base in ((0, beyond_own), (4, beyond_other)):
                rim = base + k
                moved = size * (rim_weight[rim, :, cols] * rim_shift[rim, :, here])
                layer[first + k, inner] = cut(rim_ref[rim, :, cols] + moved)

        def to_once(strip, start, value):
            once[strip, PAD + start : PAD + start + SPAN] = value

        def to_cloud(strip, start, value):
            ref = other_ref if strip else own_ref
            ref[start : start + SPAN, there] = value

        smooth_rows(layer, to_once, inverse, keep_own, keep_other, 1, 3)
        smooth_rows(once, to_cloud, inverse, keep_own, keep_other, 0, 2)


def summed_over_chips(even, odd, held, beside):
    chips = lax.axis_size("pix") // 2
    count, rank, lanes = even.shape
    from_odd = along_pix(odd, 2)
    shapes = [shaped(rank, lanes)] + [pltpu.HBM((rank, lanes), f32)] * (count - 1)
    shapes += [pltpu.HBM(x.shape, f32) for x in held]
    kept = call(
        add_kernel, [VMEM] * (2 + len(held)), [VMEM] * len(shapes), shapes, [], even, from_odd, *held, beside=beside,
    )
    mine = plus(kept[0], *[along_pix(kept[k], 4 * k) for k in (1, 2, 3)])
    distance = GROUP
    while distance < chips:
        mine = plus(mine, along_pix(mine, 2 * distance))
        distance *= 2
    parts = [mine] + [along_pix(mine, 4 * k) for k in (1, 2, 3)]
    return parts, from_odd, kept[count:]


def per_device(observed, valid_mask, pix_factor, col_factor):
    pix_count = lax.axis_size("pix")
    col_count = lax.axis_size("col")
    chips = pix_count // 2
    pixels, columns = observed.shape
    rank = pix_factor.shape[1]
    half = columns // 2
    dates = valid_mask.shape[1] // 2
    total = float(pixels * columns * pix_count * col_count)
    assert pixels == WIDTH and half == GROUP * LANES and chips % GROUP == 0 and PASSES == 2
    index = lax.axis_index("pix")
    core = index % 2
    chip = index // 2
    place = jnp.stack([core, chip % GROUP, chip]).astype(jnp.int32)

    both = 2 * pixels
    wide = 2 * LANES
    steps = half // wide
    sums_shape = shaped(8, LANES)
    pix_shape = shaped(pixels, rank)
    grad_shape = shaped(steps, rank, LANES)
    vt_shape = pltpu.VMEM((rank, half), f32)
    local = pltpu.VMEM((both, half), f32)
    strip = pltpu.VMEM((pixels, half), f32)
    factor_scratch = [pltpu.VMEM((both, 3 * rank), bf16)]

    pieces = [pltpu.VMEM((pixels // 2, half + dates), f32)] * 2

    half_in = [pl.BlockSpec((pixels, half), lambda t, s: (0, s[0])), pl.BlockSpec((pixels, dates), lambda t, s: (0, s[0]))]
    other_pieces = call(
        pack_kernel, half_in, [VMEM] * 2, pieces, [], in_hbm(observed), in_hbm(valid_mask),
        grid=(1,), place=jnp.reshape(1 - core, (1,)).astype(jnp.int32),
    )
    received = [along_pix(piece, 1) for piece in other_pieces]
    own_u, other_u = pix_factor, along_pix(pix_factor, 1)
    *own_pieces, vt, own_res, own_weight, own_sum = call(
        own_kernel, half_in + [pl.BlockSpec((half, rank), lambda t, s: (s[0], 0)), VMEM], [VMEM] * 6,
        pieces + [vt_shape, strip, strip, shaped(8, wide)], [],
        in_hbm(observed), in_hbm(valid_mask), in_hbm(col_factor), own_u, grid=(1,), place=place,
    )
    residual, weight, sums = call(
        other_kernel, [SMEM] + [VMEM] * 7, [VMEM] * 3, [local, local, sums_shape], [],
        place, *received, other_u, in_vmem(vt), in_vmem(own_res), in_vmem(own_weight), own_sum,
    )
    level_sums = everywhere(sums)

    near_own, near_other, far_own, far_other = [None, None], [None, None], [None, None], [None, None]
    for iteration in range(ITERS):
        first = iteration == 0
        if first:
            near_own[0] = to_near(held_until(own_pieces[0], level_sums), 0)
            passed = [near_own[0]]
            own_part, other_part = call(
                functools.partial(first_grad_kernel, total), [VMEM] * 3, [VMEM] * 2, [pix_shape] * 2, [],
                level_sums, in_vmem(residual), in_vmem(vt),
            )
        else:
            near_other[1] = to_near(held_until(other_pieces[1], level_sums), 1)
            near_other[0] = held_until(near_other[0], level_sums)
            far_other[0] = to_far(near_other[0])
            passed = [near_other[1], far_other[0]]
            residual, vt, own_part, other_part = call(
                functools.partial(next_grad_kernel, total), [VMEM] * 6, [VMEM] * 4,
                [local, vt_shape, pix_shape, pix_shape], [],
                level_sums, in_vmem(residual), in_vmem(shift), in_vmem(vt), even, odd, after=far_own[1:],
            )
        own_grad = summed_over_col(plus(own_part, along_pix(other_part, 1)))
        other_grad = along_pix(own_grad, 1)
        change, sums = call(
            functools.partial(change_kernel, col_count), [VMEM] * 4, [VMEM] * 2,
            [local, sums_shape], factor_scratch, own_grad, other_grad, in_vmem(vt), in_vmem(weight),
            beside=[residual],
        )
        pix_sums = everywhere(sums)
        own_u, other_u, residual, even, odd = call(
            functools.partial(pix_step_kernel, total, first), [VMEM] * 8, [VMEM] * 5,
            [pix_shape, pix_shape, local, grad_shape, grad_shape], [pltpu.VMEM((rank, 3 * both), bf16)],
            level_sums, pix_sums, own_u, other_u, own_grad, other_grad, in_vmem(residual),
            in_vmem(change), after=passed, beside=[vt, weight],
        )
        alive = [residual, vt, weight, own_u, other_u]
        if first:
            near_own[0] = held_until(near_own[0], odd)
            far_own[0] = to_far(near_own[0])
            parts, moved, _ = summed_over_chips(even, odd, [], alive)
            near_own[1] = to_near(held_until(own_pieces[1], moved), 0)
            near_other[0] = to_near(held_until(other_pieces[0], moved), 1)
            passed = [far_own[0], near_own[1], near_other[0]]
        else:
            near_other[1] = held_until(near_other[1], odd)
            far_other[1] = to_far(near_other[1])
            parts, moved, sent = summed_over_chips(even, odd, [own_u], alive)
            near_u = to_near(sent[0], 0)
            other_vt = along_pix(vt, 1)
            passed = [far_other[1], near_u]
        (even,) = call(
            stack_kernel, [VMEM] * steps, [VMEM], [grad_shape], [], *parts, after=passed, beside=alive,
        )
        odd = along_pix(even, 2)
        if first:
            near_own[1] = held_until(near_own[1], even)
            far_own[1] = to_far(near_own[1])
        else:
            near_u = held_until(near_u, even)
            far_u = to_far(near_u)
        shift, sums = call(
            functools.partial(shift_kernel, chips), [VMEM] * 6, [VMEM] * 2,
            [local, sums_shape], factor_scratch, own_u, other_u, even, odd, in_vmem(weight),
            in_vmem(residual), beside=[vt],
        )
        level_sums = everywhere(sums)

    factors = [near_u, along_pix(near_u, 1), far_u, along_pix(far_u, 1)]
    rim_scratch = [pltpu.VMEM((2 * both, 3 * rank), bf16)]
    rim_shape = pltpu.VMEM((4, pixels, half), f32)
    rim_res, rim_weight = call(
        rim_kernel, [SMEM] + [VMEM] * 13, [VMEM] * 2, [rim_shape] * 2, rim_scratch,
        place, *near_own, *near_other, *far_own, *far_other, *factors, in_vmem(vt), after=[sums],
    )
    grads = [even, odd, along_pix(even, 1), along_pix(odd, 1)]
    pair = lambda s, t: s[1] // 2 ^ t
    own_cloud, other_cloud, v = call(
        functools.partial(smooth_kernel, total, chips), [VMEM] * 15,
        [
            pl.BlockSpec((pixels, wide), lambda t, s: (0, s[0] * steps + pair(s, t))),
            pl.BlockSpec((pixels, wide), lambda t, s: (0, pair(s, t))),
            pl.BlockSpec((2, wide, rank), lambda t, s: (0, pair(s, t), 0)),
        ],
        [shaped(pixels, columns), shaped(pixels, half), shaped(2, half, rank)],
        rim_scratch + [
            pltpu.VMEM((4, pixels, wide), f32),
            pltpu.VMEM((6, pixels + 2 * PAD, LANES), f32),
            pltpu.VMEM((4, pixels + 2 * PAD, LANES), f32),
        ],
        level_sums, in_vmem(residual.reshape(2, pixels, half)), in_vmem(shift.reshape(2, pixels, half)),
        in_vmem(rim_res), in_vmem(rim_weight), *factors, in_vmem(vt), other_vt, *grads, grid=(steps,), place=place,
    )
    from_other = along_pix(other_cloud, 1)
    cloud = lax.dynamic_update_slice(own_cloud, from_other, (0, (1 - core) * half))
    return own_u, v.reshape(columns, rank), cloud


def solution(mesh):
    in_specs = (P("pix", "col"), P("pix", "col"), P("pix", None), P("col", None))
    out_specs = (P("pix", None), P("col", None), P("pix", "col"))
    return jax.shard_map(
        per_device, mesh=mesh, in_specs=in_specs, out_specs=out_specs, check_vma=False
    )
```

```python
import functools

import jax
import jax.numpy as jnp
from jax import lax
from jax.experimental import pallas as pl
from jax.experimental.pallas import tpu as pltpu
from jax.sharding import PartitionSpec as P

BANDS = 8
WIDTH = 256
ITERS = 2
PASSES = 2
LANES = 128
GROUP = 8

threshold_scale = 1.0
diffusion = 0.2
f32 = jnp.float32
bf16 = jnp.bfloat16


def along_pix(block, distance):
    count = lax.axis_size("pix")
    return lax.ppermute(block, "pix", [(i, i ^ distance) for i in range(count)])


def to_near(block, crossed):
    count = lax.axis_size("pix")
    return lax.ppermute(block, "pix", [(i, i ^ 2 ^ crossed) for i in range(count)])


def to_far(block):
    count = lax.axis_size("pix")
    route = [(i, i + (4 if i // 2 % 2 == 0 else -4)) for i in range(count)]
    return lax.ppermute(block, "pix", [(a, b) for a, b in route if 0 <= b < count])


def summed_over_col(block):
    count = lax.axis_size("col")
    step = 1
    while step < count:
        block = plus(block, lax.ppermute(block, "col", [(i, i ^ step) for i in range(count)]))
        step *= 2
    return block


def everywhere(sums, late=False):
    count = lax.axis_size("col")
    devices = lax.axis_size("pix") * count
    bits = [count << k for k in range(1, (devices // count).bit_length() - 1)]
    bits = [bits[0]] + [1 << k for k in range(count.bit_length() - 1)] + bits[1:]
    stages = [[count]] + [bits[k : k + 2] for k in range(0, len(bits), 2)]
    if late:
        stages = stages[:1] + stages[:0:-1]
    for stage in stages:
        moves = [0]
        for bit in stage:
            moves += [move ^ bit for move in moves]
        parts = [
            lax.ppermute(sums, ("pix", "col"), [(i, i ^ move) for i in range(devices)]) for move in moves[1:]
        ]
        sums = plus(sums, *parts)
    return sums


def halves(x):
    high = x.astype(bf16)
    return high, (x - high.astype(f32)).astype(bf16)


def left_parts(x, axis):
    high, low = halves(x)
    return jnp.concatenate([high, high, low], axis=axis)


def right_parts(x, axis):
    high, low = halves(x)
    return jnp.concatenate([high, low, high], axis=axis)


def product(a, b, summed=0):
    return lax.dot_general(a, b, (((1,), (summed,)), ((), ())), preferred_element_type=f32)


def rows_folded(x):
    return jnp.sum(x.reshape(x.shape[0] // 8, 8, x.shape[1]), axis=0)


def whole_sum(x):
    return jnp.sum(jnp.sum(x, axis=0, keepdims=True), axis=1, keepdims=True)


def packed_sums(shape, sums):
    lane = lax.broadcasted_iota(jnp.int32, shape, 1)
    row = lax.broadcasted_iota(jnp.int32, shape, 0)
    packed = jnp.zeros(shape, f32)
    for place, value in enumerate(sums):
        packed = packed + jnp.where((lane == place) & (row == 0), value, 0.0)
    return packed


def read_sums(ref, count):
    total = jnp.sum(ref[...], axis=0, keepdims=True)
    return [total[:, k : k + 1] for k in range(count)]


def spread_mask(mask, chip, step):
    dates = mask.shape[1]
    date = lax.broadcasted_iota(jnp.int32, (dates, 2 * LANES), 0)
    lane = lax.broadcasted_iota(jnp.int32, (dates, 2 * LANES), 1)
    chunk = chip ^ (2 * step + lane // LANES)
    pick = (date == chunk * (LANES // BANDS) + lane % LANES // BANDS).astype(bf16)
    return jnp.dot(mask.astype(f32).astype(bf16), pick, preferred_element_type=f32)


SMEM = pl.BlockSpec(memory_space=pltpu.SMEM)
VMEM = pl.BlockSpec(memory_space=pltpu.VMEM)
ANY = pl.BlockSpec(memory_space=pl.ANY)


def call(kernel, in_specs, out_specs, out_shape, scratch, *args, grid=(), place=None, after=(), beside=()):
    inputs = len(in_specs)
    lead = 0 if place is None else 1

    def body(*refs):
        used = lead + inputs
        kernel(*refs[:used], *refs[used + len(after) + len(beside) :])

    results = pl.pallas_call(
        body,
        grid_spec=pltpu.PrefetchScalarGridSpec(
            num_scalar_prefetch=lead,
            grid=grid,
            in_specs=list(in_specs) + [ANY] * len(after) + [VMEM] * len(beside),
            out_specs=list(out_specs),
            scratch_shapes=scratch,
        ),
        out_shape=list(out_shape),
        compiler_params=pltpu.CompilerParams(vmem_limit_bytes=16 * 2**20),
    )(*([place] if lead else []), *args, *after, *[in_vmem(x) for x in beside])
    return list(results)


def plus_kernel(*refs):
    total = refs[0][...]
    for ref in refs[1:-1]:
        total = total + ref[...]
    refs[-1][...] = total


def plus(*arrays):
    (total,) = call(plus_kernel, [VMEM] * len(arrays), [VMEM], [shaped(*arrays[0].shape)], [], *arrays)
    return total


def in_vmem(array):
    return pltpu.with_memory_space_constraint(array, pltpu.VMEM)


def in_hbm(array):
    return pltpu.with_memory_space_constraint(array, pltpu.HBM)


def held_until(array, *after):
    def body(*refs):
        pass

    return pl.pallas_call(
        body,
        in_specs=[ANY] * (1 + len(after)),
        out_specs=ANY,
        out_shape=jax.ShapeDtypeStruct(array.shape, array.dtype),
        input_output_aliases={0: 0},
        compiler_params=pltpu.CompilerParams(vmem_limit_bytes=2**20),
    )(array, *after)


def shaped(*shape):
    return jax.ShapeDtypeStruct(shape, f32)


def tiles(ref):
    return [slice(start, start + 2 * LANES) for start in range(0, ref.shape[-1], 2 * LANES)]


def pack_strip(obs_ref, mask_ref, out_refs):
    columns = obs_ref.shape[1]
    start = 0
    for ref in out_refs:
        rows = slice(start, start + ref.shape[0])
        ref[:, :columns] = obs_ref[rows]
        ref[:, columns:] = mask_ref[rows].astype(f32)
        start += ref.shape[0]


def pack_kernel(which, obs_ref, mask_ref, *out_refs):
    pack_strip(obs_ref, mask_ref, out_refs)


def split_factor(refs, parts_ref):
    pixels = refs[0].shape[0]
    for part, ref in enumerate(refs):
        parts_ref[part * pixels : (part + 1) * pixels] = left_parts(ref[...], 1)


def chunk_starts(chip, step):
    return [pl.multiple_of((chip ^ (2 * step + b)) * LANES, LANES) for b in range(2)]


def own_kernel(place, obs_ref, mask_ref, v_ref, u_ref, *refs):
    vt_ref, res_ref, weight_ref, sum_ref = refs[-4:]
    pack_strip(obs_ref, mask_ref, refs[:-4])
    u = left_parts(u_ref[...], 1)
    spread = 0.0
    for step, cols in enumerate(tiles(vt_ref)):
        starts = chunk_starts(place[1], step)
        vt = jnp.concatenate([v_ref[pl.ds(start, LANES)].T for start in starts], axis=1)
        vt_ref[:, cols] = vt
        weight = spread_mask(mask_ref[...], place[1], step)
        obs = jnp.concatenate([obs_ref[:, pl.ds(start, LANES)] for start in starts], axis=1)
        res = weight * (obs - product(u, right_parts(vt, 0)))
        weight_ref[:, cols] = weight
        res_ref[:, cols] = res
        spread = spread + rows_folded(res * res)
    sum_ref[...] = spread


def residual_of_pieces(pieces, chip, step, low_rank):
    half = pieces[0].shape[1] // (BANDS + 1) * BANDS
    start = 0
    for piece in pieces:
        rows = slice(start, start + piece.shape[0])
        weight = spread_mask(piece[:, half:], chip, step)
        obs = jnp.concatenate([piece[:, pl.ds(first, LANES)] for first in chunk_starts(chip, step)], axis=1)
        yield rows, weight * (obs - low_rank[rows]), weight
        start += piece.shape[0]


def other_kernel(place, *refs):
    pieces = refs[:-8]
    u_ref, vt_ref, own_res, own_weight, own_sum, res_ref, weight_ref, sums_ref = refs[-8:]
    pixels = own_res.shape[0]
    res_ref[:pixels] = own_res[...]
    weight_ref[:pixels] = own_weight[...]
    u = left_parts(u_ref[...], 1)
    spread = own_sum[...]
    for step, cols in enumerate(tiles(vt_ref)):
        low_rank = product(u, right_parts(vt_ref[:, cols], 0))
        for rows, res, weight in residual_of_pieces(pieces, place[1], step, low_rank):
            below = slice(pixels + rows.start, pixels + rows.stop)
            weight_ref[below, cols] = weight
            res_ref[below, cols] = res
            spread = spread + rows_folded(res * res)
    sums_ref[...] = packed_sums(sums_ref.shape, [whole_sum(spread)])


def level_from(spread, total):
    return threshold_scale * jnp.sqrt(jnp.maximum(spread, 0.0) / total + 1e-06)


def store_parts(grad, own_ref, other_ref):
    pixels = own_ref.shape[0]
    own_ref[...] = grad[:pixels]
    other_ref[...] = grad[pixels:]


def first_grad_kernel(total, sums_ref, res_ref, vt_ref, own_ref, other_ref):
    (spread,) = read_sums(sums_ref, 1)
    level = level_from(spread, total)
    grad = None
    for cols in tiles(res_ref):
        misfit = -jnp.clip(res_ref[:, cols], -level, level)
        part = product(left_parts(misfit, 1), right_parts(vt_ref[:, cols], 1), 1)
        grad = part if grad is None else grad + part
    store_parts(grad, own_ref, other_ref)


def column_sums(sums):
    top, curve, cross, before = sums
    step = top / curve
    return step, before + 2.0 * step * cross + step * step * curve


def next_grad_kernel(total, sums_ref, res_ref, shift_ref, vt_ref, even_ref, odd_ref,
                     res_out, vt_out, own_ref, other_ref):
    size, spread = column_sums(read_sums(sums_ref, 4))
    level = level_from(spread, total)
    grad = None
    for k, cols in enumerate(tiles(res_ref)):
        vt = vt_ref[:, cols] - size * jnp.concatenate([even_ref[k], odd_ref[k]], axis=1)
        vt_out[:, cols] = vt
        res = res_ref[:, cols] + size * shift_ref[:, cols]
        res_out[:, cols] = res
        misfit = -jnp.clip(res, -level, level)
        part = product(left_parts(misfit, 1), right_parts(vt, 1), 1)
        grad = part if grad is None else grad + part
    store_parts(grad, own_ref, other_ref)


def change_kernel(col_count, own_grad, other_grad, vt_ref, weight_ref, change_ref, sums_ref, g_parts):
    split_factor((own_grad, other_grad), g_parts)
    curve = 0.0
    for cols in tiles(vt_ref):
        change = weight_ref[:, cols] * product(g_parts[...], right_parts(vt_ref[:, cols], 0))
        change_ref[:, cols] = change
        curve = curve + rows_folded(change * change)
    top = whole_sum(own_grad[...] * own_grad[...]) / col_count
    sums_ref[...] = packed_sums(sums_ref.shape, [top, whole_sum(curve)])


def pix_step_kernel(total, first, level_sums, sums_ref, own_u, other_u, own_grad, other_grad, res_ref,
                    change_ref, own_out, other_out, res_out, even_ref, odd_ref, ut_parts):
    pixels = own_grad.shape[0]
    top, curve = read_sums(sums_ref, 2)
    size = top / curve
    if first:
        (spread,) = read_sums(level_sums, 1)
    else:
        _, spread = column_sums(read_sums(level_sums, 4))
    level = level_from(spread, total)
    strips = ((own_u, own_grad, own_out), (other_u, other_grad, other_out))
    for part, (old, grad, out) in enumerate(strips):
        u = old[...] - size * grad[...]
        out[...] = u
        high, low = halves(u.T)
        for k, value in enumerate((high, high, low)):
            first_col = (2 * k + part) * pixels
            ut_parts[:, first_col : first_col + pixels] = value
    for k, cols in enumerate(tiles(res_ref)):
        res = res_ref[:, cols]
        moved = size * change_ref[:, cols]
        res_out[:, cols] = res + moved
        misfit = -(jnp.clip(res, -level, level) + moved)
        grad = product(ut_parts[...], right_parts(misfit, 0))
        even_ref[k] = grad[:, :LANES]
        odd_ref[k] = grad[:, LANES:]


def shift_kernel(chips, own_u, other_u, even_ref, odd_ref, weight_ref, res_ref, shift_ref, sums_ref, u_parts):
    split_factor((own_u, other_u), u_parts)
    top = curve = cross = spread = 0.0
    for k, cols in enumerate(tiles(res_ref)):
        grad = jnp.concatenate([even_ref[k], odd_ref[k]], axis=1)
        top = top + rows_folded(grad * grad)
        shift = weight_ref[:, cols] * product(u_parts[...], right_parts(grad, 0))
        shift_ref[:, cols] = shift
        res = res_ref[:, cols]
        curve = curve + rows_folded(shift * shift)
        cross = cross + rows_folded(shift * res)
        spread = spread + rows_folded(res * res)
    sums = [whole_sum(top) / chips, whole_sum(curve), whole_sum(cross), whole_sum(spread)]
    sums_ref[...] = packed_sums(sums_ref.shape, sums)


def rim_kernel(place, *refs):
    packs = [refs[3 * k : 3 * k + 3] for k in range(4)]
    factors = refs[12:16]
    vt_ref, res_ref, weight_ref, u_parts = refs[16:]
    pixels = factors[0].shape[0]
    split_factor(factors, u_parts)
    for step, cols in enumerate(tiles(vt_ref)):
        low_rank = product(u_parts[...], right_parts(vt_ref[:, cols], 0))
        for part, pieces in enumerate(packs):
            strip = low_rank[part * pixels : (part + 1) * pixels]
            for rows, res, weight in residual_of_pieces(pieces, place[1], step, strip):
                weight_ref[part, rows, cols] = weight
                res_ref[part, rows, cols] = res


def add_kernel(kept_ref, from_ref, *refs):
    count = kept_ref.shape[0]
    held = (len(refs) - count) // 2
    for k, ref in enumerate(refs[held : held + count]):
        ref[...] = kept_ref[k] + from_ref[k]
    for source, target in zip(refs[:held], refs[held + count :]):
        target[...] = source[...]


def stack_kernel(*refs):
    for k, ref in enumerate(refs[:-1]):
        refs[-1][k] = ref[...]


def flux_of(diff):
    below = 1.0 + diff * diff
    guess = pl.reciprocal(below, approx=True)
    return diff * (guess * (2.0 - below * guess))


PAD = 8
SPAN = 64


def smooth_rows(source, target, keep_north, keep_south, north_edge, south_edge):
    count = source.shape[0]
    for start in range(0, WIDTH, SPAN):
        row = lax.broadcasted_iota(jnp.int32, (SPAN + 2 * PAD, LANES), 0) + (start - PAD)
        inside = (row >= 0) & (row < WIDTH - 1)
        around = slice(start, start + SPAN + 2 * PAD)
        middle = slice(PAD, PAD + SPAN)
        before = None
        here = source[0, around]
        for k in range(count - 1):
            after = source[k + 1, around]
            cross = flux_of(after[middle] - here[middle])
            if k == north_edge:
                cross = cross * keep_north
            if k == south_edge:
                cross = cross * keep_south
            if k > 0:
                east = flux_of(pltpu.roll(here, SPAN + 2 * PAD - 1, 0) - here)
                east = jnp.where(inside, east, 0.0)
                west = pltpu.roll(east, 1, 0)
                along = east[middle] - west[middle]
                target(k - 1, start, here[middle] + diffusion * ((cross - before) + along))
            before = cross
            here = after


def smooth_kernel(total, chips, place, sums_ref, res_ref, shift_ref, rim_ref, rim_weight, *refs):
    factors = refs[:4]
    own_vt, other_vt, own_even, own_odd, other_even, other_odd = refs[4:10]
    own_ref, other_ref, v_ref, u_parts, rim_shift, layer, once = refs[10:]
    step = pl.program_id(0)
    core, chip = place[0], place[2]
    pixels = own_ref.shape[0]

    @pl.when(step == 0)
    def _():
        split_factor(factors, u_parts)

    size, spread = column_sums(read_sums(sums_ref, 4))
    level = level_from(spread, total)
    inverse = 1.0 / level
    grad = jnp.concatenate([own_even[step], own_odd[step]], axis=1)
    moved = product(u_parts[...], right_parts(grad, 0))
    rim_shift[...] = moved.reshape(rim_shift.shape)

    def cut(res):
        return (res - jnp.clip(res, -level, level)) * inverse

    south = 2 * (chip % 2)
    beyond_own = jnp.where(core == 0, 2 - south, south)
    beyond_other = 2 - beyond_own
    keep_north = jnp.where(chip > 0, 1.0, 0.0).astype(f32)
    keep_south = jnp.where(chip < chips - 1, 1.0, 0.0).astype(f32)
    keep_own = jnp.where(core == 0, keep_north, keep_south)
    keep_other = jnp.where(core == 0, keep_south, keep_north)
    inner = slice(PAD, PAD + pixels)
    pair = ((own_even, other_even), (own_odd, other_odd))
    for b in range(2):
        cols = pl.ds(pl.multiple_of((2 * step + b) * LANES, LANES), LANES)
        here = slice(b * LANES, (b + 1) * LANES)
        there = pl.ds(pl.multiple_of((chip % 2 ^ b) * LANES, LANES), LANES)
        v_ref[core, there] = (own_vt[:, cols] - size * pair[b][0][step]).T
        v_ref[1 - core, there] = (other_vt[:, cols] - size * pair[b][1][step]).T
        for k in range(2):
            layer[2 + k, inner] = cut(res_ref[k, :, cols] + size * shift_ref[k, :, cols])
            for first, base in ((0, beyond_own), (4, beyond_other)):
                rim = base + k
                moved = size * (rim_weight[rim, :, cols] * rim_shift[rim, :, here])
                layer[first + k, inner] = cut(rim_ref[rim, :, cols] + moved)

        def to_once(strip, start, value):
            once[strip, PAD + start : PAD + start + SPAN] = value

        def to_cloud(strip, start, value):
            ref = other_ref if strip else own_ref
            ref[start : start + SPAN, there] = level * value

        smooth_rows(layer, to_once, keep_own, keep_other, 1, 3)
        smooth_rows(once, to_cloud, keep_own, keep_other, 0, 2)


def summed_over_chips(even, odd, held, beside):
    chips = lax.axis_size("pix") // 2
    count, rank, lanes = even.shape
    from_odd = along_pix(odd, 2)
    shapes = [shaped(rank, lanes)] * count + [shaped(*x.shape) for x in held]
    kept = call(
        add_kernel, [VMEM] * (2 + len(held)), [VMEM] * len(shapes), shapes, [], even, from_odd, *held, beside=beside,
    )
    mine = plus(kept[0], *[along_pix(kept[k], 4 * k) for k in (1, 2, 3)])
    distance = GROUP
    while distance < chips:
        mine = plus(mine, along_pix(mine, 2 * distance))
        distance *= 2
    parts = [mine] + [along_pix(mine, 4 * k) for k in (1, 2, 3)]
    return parts, from_odd, kept[count:]


def per_device(observed, valid_mask, pix_factor, col_factor):
    pix_count = lax.axis_size("pix")
    col_count = lax.axis_size("col")
    chips = pix_count // 2
    pixels, columns = observed.shape
    rank = pix_factor.shape[1]
    half = columns // 2
    dates = valid_mask.shape[1] // 2
    total = float(pixels * columns * pix_count * col_count)
    assert pixels == WIDTH and half == GROUP * LANES and chips % GROUP == 0 and PASSES == 2
    index = lax.axis_index("pix")
    core = index % 2
    chip = index // 2
    place = jnp.stack([core, chip % GROUP, chip]).astype(jnp.int32)

    both = 2 * pixels
    wide = 2 * LANES
    steps = half // wide
    sums_shape = shaped(8, LANES)
    pix_shape = shaped(pixels, rank)
    grad_shape = shaped(steps, rank, LANES)
    vt_shape = pltpu.VMEM((rank, half), f32)
    local = pltpu.VMEM((both, half), f32)
    strip = pltpu.VMEM((pixels, half), f32)
    factor_scratch = [pltpu.VMEM((both, 3 * rank), bf16)]

    unit = pixels // 32
    own_rows, other_rows = [13 * unit, 13 * unit, 6 * unit], [7 * unit, 12 * unit, 13 * unit]

    def pieces(rows):
        return [pltpu.VMEM((n, half + dates), f32) for n in rows]

    half_in = [pl.BlockSpec((pixels, half), lambda t, s: (0, s[0])), pl.BlockSpec((pixels, dates), lambda t, s: (0, s[0]))]
    other_pieces = call(
        pack_kernel, half_in, [VMEM] * 3, pieces(other_rows), [], in_hbm(observed), in_hbm(valid_mask),
        grid=(1,), place=jnp.reshape(1 - core, (1,)).astype(jnp.int32),
    )
    received = [along_pix(piece, 1) for piece in other_pieces]
    own_u, other_u = pix_factor, along_pix(pix_factor, 1)
    *own_pieces, vt, own_res, own_weight, own_sum = call(
        own_kernel, half_in + [pl.BlockSpec((half, rank), lambda t, s: (s[0], 0)), VMEM], [VMEM] * 7,
        pieces(own_rows) + [vt_shape, strip, strip, shaped(8, wide)], [],
        in_hbm(observed), in_hbm(valid_mask), in_hbm(col_factor), own_u, grid=(1,), place=place,
    )
    near_own, near_other, far_own, far_other = [None] * 3, [None] * 3, [None] * 3, [None] * 3
    near_own[0] = to_near(own_pieces[0], 0)
    residual, weight, sums = call(
        other_kernel, [SMEM] + [VMEM] * 8, [VMEM] * 3, [local, local, sums_shape], [],
        place, *received, other_u, in_vmem(vt), in_vmem(own_res), in_vmem(own_weight), own_sum,
    )
    level_sums = everywhere(sums, late=True)

    for iteration in range(ITERS):
        first = iteration == 0
        if first:
            near_own[1] = to_near(held_until(own_pieces[1], level_sums), 0)
            near_own[0] = held_until(near_own[0], level_sums)
            far_own[0] = to_far(near_own[0])
            passed = [near_own[1], far_own[0]]
            own_part, other_part = call(
                functools.partial(first_grad_kernel, total), [VMEM] * 3, [VMEM] * 2, [pix_shape] * 2, [],
                level_sums, in_vmem(residual), in_vmem(vt), after=near_own[:1],
            )
        else:
            near_other[2] = to_near(held_until(other_pieces[2], level_sums), 1)
            near_other[1] = held_until(near_other[1], level_sums)
            far_other[1] = to_far(near_other[1])
            passed = [near_other[2], far_other[1]]
            residual, vt, own_part, other_part = call(
                functools.partial(next_grad_kernel, total), [VMEM] * 6, [VMEM] * 4,
                [local, vt_shape, pix_shape, pix_shape], [],
                level_sums, in_vmem(residual), in_vmem(shift), in_vmem(vt), even, odd, after=[far_own[2], far_other[0]],
            )
        own_grad = summed_over_col(plus(own_part, along_pix(other_part, 1)))
        other_grad = along_pix(own_grad, 1)
        change, sums = call(
            functools.partial(change_kernel, col_count), [VMEM] * 4, [VMEM] * 2,
            [local, sums_shape], factor_scratch, own_grad, other_grad, in_vmem(vt), in_vmem(weight),
            beside=[residual],
        )
        pix_sums = everywhere(sums)
        own_u, other_u, residual, even, odd = call(
            functools.partial(pix_step_kernel, total, first), [VMEM] * 8, [VMEM] * 5,
            [pix_shape, pix_shape, local, grad_shape, grad_shape], [pltpu.VMEM((rank, 3 * both), bf16)],
            level_sums, pix_sums, own_u, other_u, own_grad, other_grad, in_vmem(residual),
            in_vmem(change), after=passed, beside=[vt, weight],
        )
        alive = [residual, vt, weight, own_u, other_u]
        if first:
            near_own[1] = held_until(near_own[1], odd)
            far_own[1] = to_far(near_own[1])
            parts, moved, _ = summed_over_chips(even, odd, [], alive)
            near_own[2] = to_near(held_until(own_pieces[2], moved), 0)
            near_other[0] = to_near(held_until(other_pieces[0], moved), 1)
            near_other[1] = to_near(held_until(other_pieces[1], moved), 1)
            passed = [far_own[1], near_own[2], near_other[0], near_other[1]]
        else:
            near_other[2] = held_until(near_other[2], odd)
            far_other[2] = to_far(near_other[2])
            parts, moved, sent = summed_over_chips(even, odd, [own_u], alive)
            near_u = to_near(sent[0], 0)
            other_vt = along_pix(vt, 1)
            passed = [far_other[2], near_u]
        (even,) = call(
            stack_kernel, [VMEM] * steps, [VMEM], [grad_shape], [], *parts, after=passed, beside=alive,
        )
        odd = along_pix(even, 2)
        if first:
            near_own[2] = held_until(near_own[2], even)
            near_other[0] = held_until(near_other[0], even)
            far_own[2] = to_far(near_own[2])
            far_other[0] = to_far(near_other[0])
        else:
            near_u = held_until(near_u, even)
            far_u = to_far(near_u)
        shift, sums = call(
            functools.partial(shift_kernel, chips), [VMEM] * 6, [VMEM] * 2,
            [local, sums_shape], factor_scratch, own_u, other_u, even, odd, in_vmem(weight),
            in_vmem(residual), beside=[vt],
        )
        level_sums = everywhere(sums)

    factors = [near_u, along_pix(near_u, 1), far_u, along_pix(far_u, 1)]
    rim_scratch = [pltpu.VMEM((2 * both, 3 * rank), bf16)]
    rim_shape = pltpu.VMEM((4, pixels, half), f32)
    rim_res, rim_weight = call(
        rim_kernel, [SMEM] + [VMEM] * 17, [VMEM] * 2, [rim_shape] * 2, rim_scratch,
        place, *near_own, *near_other, *far_own, *far_other, *factors, in_vmem(vt), after=[sums],
    )
    grads = [even, odd, along_pix(even, 1), along_pix(odd, 1)]
    pair = lambda s, t: s[1] // 2 ^ t
    own_cloud, other_cloud, v = call(
        functools.partial(smooth_kernel, total, chips), [VMEM] * 15,
        [
            pl.BlockSpec((pixels, wide), lambda t, s: (0, s[0] * steps + pair(s, t))),
            pl.BlockSpec((pixels, wide), lambda t, s: (0, pair(s, t))),
            pl.BlockSpec((2, wide, rank), lambda t, s: (0, pair(s, t), 0)),
        ],
        [shaped(pixels, columns), shaped(pixels, half), shaped(2, half, rank)],
        rim_scratch + [
            pltpu.VMEM((4, pixels, wide), f32),
            pltpu.VMEM((6, pixels + 2 * PAD, LANES), f32),
            pltpu.VMEM((4, pixels + 2 * PAD, LANES), f32),
        ],
        level_sums, in_vmem(residual.reshape(2, pixels, half)), in_vmem(shift.reshape(2, pixels, half)),
        in_vmem(rim_res), in_vmem(rim_weight), *factors, in_vmem(vt), other_vt, *grads, grid=(steps,), place=place,
    )
    from_other = along_pix(other_cloud, 1)
    cloud = lax.dynamic_update_slice(own_cloud, from_other, (0, (1 - core) * half))
    return own_u, v.reshape(columns, rank), cloud


def solution(mesh):
    in_specs = (P("pix", "col"), P("pix", "col"), P("pix", None), P("col", None))
    out_specs = (P("pix", None), P("col", None), P("pix", "col"))
    return jax.shard_map(
        per_device, mesh=mesh, in_specs=in_specs, out_specs=out_specs, check_vma=False
    )
```

```python
import functools

import jax
import jax.numpy as jnp
from jax import lax
from jax.experimental import pallas as pl
from jax.experimental.pallas import tpu as pltpu
from jax.sharding import PartitionSpec as P

BANDS = 8
WIDTH = 256
ITERS = 2
PASSES = 2
LANES = 128
GROUP = 8

threshold_scale = 1.0
diffusion = 0.2
f32 = jnp.float32
bf16 = jnp.bfloat16


def along_pix(block, distance):
    count = lax.axis_size("pix")
    return lax.ppermute(block, "pix", [(i, i ^ distance) for i in range(count)])


def to_near(block, crossed):
    count = lax.axis_size("pix")
    return lax.ppermute(block, "pix", [(i, i ^ 2 ^ crossed) for i in range(count)])


def to_far(block):
    count = lax.axis_size("pix")
    route = [(i, i + (4 if i // 2 % 2 == 0 else -4)) for i in range(count)]
    return lax.ppermute(block, "pix", [(a, b) for a, b in route if 0 <= b < count])


def summed_over_col(block):
    count = lax.axis_size("col")
    step = 1
    while step < count:
        block = plus(block, lax.ppermute(block, "col", [(i, i ^ step) for i in range(count)]))
        step *= 2
    return block


def everywhere(sums, late=False, beside=None):
    count = lax.axis_size("col")
    devices = lax.axis_size("pix") * count
    bits = [count << k for k in range(1, (devices // count).bit_length() - 1)]
    bits = [bits[0]] + [1 << k for k in range(count.bit_length() - 1)] + bits[1:]
    stages = [[count]] + [bits[k : k + 2] for k in range(0, len(bits), 2)]
    if late:
        stages = stages[:1] + stages[:0:-1]
    for stage in stages:
        moves = [0]
        for bit in stage:
            moves += [move ^ bit for move in moves]
        parts = [
            lax.ppermute(sums, ("pix", "col"), [(i, i ^ move) for i in range(devices)]) for move in moves[1:]
        ]
        sums = plus(sums, *parts, after=extra[-1:] if beside and stage is stages[2] else ())
        if beside and stage is stages[1]:
            extra = beside(sums)
    return (sums, extra) if beside else sums


def halves(x):
    high = x.astype(bf16)
    return high, (x - high.astype(f32)).astype(bf16)


def left_parts(x, axis):
    high, low = halves(x)
    return jnp.concatenate([high, high, low], axis=axis)


def right_parts(x, axis):
    high, low = halves(x)
    return jnp.concatenate([high, low, high], axis=axis)


def product(a, b, summed=0):
    return lax.dot_general(a, b, (((1,), (summed,)), ((), ())), preferred_element_type=f32)


def rows_folded(x):
    return jnp.sum(x.reshape(x.shape[0] // 8, 8, x.shape[1]), axis=0)


def whole_sum(x):
    return jnp.sum(jnp.sum(x, axis=0, keepdims=True), axis=1, keepdims=True)


def packed_sums(shape, sums):
    lane = lax.broadcasted_iota(jnp.int32, shape, 1)
    row = lax.broadcasted_iota(jnp.int32, shape, 0)
    packed = jnp.zeros(shape, f32)
    for place, value in enumerate(sums):
        packed = packed + jnp.where((lane == place) & (row == 0), value, 0.0)
    return packed


def read_sums(ref, count):
    total = jnp.sum(ref[...], axis=0, keepdims=True)
    return [total[:, k : k + 1] for k in range(count)]


def spread_mask(mask, chip, step):
    dates = mask.shape[1]
    date = lax.broadcasted_iota(jnp.int32, (dates, 2 * LANES), 0)
    lane = lax.broadcasted_iota(jnp.int32, (dates, 2 * LANES), 1)
    chunk = chip ^ (2 * step + lane // LANES)
    pick = (date == chunk * (LANES // BANDS) + lane % LANES // BANDS).astype(bf16)
    return jnp.dot(mask.astype(f32).astype(bf16), pick, preferred_element_type=f32)


SMEM = pl.BlockSpec(memory_space=pltpu.SMEM)
VMEM = pl.BlockSpec(memory_space=pltpu.VMEM)
ANY = pl.BlockSpec(memory_space=pl.ANY)


def call(kernel, in_specs, out_specs, out_shape, scratch, *args, grid=(), place=None, after=(), beside=()):
    inputs = len(in_specs)
    lead = 0 if place is None else 1

    def body(*refs):
        used = lead + inputs
        kernel(*refs[:used], *refs[used + len(after) + len(beside) :])

    results = pl.pallas_call(
        body,
        grid_spec=pltpu.PrefetchScalarGridSpec(
            num_scalar_prefetch=lead,
            grid=grid,
            in_specs=list(in_specs) + [ANY] * len(after) + [VMEM] * len(beside),
            out_specs=list(out_specs),
            scratch_shapes=scratch,
        ),
        out_shape=list(out_shape),
        compiler_params=pltpu.CompilerParams(vmem_limit_bytes=16 * 2**20),
    )(*([place] if lead else []), *args, *after, *[in_vmem(x) for x in beside])
    return list(results)


def plus_kernel(*refs):
    total = refs[0][...]
    for ref in refs[1:-1]:
        total = total + ref[...]
    refs[-1][...] = total


def plus(*arrays, after=()):
    (total,) = call(plus_kernel, [VMEM] * len(arrays), [VMEM], [shaped(*arrays[0].shape)], [], *arrays, after=after)
    return total


def in_vmem(array):
    return pltpu.with_memory_space_constraint(array, pltpu.VMEM)


def in_hbm(array):
    return pltpu.with_memory_space_constraint(array, pltpu.HBM)


def held_until(array, *after):
    def body(*refs):
        pass

    return pl.pallas_call(
        body,
        in_specs=[ANY] * (1 + len(after)),
        out_specs=ANY,
        out_shape=jax.ShapeDtypeStruct(array.shape, array.dtype),
        input_output_aliases={0: 0},
        compiler_params=pltpu.CompilerParams(vmem_limit_bytes=2**20),
    )(array, *after)


def shaped(*shape):
    return jax.ShapeDtypeStruct(shape, f32)


def tiles(ref):
    return [slice(start, start + 2 * LANES) for start in range(0, ref.shape[-1], 2 * LANES)]


def pack_strip(obs_ref, mask_ref, out_refs):
    columns = obs_ref.shape[1]
    start = 0
    for ref in out_refs:
        rows = slice(start, start + ref.shape[0])
        ref[:, :columns] = obs_ref[rows]
        ref[:, columns:] = mask_ref[rows].astype(f32)
        start += ref.shape[0]


def pack_kernel(which, obs_ref, mask_ref, *out_refs):
    pack_strip(obs_ref, mask_ref, out_refs)


def split_factor(refs, parts_ref):
    pixels = refs[0].shape[0]
    for part, ref in enumerate(refs):
        parts_ref[part * pixels : (part + 1) * pixels] = left_parts(ref[...], 1)


def chunk_starts(chip, step):
    return [pl.multiple_of((chip ^ (2 * step + b)) * LANES, LANES) for b in range(2)]


def own_kernel(place, obs_ref, mask_ref, v_ref, u_ref, *refs):
    vt_ref, res_ref, weight_ref, sum_ref = refs[-4:]
    pack_strip(obs_ref, mask_ref, refs[:-4])
    u = left_parts(u_ref[...], 1)
    spread = 0.0
    for step, cols in enumerate(tiles(vt_ref)):
        starts = chunk_starts(place[1], step)
        vt = jnp.concatenate([v_ref[pl.ds(start, LANES)].T for start in starts], axis=1)
        vt_ref[:, cols] = vt
        weight = spread_mask(mask_ref[...], place[1], step)
        obs = jnp.concatenate([obs_ref[:, pl.ds(start, LANES)] for start in starts], axis=1)
        res = weight * (obs - product(u, right_parts(vt, 0)))
        weight_ref[:, cols] = weight
        res_ref[:, cols] = res
        spread = spread + rows_folded(res * res)
    sum_ref[...] = spread


def residual_of_pieces(pieces, chip, step, low_rank):
    half = pieces[0].shape[1] // (BANDS + 1) * BANDS
    start = 0
    for piece in pieces:
        rows = slice(start, start + piece.shape[0])
        weight = spread_mask(piece[:, half:], chip, step)
        obs = jnp.concatenate([piece[:, pl.ds(first, LANES)] for first in chunk_starts(chip, step)], axis=1)
        yield rows, weight * (obs - low_rank[rows]), weight
        start += piece.shape[0]


def other_kernel(place, *refs):
    pieces = refs[:-8]
    u_ref, vt_ref, own_res, own_weight, own_sum, res_ref, weight_ref, sums_ref = refs[-8:]
    pixels = own_res.shape[0]
    res_ref[:pixels] = own_res[...]
    weight_ref[:pixels] = own_weight[...]
    u = left_parts(u_ref[...], 1)
    spread = own_sum[...]
    for step, cols in enumerate(tiles(vt_ref)):
        low_rank = product(u, right_parts(vt_ref[:, cols], 0))
        for rows, res, weight in residual_of_pieces(pieces, place[1], step, low_rank):
            below = slice(pixels + rows.start, pixels + rows.stop)
            weight_ref[below, cols] = weight
            res_ref[below, cols] = res
            spread = spread + rows_folded(res * res)
    sums_ref[...] = packed_sums(sums_ref.shape, [whole_sum(spread)])


def level_from(spread, total):
    return threshold_scale * jnp.sqrt(jnp.maximum(spread, 0.0) / total + 1e-06)


def store_parts(grad, own_ref, other_ref):
    pixels = own_ref.shape[0]
    own_ref[...] = grad[:pixels]
    other_ref[...] = grad[pixels:]


def first_grad_kernel(total, sums_ref, res_ref, vt_ref, own_ref, other_ref):
    (spread,) = read_sums(sums_ref, 1)
    level = level_from(spread, total)
    grad = None
    for cols in tiles(res_ref):
        misfit = -jnp.clip(res_ref[:, cols], -level, level)
        part = product(left_parts(misfit, 1), right_parts(vt_ref[:, cols], 1), 1)
        grad = part if grad is None else grad + part
    store_parts(grad, own_ref, other_ref)


def column_sums(sums):
    top, curve, cross, before = sums
    step = top / curve
    return step, before + 2.0 * step * cross + step * step * curve


def next_grad_kernel(total, sums_ref, res_ref, shift_ref, vt_ref, step_ref,
                     res_out, vt_out, own_ref, other_ref):
    size, spread = column_sums(read_sums(sums_ref, 4))
    level = level_from(spread, total)
    grad = None
    for cols in tiles(res_ref):
        vt = vt_ref[:, cols] - size * step_ref[:, cols]
        vt_out[:, cols] = vt
        res = res_ref[:, cols] + size * shift_ref[:, cols]
        res_out[:, cols] = res
        misfit = -jnp.clip(res, -level, level)
        part = product(left_parts(misfit, 1), right_parts(vt, 1), 1)
        grad = part if grad is None else grad + part
    store_parts(grad, own_ref, other_ref)


def change_kernel(col_count, own_grad, other_grad, vt_ref, weight_ref, change_ref, sums_ref, g_parts):
    split_factor((own_grad, other_grad), g_parts)
    curve = 0.0
    for cols in tiles(vt_ref):
        change = weight_ref[:, cols] * product(g_parts[...], right_parts(vt_ref[:, cols], 0))
        change_ref[:, cols] = change
        curve = curve + rows_folded(change * change)
    top = whole_sum(own_grad[...] * own_grad[...]) / col_count
    sums_ref[...] = packed_sums(sums_ref.shape, [top, whole_sum(curve)])


def pix_step_kernel(total, first, level_sums, sums_ref, own_u, other_u, own_grad, other_grad, res_ref,
                    change_ref, own_out, other_out, res_out, copy_ref, even_ref, odd_ref, ut_parts):
    pixels = own_grad.shape[0]
    top, curve = read_sums(sums_ref, 2)
    size = top / curve
    if first:
        (spread,) = read_sums(level_sums, 1)
    else:
        _, spread = column_sums(read_sums(level_sums, 4))
    level = level_from(spread, total)
    strips = ((own_u, own_grad, own_out), (other_u, other_grad, other_out))
    for part, (old, grad, out) in enumerate(strips):
        u = old[...] - size * grad[...]
        out[...] = u
        if part == 0:
            copy_ref[...] = u
        high, low = halves(u.T)
        for k, value in enumerate((high, high, low)):
            first_col = (2 * k + part) * pixels
            ut_parts[:, first_col : first_col + pixels] = value
    for k, cols in enumerate(tiles(res_ref)):
        res = res_ref[:, cols]
        moved = size * change_ref[:, cols]
        res_out[:, cols] = res + moved
        misfit = -(jnp.clip(res, -level, level) + moved)
        grad = product(ut_parts[...], right_parts(misfit, 0))
        even_ref[k] = grad[:, :LANES]
        odd_ref[k] = grad[:, LANES:]


def shift_kernel(chips, own_u, other_u, weight_ref, res_ref, *refs):
    chunk_refs = refs[:GROUP]
    shift_ref, grad_ref, sums_ref, u_parts = refs[GROUP:]
    split_factor((own_u, other_u), u_parts)
    top = curve = cross = spread = 0.0
    for k, cols in enumerate(tiles(res_ref)):
        grad = jnp.concatenate([chunk_refs[2 * k][...], chunk_refs[2 * k + 1][...]], axis=1)
        grad_ref[:, cols] = grad
        top = top + rows_folded(grad * grad)
        shift = weight_ref[:, cols] * product(u_parts[...], right_parts(grad, 0))
        shift_ref[:, cols] = shift
        res = res_ref[:, cols]
        curve = curve + rows_folded(shift * shift)
        cross = cross + rows_folded(shift * res)
        spread = spread + rows_folded(res * res)
    sums = [whole_sum(top) / chips, whole_sum(curve), whole_sum(cross), whole_sum(spread)]
    sums_ref[...] = packed_sums(sums_ref.shape, sums)


def rim_kernel(place, *refs):
    packs = [refs[3 * k : 3 * k + 3] for k in range(4)]
    factors = refs[12:16]
    vt_ref, res_ref, weight_ref, u_parts = refs[16:]
    pixels = factors[0].shape[0]
    split_factor(factors, u_parts)
    for step, cols in enumerate(tiles(vt_ref)):
        low_rank = product(u_parts[...], right_parts(vt_ref[:, cols], 0))
        for part, pieces in enumerate(packs):
            strip = low_rank[part * pixels : (part + 1) * pixels]
            for rows, res, weight in residual_of_pieces(pieces, place[1], step, strip):
                weight_ref[part, rows, cols] = weight
                res_ref[part, rows, cols] = res


def add_kernel(kept_ref, from_ref, *out_refs):
    for k, ref in enumerate(out_refs):
        ref[...] = kept_ref[k] + from_ref[k]


def flux_of(diff):
    below = 1.0 + diff * diff
    return diff * pl.reciprocal(below, approx=True)


PAD = 8
SPAN = 64


def smooth_rows(source, target, keep_north, keep_south, north_edge, south_edge):
    count = source.shape[0]
    for start in range(0, WIDTH, SPAN):
        row = lax.broadcasted_iota(jnp.int32, (SPAN + 2 * PAD, LANES), 0) + (start - PAD)
        inside = (row >= 0) & (row < WIDTH - 1)
        around = slice(start, start + SPAN + 2 * PAD)
        middle = slice(PAD, PAD + SPAN)
        before = None
        here = source[0, around]
        for k in range(count - 1):
            after = source[k + 1, around]
            cross = flux_of(after[middle] - here[middle])
            if k == north_edge:
                cross = cross * keep_north
            if k == south_edge:
                cross = cross * keep_south
            if k > 0:
                east = flux_of(pltpu.roll(here, SPAN + 2 * PAD - 1, 0) - here)
                east = jnp.where(inside, east, 0.0)
                west = pltpu.roll(east, 1, 0)
                along = east[middle] - west[middle]
                target(k - 1, start, here[middle] + diffusion * ((cross - before) + along))
            before = cross
            here = after


def smooth_kernel(total, chips, place, sums_ref, res_ref, shift_ref, rim_ref, rim_weight, *refs):
    factors = refs[:4]
    own_vt, other_vt, own_grad, other_grad = refs[4:8]
    own_ref, other_ref, v_ref, u_parts, rim_shift, layer, once = refs[8:]
    step = pl.program_id(0)
    core, chip = place[0], place[2]
    pixels = own_ref.shape[0]

    @pl.when(step == 0)
    def _():
        split_factor(factors, u_parts)

    size, spread = column_sums(read_sums(sums_ref, 4))
    level = level_from(spread, total)
    inverse = 1.0 / level
    both_chunks = pl.ds(pl.multiple_of(step * 2 * LANES, 2 * LANES), 2 * LANES)
    moved = product(u_parts[...], right_parts(own_grad[:, both_chunks], 0))
    rim_shift[...] = moved.reshape(rim_shift.shape)

    def cut(res):
        return (res - jnp.clip(res, -level, level)) * inverse

    south = 2 * (chip % 2)
    beyond_own = jnp.where(core == 0, 2 - south, south)
    beyond_other = 2 - beyond_own
    keep_north = jnp.where(chip > 0, 1.0, 0.0).astype(f32)
    keep_south = jnp.where(chip < chips - 1, 1.0, 0.0).astype(f32)
    keep_own = jnp.where(core == 0, keep_north, keep_south)
    keep_other = jnp.where(core == 0, keep_south, keep_north)
    inner = slice(PAD, PAD + pixels)
    for b in range(2):
        cols = pl.ds(pl.multiple_of((2 * step + b) * LANES, LANES), LANES)
        here = slice(b * LANES, (b + 1) * LANES)
        there = pl.ds(pl.multiple_of((chip % 2 ^ b) * LANES, LANES), LANES)
        v_ref[core, there] = (own_vt[:, cols] - size * own_grad[:, cols]).T
        v_ref[1 - core, there] = (other_vt[:, cols] - size * other_grad[:, cols]).T
        for k in range(2):
            layer[2 + k, inner] = cut(res_ref[k, :, cols] + size * shift_ref[k, :, cols])
            for first, base in ((0, beyond_own), (4, beyond_other)):
                rim = base + k
                moved = size * (rim_weight[rim, :, cols] * rim_shift[rim, :, here])
                layer[first + k, inner] = cut(rim_ref[rim, :, cols] + moved)

        def to_once(strip, start, value):
            once[strip, PAD + start : PAD + start + SPAN] = value

        def to_cloud(strip, start, value):
            ref = other_ref if strip else own_ref
            ref[start : start + SPAN, there] = level * value

        smooth_rows(layer, to_once, keep_own, keep_other, 1, 3)
        smooth_rows(once, to_cloud, keep_own, keep_other, 0, 2)


def summed_over_chips(even, odd, meanwhile):
    chips = lax.axis_size("pix") // 2
    count, rank, lanes = even.shape
    from_odd = along_pix(odd, 2)
    kept = call(add_kernel, [VMEM] * 2, [VMEM] * count, [shaped(rank, lanes)] * count, [], even, from_odd)
    before_sum, before_end = meanwhile(from_odd)
    mine = plus(kept[0], *[along_pix(kept[k], 4 * k) for k in (1, 2, 3)], after=before_sum)
    distance = GROUP
    while distance < chips:
        mine = plus(mine, along_pix(mine, 2 * distance))
        distance *= 2
    parts = [mine] + [along_pix(mine, 4 * k) for k in (1, 2, 3)]
    parts[3] = held_until(parts[3], *before_end)
    summed = []
    for part in parts:
        summed += [part, along_pix(part, 2)]
    return summed


def per_device(observed, valid_mask, pix_factor, col_factor):
    pix_count = lax.axis_size("pix")
    col_count = lax.axis_size("col")
    chips = pix_count // 2
    pixels, columns = observed.shape
    rank = pix_factor.shape[1]
    half = columns // 2
    dates = valid_mask.shape[1] // 2
    total = float(pixels * columns * pix_count * col_count)
    assert pixels == WIDTH and half == GROUP * LANES and chips % GROUP == 0 and PASSES == 2
    index = lax.axis_index("pix")
    core = index % 2
    chip = index // 2
    place = jnp.stack([core, chip % GROUP, chip]).astype(jnp.int32)

    both = 2 * pixels
    wide = 2 * LANES
    steps = half // wide
    sums_shape = shaped(8, LANES)
    pix_shape = shaped(pixels, rank)
    half_shape = shaped(steps, rank, LANES)
    vt_shape = pltpu.VMEM((rank, half), f32)
    local = pltpu.VMEM((both, half), f32)
    strip = pltpu.VMEM((pixels, half), f32)
    factor_scratch = [pltpu.VMEM((both, 3 * rank), bf16)]

    unit = pixels // 32
    own_rows, other_rows = [13 * unit, 13 * unit, 6 * unit], [7 * unit, 12 * unit, 13 * unit]

    def pieces(rows):
        return [pltpu.VMEM((n, half + dates), f32) for n in rows]

    half_in = [pl.BlockSpec((pixels, half), lambda t, s: (0, s[0])), pl.BlockSpec((pixels, dates), lambda t, s: (0, s[0]))]
    other_pieces = call(
        pack_kernel, half_in, [VMEM] * 3, pieces(other_rows), [], in_hbm(observed), in_hbm(valid_mask),
        grid=(1,), place=jnp.reshape(1 - core, (1,)).astype(jnp.int32),
    )
    received = [along_pix(piece, 1) for piece in other_pieces]
    own_u, other_u = pix_factor, along_pix(pix_factor, 1)
    *own_pieces, vt, own_res, own_weight, own_sum = call(
        own_kernel, half_in + [pl.BlockSpec((half, rank), lambda t, s: (s[0], 0)), VMEM], [VMEM] * 7,
        pieces(own_rows) + [vt_shape, strip, strip, shaped(8, wide)], [],
        in_hbm(observed), in_hbm(valid_mask), in_hbm(col_factor), own_u, grid=(1,), place=place, after=[other_u],
    )
    near_own, near_other, far_own, far_other = [None] * 3, [None] * 3, [None] * 3, [None] * 3
    near_own[0] = to_near(held_until(own_pieces[0], *received), 0)
    residual, weight, sums = call(
        other_kernel, [SMEM] + [VMEM] * 8, [VMEM] * 3, [local, local, sums_shape], [],
        place, *received, other_u, in_vmem(vt), in_vmem(own_res), in_vmem(own_weight), own_sum,
    )
    level_sums = everywhere(sums, late=True)

    for iteration in range(ITERS):
        first = iteration == 0
        if first:
            near_own[1] = to_near(held_until(own_pieces[1], level_sums), 0)
            near_own[0] = held_until(near_own[0], level_sums)
            far_own[0] = to_far(near_own[0])
            passed = [near_own[1], far_own[0]]
            own_part, other_part = call(
                functools.partial(first_grad_kernel, total), [VMEM] * 3, [VMEM] * 2, [pix_shape] * 2, [],
                level_sums, in_vmem(residual), in_vmem(vt), after=near_own[:1],
            )
        else:
            near_other[2] = to_near(held_until(other_pieces[2], level_sums), 1)
            near_other[1] = held_until(near_other[1], level_sums)
            far_other[1] = to_far(near_other[1])
            passed = [near_other[2], far_other[1]]
            residual, vt, own_part, other_part = call(
                functools.partial(next_grad_kernel, total), [VMEM] * 5, [VMEM] * 4,
                [local, vt_shape, pix_shape, pix_shape], [],
                level_sums, in_vmem(residual), in_vmem(shift), in_vmem(vt), in_vmem(grad), after=[far_own[2], far_other[0]],
            )
        own_grad = summed_over_col(plus(own_part, along_pix(other_part, 1)))
        other_grad = along_pix(own_grad, 1)
        change, sums = call(
            functools.partial(change_kernel, col_count), [VMEM] * 4, [VMEM] * 2,
            [local, sums_shape], factor_scratch, own_grad, other_grad, in_vmem(vt), in_vmem(weight),
            beside=[residual],
        )
        pix_sums = everywhere(sums)
        u_next, other_u, residual, own_u, even, odd = call(
            functools.partial(pix_step_kernel, total, first), [VMEM] * 8, [VMEM] * 6,
            [pix_shape, pix_shape, local, pix_shape, half_shape, half_shape], [pltpu.VMEM((rank, 3 * both), bf16)],
            level_sums, pix_sums, own_u, other_u, own_grad, other_grad, in_vmem(residual),
            in_vmem(change), after=passed, beside=[vt, weight],
        )
        if first:
            near_own[1] = held_until(near_own[1], odd)
            far_own[1] = to_far(near_own[1])

            def meanwhile(moved):
                near_own[2] = to_near(held_until(own_pieces[2], moved), 0)
                near_other[0] = to_near(held_until(other_pieces[0], moved), 1)
                near_other[1] = to_near(held_until(other_pieces[1], moved), 1)
                return [], [far_own[1], near_own[2], near_other[0]]

        else:
            near_other[2] = held_until(near_other[2], odd)
            far_other[2] = to_far(near_other[2])
            sent = []

            def meanwhile(moved):
                sent.append(held_until(own_u, moved))
                sent.append(to_near(sent[0], 0))
                return [], [far_other[2], sent[1]]

            other_vt = along_pix(vt, 1)
        summed = summed_over_chips(even, odd, meanwhile)
        if first:
            near_own[2] = held_until(near_own[2], summed[6])
            near_other[0] = held_until(near_other[0], summed[6])
            far_own[2] = to_far(near_own[2])
            far_other[0] = to_far(near_other[0])
            passed = near_other[1:2]
        else:
            own_u = sent[0]
            near_u = held_until(sent[1], summed[6])
            far_u = to_far(near_u)
            passed = [far_u]
        shift, grad, sums = call(
            functools.partial(shift_kernel, chips), [VMEM] * (4 + GROUP), [VMEM] * 3,
            [local, vt_shape, sums_shape], factor_scratch, own_u, other_u, in_vmem(weight), in_vmem(residual),
            *summed, after=passed, beside=[vt],
        )
        if first:
            level_sums = everywhere(sums)

    near_other_u = along_pix(near_u, 1)
    rim_scratch = [pltpu.VMEM((2 * both, 3 * rank), bf16)]
    rim_shape = pltpu.VMEM((4, pixels, half), f32)

    def rim(group_sums):
        far = held_until(far_u, group_sums)
        factors = [near_u, near_other_u, far, along_pix(far, 1)]
        other_grad = along_pix(held_until(grad, group_sums), 1)
        return factors, other_grad, *call(
            rim_kernel, [SMEM] + [VMEM] * 17, [VMEM] * 2, [rim_shape] * 2, rim_scratch,
            place, *near_own, *near_other, *far_own, *far_other, *factors, in_vmem(vt), after=[group_sums],
        )

    level_sums, (factors, other_grad, rim_res, rim_weight) = everywhere(sums, beside=rim)
    pair = lambda s, t: s[1] // 2 ^ t
    own_cloud, other_cloud, v = call(
        functools.partial(smooth_kernel, total, chips), [VMEM] * 13,
        [
            pl.BlockSpec((pixels, wide), lambda t, s: (0, s[0] * steps + pair(s, t))),
            pl.BlockSpec((pixels, wide), lambda t, s: (0, pair(s, t))),
            pl.BlockSpec((2, wide, rank), lambda t, s: (0, pair(s, t), 0)),
        ],
        [shaped(pixels, columns), shaped(pixels, half), shaped(2, half, rank)],
        rim_scratch + [
            pltpu.VMEM((4, pixels, wide), f32),
            pltpu.VMEM((6, pixels + 2 * PAD, LANES), f32),
            pltpu.VMEM((4, pixels + 2 * PAD, LANES), f32),
        ],
        level_sums, in_vmem(residual.reshape(2, pixels, half)), in_vmem(shift.reshape(2, pixels, half)),
        in_vmem(rim_res), in_vmem(rim_weight), *factors, in_vmem(vt), other_vt, in_vmem(grad),
        other_grad, grid=(steps,), place=place,
    )
    from_other = along_pix(other_cloud, 1)
    cloud = lax.dynamic_update_slice(own_cloud, from_other, (0, (1 - core) * half))
    return u_next, v.reshape(columns, rank), cloud


def solution(mesh):
    in_specs = (P("pix", "col"), P("pix", "col"), P("pix", None), P("col", None))
    out_specs = (P("pix", None), P("col", None), P("pix", "col"))
    return jax.shard_map(
        per_device, mesh=mesh, in_specs=in_specs, out_specs=out_specs, check_vma=False
    )
```

```python
import functools

import jax
import jax.numpy as jnp
from jax import lax
from jax.experimental import pallas as pl
from jax.experimental.pallas import tpu as pltpu
from jax.sharding import PartitionSpec as P

BANDS = 8
WIDTH = 256
ITERS = 2
PASSES = 2
LANES = 128
GROUP = 8

threshold_scale = 1.0
diffusion = 0.2
f32 = jnp.float32
bf16 = jnp.bfloat16


def along_pix(block, distance):
    count = lax.axis_size("pix")
    return lax.ppermute(block, "pix", [(i, i ^ distance) for i in range(count)])


def to_near(block, crossed):
    count = lax.axis_size("pix")
    return lax.ppermute(block, "pix", [(i, i ^ 2 ^ crossed) for i in range(count)])


def to_far(block):
    count = lax.axis_size("pix")
    route = [(i, i + (4 if i // 2 % 2 == 0 else -4)) for i in range(count)]
    return lax.ppermute(block, "pix", [(a, b) for a, b in route if 0 <= b < count])


def summed_over_col(block):
    count = lax.axis_size("col")
    step = 1
    while step < count:
        block = plus(block, lax.ppermute(block, "col", [(i, i ^ step) for i in range(count)]))
        step *= 2
    return block


def everywhere(sums, late=False, beside=None):
    count = lax.axis_size("col")
    devices = lax.axis_size("pix") * count
    bits = [count << k for k in range(1, (devices // count).bit_length() - 1)]
    bits = [bits[0]] + [1 << k for k in range(count.bit_length() - 1)] + bits[1:]
    stages = [[count]] + [bits[k : k + 2] for k in range(0, len(bits), 2)]
    if late:
        stages = stages[:1] + stages[:0:-1]
    for stage in stages:
        moves = [0]
        for bit in stage:
            moves += [move ^ bit for move in moves]
        parts = [
            lax.ppermute(sums, ("pix", "col"), [(i, i ^ move) for i in range(devices)]) for move in moves[1:]
        ]
        sums = plus(sums, *parts, after=extra[-1:] if beside and stage is stages[2] else ())
        if beside and stage is stages[1]:
            extra = beside(sums)
    return (sums, extra) if beside else sums


def halves(x):
    high = x.astype(bf16)
    return high, (x - high.astype(f32)).astype(bf16)


def left_parts(x, axis):
    high, low = halves(x)
    return jnp.concatenate([high, high, low], axis=axis)


def right_parts(x, axis):
    high, low = halves(x)
    return jnp.concatenate([high, low, high], axis=axis)


def product(a, b, summed=0):
    return lax.dot_general(a, b, (((1,), (summed,)), ((), ())), preferred_element_type=f32)


def rows_folded(x):
    return jnp.sum(x.reshape(x.shape[0] // 8, 8, x.shape[1]), axis=0)


def whole_sum(x):
    return jnp.sum(jnp.sum(x, axis=0, keepdims=True), axis=1, keepdims=True)


def packed_sums(shape, sums):
    lane = lax.broadcasted_iota(jnp.int32, shape, 1)
    row = lax.broadcasted_iota(jnp.int32, shape, 0)
    packed = jnp.zeros(shape, f32)
    for place, value in enumerate(sums):
        packed = packed + jnp.where((lane == place) & (row == 0), value, 0.0)
    return packed


def read_sums(ref, count):
    total = jnp.sum(ref[...], axis=0, keepdims=True)
    return [total[:, k : k + 1] for k in range(count)]


def spread_mask(mask, chip, step):
    dates = mask.shape[1]
    date = lax.broadcasted_iota(jnp.int32, (dates, 2 * LANES), 0)
    lane = lax.broadcasted_iota(jnp.int32, (dates, 2 * LANES), 1)
    chunk = chip ^ (2 * step + lane // LANES)
    pick = (date == chunk * (LANES // BANDS) + lane % LANES // BANDS).astype(bf16)
    return jnp.dot(mask.astype(f32).astype(bf16), pick, preferred_element_type=f32)


SMEM = pl.BlockSpec(memory_space=pltpu.SMEM)
VMEM = pl.BlockSpec(memory_space=pltpu.VMEM)
ANY = pl.BlockSpec(memory_space=pl.ANY)


def call(kernel, in_specs, out_specs, out_shape, scratch, *args, grid=(), place=None, after=(), beside=()):
    inputs = len(in_specs)
    lead = 0 if place is None else 1

    def body(*refs):
        used = lead + inputs
        kernel(*refs[:used], *refs[used + len(after) + len(beside) :])

    results = pl.pallas_call(
        body,
        grid_spec=pltpu.PrefetchScalarGridSpec(
            num_scalar_prefetch=lead,
            grid=grid,
            in_specs=list(in_specs) + [ANY] * len(after) + [VMEM] * len(beside),
            out_specs=list(out_specs),
            scratch_shapes=scratch,
        ),
        out_shape=list(out_shape),
        compiler_params=pltpu.CompilerParams(vmem_limit_bytes=16 * 2**20),
    )(*([place] if lead else []), *args, *after, *[in_vmem(x) for x in beside])
    return list(results)


def plus_kernel(*refs):
    total = refs[0][...]
    for ref in refs[1:-1]:
        total = total + ref[...]
    refs[-1][...] = total


def plus(*arrays, after=()):
    (total,) = call(plus_kernel, [VMEM] * len(arrays), [VMEM], [shaped(*arrays[0].shape)], [], *arrays, after=after)
    return total


def in_vmem(array):
    return pltpu.with_memory_space_constraint(array, pltpu.VMEM)


def in_hbm(array):
    return pltpu.with_memory_space_constraint(array, pltpu.HBM)


def held_until(array, *after):
    def body(*refs):
        pass

    return pl.pallas_call(
        body,
        in_specs=[ANY] * (1 + len(after)),
        out_specs=ANY,
        out_shape=jax.ShapeDtypeStruct(array.shape, array.dtype),
        input_output_aliases={0: 0},
        compiler_params=pltpu.CompilerParams(vmem_limit_bytes=2**20),
    )(array, *after)


def shaped(*shape):
    return jax.ShapeDtypeStruct(shape, f32)


def tiles(ref):
    return [slice(start, start + 2 * LANES) for start in range(0, ref.shape[-1], 2 * LANES)]


def pack_strip(obs_ref, mask_ref, out_refs):
    columns = obs_ref.shape[1]
    start = 0
    for ref in out_refs:
        rows = slice(start, start + ref.shape[0])
        ref[:, :columns] = obs_ref[rows]
        ref[:, columns:] = mask_ref[rows].astype(f32)
        start += ref.shape[0]


def pack_kernel(which, obs_ref, mask_ref, *out_refs):
    pack_strip(obs_ref, mask_ref, out_refs)


def split_factor(refs, parts_ref):
    pixels = refs[0].shape[0]
    for part, ref in enumerate(refs):
        parts_ref[part * pixels : (part + 1) * pixels] = left_parts(ref[...], 1)


def chunk_starts(chip, step):
    return [pl.multiple_of((chip ^ (2 * step + b)) * LANES, LANES) for b in range(2)]


def own_kernel(place, obs_ref, mask_ref, v_ref, u_ref, *refs):
    vt_ref, res_ref, weight_ref, sum_ref = refs[-4:]
    pack_strip(obs_ref, mask_ref, refs[:-4])
    u = left_parts(u_ref[...], 1)
    spread = 0.0
    for step, cols in enumerate(tiles(vt_ref)):
        starts = chunk_starts(place[1], step)
        vt = jnp.concatenate([v_ref[pl.ds(start, LANES)].T for start in starts], axis=1)
        vt_ref[:, cols] = vt
        weight = spread_mask(mask_ref[...], place[1], step)
        obs = jnp.concatenate([obs_ref[:, pl.ds(start, LANES)] for start in starts], axis=1)
        res = weight * (obs - product(u, right_parts(vt, 0)))
        weight_ref[:, cols] = weight
        res_ref[:, cols] = res
        spread = spread + rows_folded(res * res)
    sum_ref[...] = spread


def residual_of_pieces(pieces, chip, step, low_rank):
    half = pieces[0].shape[1] // (BANDS + 1) * BANDS
    start = 0
    for piece in pieces:
        rows = slice(start, start + piece.shape[0])
        weight = spread_mask(piece[:, half:], chip, step)
        obs = jnp.concatenate([piece[:, pl.ds(first, LANES)] for first in chunk_starts(chip, step)], axis=1)
        yield rows, weight * (obs - low_rank[rows]), weight
        start += piece.shape[0]


def other_kernel(place, *refs):
    pieces = refs[:-8]
    u_ref, vt_ref, own_res, own_weight, own_sum, res_ref, weight_ref, sums_ref = refs[-8:]
    pixels = own_res.shape[0]
    res_ref[:pixels] = own_res[...]
    weight_ref[:pixels] = own_weight[...]
    u = left_parts(u_ref[...], 1)
    spread = own_sum[...]
    for step, cols in enumerate(tiles(vt_ref)):
        low_rank = product(u, right_parts(vt_ref[:, cols], 0))
        for rows, res, weight in residual_of_pieces(pieces, place[1], step, low_rank):
            below = slice(pixels + rows.start, pixels + rows.stop)
            weight_ref[below, cols] = weight
            res_ref[below, cols] = res
            spread = spread + rows_folded(res * res)
    sums_ref[...] = packed_sums(sums_ref.shape, [whole_sum(spread)])


def level_from(spread, total):
    return threshold_scale * jnp.sqrt(jnp.maximum(spread, 0.0) / total + 1e-06)


def store_parts(grad, own_ref, other_ref):
    pixels = own_ref.shape[0]
    own_ref[...] = grad[:pixels]
    other_ref[...] = grad[pixels:]


def first_grad_kernel(total, sums_ref, res_ref, vt_ref, own_ref, other_ref):
    (spread,) = read_sums(sums_ref, 1)
    level = level_from(spread, total)
    grad = None
    for cols in tiles(res_ref):
        misfit = -jnp.clip(res_ref[:, cols], -level, level)
        part = product(left_parts(misfit, 1), right_parts(vt_ref[:, cols], 1), 1)
        grad = part if grad is None else grad + part
    store_parts(grad, own_ref, other_ref)


def column_sums(sums):
    top, curve, cross, before = sums
    step = top / curve
    return step, before + 2.0 * step * cross + step * step * curve


def next_grad_kernel(total, sums_ref, res_ref, shift_ref, vt_ref, step_ref,
                     res_out, vt_out, own_ref, other_ref):
    size, spread = column_sums(read_sums(sums_ref, 4))
    level = level_from(spread, total)
    grad = None
    for cols in tiles(res_ref):
        vt = vt_ref[:, cols] - size * step_ref[:, cols]
        vt_out[:, cols] = vt
        res = res_ref[:, cols] + size * shift_ref[:, cols]
        res_out[:, cols] = res
        misfit = -jnp.clip(res, -level, level)
        part = product(left_parts(misfit, 1), right_parts(vt, 1), 1)
        grad = part if grad is None else grad + part
    store_parts(grad, own_ref, other_ref)


def change_kernel(col_count, own_grad, other_grad, vt_ref, weight_ref, change_ref, sums_ref, g_parts):
    split_factor((own_grad, other_grad), g_parts)
    curve = 0.0
    for cols in tiles(vt_ref):
        change = weight_ref[:, cols] * product(g_parts[...], right_parts(vt_ref[:, cols], 0))
        change_ref[:, cols] = change
        curve = curve + rows_folded(change * change)
    top = whole_sum(own_grad[...] * own_grad[...]) / col_count
    sums_ref[...] = packed_sums(sums_ref.shape, [top, whole_sum(curve)])


def pix_step_kernel(total, first, level_sums, sums_ref, own_u, other_u, own_grad, other_grad, res_ref,
                    change_ref, own_out, other_out, res_out, copy_ref, even_ref, odd_ref, ut_parts):
    pixels = own_grad.shape[0]
    top, curve = read_sums(sums_ref, 2)
    size = top / curve
    if first:
        (spread,) = read_sums(level_sums, 1)
    else:
        _, spread = column_sums(read_sums(level_sums, 4))
    level = level_from(spread, total)
    strips = ((own_u, own_grad, own_out), (other_u, other_grad, other_out))
    for part, (old, grad, out) in enumerate(strips):
        u = old[...] - size * grad[...]
        out[...] = u
        if part == 0:
            copy_ref[...] = u
        high, low = halves(u.T)
        for k, value in enumerate((high, high, low)):
            first_col = (2 * k + part) * pixels
            ut_parts[:, first_col : first_col + pixels] = value
    for k, cols in enumerate(tiles(res_ref)):
        res = res_ref[:, cols]
        moved = size * change_ref[:, cols]
        res_out[:, cols] = res + moved
        misfit = -(jnp.clip(res, -level, level) + moved)
        grad = product(ut_parts[...], right_parts(misfit, 0))
        even_ref[k] = grad[:, :LANES]
        odd_ref[k] = grad[:, LANES:]


def shift_kernel(chips, own_u, other_u, weight_ref, res_ref, *refs):
    chunk_refs = refs[:GROUP]
    shift_ref, grad_ref, sums_ref, u_parts = refs[GROUP:]
    split_factor((own_u, other_u), u_parts)
    top = curve = cross = spread = 0.0
    for k, cols in enumerate(tiles(res_ref)):
        grad = jnp.concatenate([chunk_refs[2 * k][...], chunk_refs[2 * k + 1][...]], axis=1)
        grad_ref[:, cols] = grad
        top = top + rows_folded(grad * grad)
        shift = weight_ref[:, cols] * product(u_parts[...], right_parts(grad, 0))
        shift_ref[:, cols] = shift
        res = res_ref[:, cols]
        curve = curve + rows_folded(shift * shift)
        cross = cross + rows_folded(shift * res)
        spread = spread + rows_folded(res * res)
    sums = [whole_sum(top) / chips, whole_sum(curve), whole_sum(cross), whole_sum(spread)]
    sums_ref[...] = packed_sums(sums_ref.shape, sums)


def rim_kernel(place, *refs):
    packs = [refs[3 * k : 3 * k + 3] for k in range(4)]
    factors = refs[12:16]
    vt_ref, res_ref, weight_ref, u_parts = refs[16:]
    pixels = factors[0].shape[0]
    split_factor(factors, u_parts)
    for step, cols in enumerate(tiles(vt_ref)):
        low_rank = product(u_parts[...], right_parts(vt_ref[:, cols], 0))
        for part, pieces in enumerate(packs):
            strip = low_rank[part * pixels : (part + 1) * pixels]
            for rows, res, weight in residual_of_pieces(pieces, place[1], step, strip):
                weight_ref[part, rows, cols] = weight
                res_ref[part, rows, cols] = res


def add_kernel(kept_ref, from_ref, *out_refs):
    for k, ref in enumerate(out_refs):
        ref[...] = kept_ref[k] + from_ref[k]


def flux_of(diff):
    below = 1.0 + diff * diff
    return diff * pl.reciprocal(below, approx=True)


PAD = 8
SPAN = 64


def smooth_rows(source, target, keep_north, keep_south, north_edge, south_edge):
    count = source.shape[0]
    for start in range(0, WIDTH, SPAN):
        row = lax.broadcasted_iota(jnp.int32, (SPAN + 2 * PAD, LANES), 0) + (start - PAD)
        edge = start == 0 or start + SPAN == WIDTH
        around = slice(start, start + SPAN + 2 * PAD)
        middle = slice(PAD, PAD + SPAN)
        before = None
        here = source[0, around]
        for k in range(count - 1):
            after = source[k + 1, around]
            cross = flux_of(after[middle] - here[middle])
            if k == north_edge:
                cross = cross * keep_north
            if k == south_edge:
                cross = cross * keep_south
            if k > 0:
                east = flux_of(pltpu.roll(here, SPAN + 2 * PAD - 1, 0) - here)
                if edge:
                    east = jnp.where((row >= 0) & (row < WIDTH - 1), east, 0.0)
                west = pltpu.roll(east, 1, 0)
                along = east[middle] - west[middle]
                target(k - 1, start, here[middle] + diffusion * ((cross - before) + along))
            before = cross
            here = after


def smooth_kernel(total, chips, place, sums_ref, res_ref, shift_ref, rim_ref, rim_weight, *refs):
    factors = refs[:4]
    own_vt, other_vt, own_grad, other_grad = refs[4:8]
    own_ref, other_ref, v_ref, u_parts, rim_shift, layer, once = refs[8:]
    step = pl.program_id(0)
    core, chip = place[0], place[2]
    pixels = own_ref.shape[0]

    @pl.when(step == 0)
    def _():
        split_factor(factors, u_parts)

    size, spread = column_sums(read_sums(sums_ref, 4))
    level = level_from(spread, total)
    inverse = 1.0 / level
    both_chunks = pl.ds(pl.multiple_of(step * 2 * LANES, 2 * LANES), 2 * LANES)
    moved = product(u_parts[...], right_parts(own_grad[:, both_chunks], 0))
    rim_shift[...] = moved.reshape(rim_shift.shape)

    def cut(res):
        return (res - jnp.clip(res, -level, level)) * inverse

    south = 2 * (chip % 2)
    beyond_own = jnp.where(core == 0, 2 - south, south)
    beyond_other = 2 - beyond_own
    keep_north = jnp.where(chip > 0, 1.0, 0.0).astype(f32)
    keep_south = jnp.where(chip < chips - 1, 1.0, 0.0).astype(f32)
    keep_own = jnp.where(core == 0, keep_north, keep_south)
    keep_other = jnp.where(core == 0, keep_south, keep_north)
    inner = slice(PAD, PAD + pixels)
    for b in range(2):
        cols = pl.ds(pl.multiple_of((2 * step + b) * LANES, LANES), LANES)
        here = slice(b * LANES, (b + 1) * LANES)
        there = pl.ds(pl.multiple_of((chip % 2 ^ b) * LANES, LANES), LANES)
        v_ref[core, there] = (own_vt[:, cols] - size * own_grad[:, cols]).T
        v_ref[1 - core, there] = (other_vt[:, cols] - size * other_grad[:, cols]).T
        for k in range(2):
            layer[2 + k, inner] = cut(res_ref[k, :, cols] + size * shift_ref[k, :, cols])
            for first, base in ((0, beyond_own), (4, beyond_other)):
                rim = base + k
                moved = size * (rim_weight[rim, :, cols] * rim_shift[rim, :, here])
                layer[first + k, inner] = cut(rim_ref[rim, :, cols] + moved)

        def to_once(strip, start, value):
            once[strip, PAD + start : PAD + start + SPAN] = value

        def to_cloud(strip, start, value):
            ref = other_ref if strip else own_ref
            ref[start : start + SPAN, there] = level * value

        smooth_rows(layer, to_once, keep_own, keep_other, 1, 3)
        smooth_rows(once, to_cloud, keep_own, keep_other, 0, 2)


def summed_over_chips(even, odd, meanwhile):
    chips = lax.axis_size("pix") // 2
    count, rank, lanes = even.shape
    from_odd = along_pix(odd, 2)
    kept = call(add_kernel, [VMEM] * 2, [VMEM] * count, [shaped(rank, lanes)] * count, [], even, from_odd)
    before_sum, before_end = meanwhile(from_odd)
    mine = plus(kept[0], *[along_pix(kept[k], 4 * k) for k in (1, 2, 3)], after=before_sum)
    distance = GROUP
    while distance < chips:
        mine = plus(mine, along_pix(mine, 2 * distance))
        distance *= 2
    parts = [mine] + [along_pix(mine, 4 * k) for k in (1, 2, 3)]
    parts[3] = held_until(parts[3], *before_end)
    summed = []
    for part in parts:
        summed += [part, along_pix(part, 2)]
    return summed


def per_device(observed, valid_mask, pix_factor, col_factor):
    pix_count = lax.axis_size("pix")
    col_count = lax.axis_size("col")
    chips = pix_count // 2
    pixels, columns = observed.shape
    rank = pix_factor.shape[1]
    half = columns // 2
    dates = valid_mask.shape[1] // 2
    total = float(pixels * columns * pix_count * col_count)
    assert pixels == WIDTH and half == GROUP * LANES and chips % GROUP == 0 and PASSES == 2
    index = lax.axis_index("pix")
    core = index % 2
    chip = index // 2
    place = jnp.stack([core, chip % GROUP, chip]).astype(jnp.int32)

    both = 2 * pixels
    wide = 2 * LANES
    steps = half // wide
    sums_shape = shaped(8, LANES)
    pix_shape = shaped(pixels, rank)
    half_shape = shaped(steps, rank, LANES)
    vt_shape = pltpu.VMEM((rank, half), f32)
    local = pltpu.VMEM((both, half), f32)
    strip = pltpu.VMEM((pixels, half), f32)
    factor_scratch = [pltpu.VMEM((both, 3 * rank), bf16)]

    unit = pixels // 32
    own_rows, other_rows = [13 * unit, 13 * unit, 6 * unit], [7 * unit, 12 * unit, 13 * unit]

    def pieces(rows):
        return [pltpu.VMEM((n, half + dates), f32) for n in rows]

    half_in = [pl.BlockSpec((pixels, half), lambda t, s: (0, s[0])), pl.BlockSpec((pixels, dates), lambda t, s: (0, s[0]))]
    other_pieces = call(
        pack_kernel, half_in, [VMEM] * 3, pieces(other_rows), [], in_hbm(observed), in_hbm(valid_mask),
        grid=(1,), place=jnp.reshape(1 - core, (1,)).astype(jnp.int32),
    )
    received = [along_pix(piece, 1) for piece in other_pieces]
    own_u, other_u = pix_factor, along_pix(pix_factor, 1)
    *own_pieces, vt, own_res, own_weight, own_sum = call(
        own_kernel, half_in + [pl.BlockSpec((half, rank), lambda t, s: (s[0], 0)), VMEM], [VMEM] * 7,
        pieces(own_rows) + [vt_shape, strip, strip, shaped(8, wide)], [],
        in_hbm(observed), in_hbm(valid_mask), in_hbm(col_factor), own_u, grid=(1,), place=place, after=[other_u],
    )
    near_own, near_other, far_own, far_other = [None] * 3, [None] * 3, [None] * 3, [None] * 3
    near_own[0] = to_near(held_until(own_pieces[0], *received), 0)
    residual, weight, sums = call(
        other_kernel, [SMEM] + [VMEM] * 8, [VMEM] * 3, [local, local, sums_shape], [],
        place, *received, other_u, in_vmem(vt), in_vmem(own_res), in_vmem(own_weight), own_sum,
    )
    level_sums = everywhere(sums, late=True)

    for iteration in range(ITERS):
        first = iteration == 0
        if first:
            near_own[1] = to_near(held_until(own_pieces[1], level_sums), 0)
            near_own[0] = held_until(near_own[0], level_sums)
            far_own[0] = to_far(near_own[0])
            passed = [near_own[1], far_own[0]]
            own_part, other_part = call(
                functools.partial(first_grad_kernel, total), [VMEM] * 3, [VMEM] * 2, [pix_shape] * 2, [],
                level_sums, in_vmem(residual), in_vmem(vt), after=near_own[:1],
            )
        else:
            near_other[2] = to_near(held_until(other_pieces[2], level_sums), 1)
            near_other[1] = held_until(near_other[1], level_sums)
            far_other[1] = to_far(near_other[1])
            passed = [near_other[2], far_other[1]]
            residual, vt, own_part, other_part = call(
                functools.partial(next_grad_kernel, total), [VMEM] * 5, [VMEM] * 4,
                [local, vt_shape, pix_shape, pix_shape], [],
                level_sums, in_vmem(residual), in_vmem(shift), in_vmem(vt), in_vmem(grad), after=[far_own[2], far_other[0]],
            )
        own_grad = summed_over_col(plus(own_part, along_pix(other_part, 1)))
        other_grad = along_pix(own_grad, 1)
        change, sums = call(
            functools.partial(change_kernel, col_count), [VMEM] * 4, [VMEM] * 2,
            [local, sums_shape], factor_scratch, own_grad, other_grad, in_vmem(vt), in_vmem(weight),
            beside=[residual],
        )
        pix_sums = everywhere(sums, late=True)
        u_next, other_u, residual, own_u, even, odd = call(
            functools.partial(pix_step_kernel, total, first), [VMEM] * 8, [VMEM] * 6,
            [pix_shape, pix_shape, local, pix_shape, half_shape, half_shape], [pltpu.VMEM((rank, 3 * both), bf16)],
            level_sums, pix_sums, own_u, other_u, own_grad, other_grad, in_vmem(residual),
            in_vmem(change), after=passed, beside=[vt, weight],
        )
        if first:
            near_own[1] = held_until(near_own[1], odd)
            far_own[1] = to_far(near_own[1])

            def meanwhile(moved):
                near_own[2] = to_near(held_until(own_pieces[2], moved), 0)
                near_other[0] = to_near(held_until(other_pieces[0], moved), 1)
                near_other[1] = to_near(held_until(other_pieces[1], moved), 1)
                return [], [far_own[1], near_own[2], near_other[0]]

        else:
            near_other[2] = held_until(near_other[2], odd)
            far_other[2] = to_far(near_other[2])
            sent = []

            def meanwhile(moved):
                sent.append(held_until(own_u, moved))
                sent.append(to_near(sent[0], 0))
                return [], [far_other[2], sent[1]]

            other_vt = along_pix(vt, 1)
        summed = summed_over_chips(even, odd, meanwhile)
        if first:
            near_own[2] = held_until(near_own[2], summed[6])
            near_other[0] = held_until(near_other[0], summed[6])
            far_own[2] = to_far(near_own[2])
            far_other[0] = to_far(near_other[0])
            passed = near_other[1:2]
        else:
            own_u = sent[0]
            near_u = held_until(sent[1], summed[6])
            far_u = to_far(near_u)
            passed = [far_u]
        shift, grad, sums = call(
            functools.partial(shift_kernel, chips), [VMEM] * (4 + GROUP), [VMEM] * 3,
            [local, vt_shape, sums_shape], factor_scratch, own_u, other_u, in_vmem(weight), in_vmem(residual),
            *summed, after=passed, beside=[vt],
        )
        if first:
            level_sums = everywhere(sums)

    near_other_u = along_pix(near_u, 1)
    rim_scratch = [pltpu.VMEM((2 * both, 3 * rank), bf16)]
    rim_shape = pltpu.VMEM((4, pixels, half), f32)

    def rim(group_sums):
        far = held_until(far_u, group_sums)
        factors = [near_u, near_other_u, far, along_pix(far, 1)]
        other_grad = along_pix(held_until(grad, group_sums), 1)
        return factors, other_grad, *call(
            rim_kernel, [SMEM] + [VMEM] * 17, [VMEM] * 2, [rim_shape] * 2, rim_scratch,
            place, *near_own, *near_other, *far_own, *far_other, *factors, in_vmem(vt), after=[group_sums],
        )

    level_sums, (factors, other_grad, rim_res, rim_weight) = everywhere(sums, beside=rim)
    pair = lambda s, t: s[1] // 2 ^ t
    own_cloud, other_cloud, v = call(
        functools.partial(smooth_kernel, total, chips), [VMEM] * 13,
        [
            pl.BlockSpec((pixels, wide), lambda t, s: (0, s[0] * steps + pair(s, t))),
            pl.BlockSpec((pixels, wide), lambda t, s: (0, pair(s, t))),
            pl.BlockSpec((2, wide, rank), lambda t, s: (0, pair(s, t), 0)),
        ],
        [shaped(pixels, columns), shaped(pixels, half), shaped(2, half, rank)],
        rim_scratch + [
            pltpu.VMEM((4, pixels, wide), f32),
            pltpu.VMEM((6, pixels + 2 * PAD, LANES), f32),
            pltpu.VMEM((4, pixels + 2 * PAD, LANES), f32),
        ],
        level_sums, in_vmem(residual.reshape(2, pixels, half)), in_vmem(shift.reshape(2, pixels, half)),
        in_vmem(rim_res), in_vmem(rim_weight), *factors, in_vmem(vt), other_vt, in_vmem(grad),
        other_grad, grid=(steps,), place=place,
    )
    from_other = along_pix(other_cloud, 1)
    cloud = lax.dynamic_update_slice(own_cloud, from_other, (0, (1 - core) * half))
    return u_next, v.reshape(columns, rank), cloud


def solution(mesh):
    in_specs = (P("pix", "col"), P("pix", "col"), P("pix", None), P("col", None))
    out_specs = (P("pix", None), P("col", None), P("pix", "col"))
    return jax.shard_map(
        per_device, mesh=mesh, in_specs=in_specs, out_specs=out_specs, check_vma=False
    )
```

```python
import functools

import jax
import jax.numpy as jnp
from jax import lax
from jax.experimental import pallas as pl
from jax.experimental.pallas import tpu as pltpu
from jax.sharding import PartitionSpec as P

BANDS = 8
WIDTH = 256
ITERS = 2
PASSES = 2
LANES = 128
GROUP = 8

threshold_scale = 1.0
diffusion = 0.2
f32 = jnp.float32
bf16 = jnp.bfloat16


def along_pix(block, distance):
    count = lax.axis_size("pix")
    return lax.ppermute(block, "pix", [(i, i ^ distance) for i in range(count)])


def to_near(block, crossed):
    count = lax.axis_size("pix")
    return lax.ppermute(block, "pix", [(i, i ^ 2 ^ crossed) for i in range(count)])


def to_far(block):
    count = lax.axis_size("pix")
    route = [(i, i + (4 if i // 2 % 2 == 0 else -4)) for i in range(count)]
    return lax.ppermute(block, "pix", [(a, b) for a, b in route if 0 <= b < count])


def summed_over_col(block):
    count = lax.axis_size("col")
    step = 1
    while step < count:
        block = plus(block, lax.ppermute(block, "col", [(i, i ^ step) for i in range(count)]))
        step *= 2
    return block


def everywhere(sums, late=False, beside=None):
    count = lax.axis_size("col")
    devices = lax.axis_size("pix") * count
    bits = [count << k for k in range(1, (devices // count).bit_length() - 1)]
    bits = [bits[0]] + [1 << k for k in range(count.bit_length() - 1)] + bits[1:]
    stages = [[count]] + [bits[k : k + 2] for k in range(0, len(bits), 2)]
    if late:
        stages = stages[:1] + stages[:0:-1]
    for stage in stages:
        moves = [0]
        for bit in stage:
            moves += [move ^ bit for move in moves]
        parts = [
            lax.ppermute(sums, ("pix", "col"), [(i, i ^ move) for i in range(devices)]) for move in moves[1:]
        ]
        sums = plus(sums, *parts, after=extra[-1:] if beside and stage is stages[2] else ())
        if beside and stage is stages[1]:
            extra = beside(sums)
    return (sums, extra) if beside else sums


def halves(x):
    high = x.astype(bf16)
    return high, (x - high.astype(f32)).astype(bf16)


def left_parts(x, axis):
    high, low = halves(x)
    return jnp.concatenate([high, high, low], axis=axis)


def right_parts(x, axis):
    high, low = halves(x)
    return jnp.concatenate([high, low, high], axis=axis)


def product(a, b, summed=0):
    return lax.dot_general(a, b, (((1,), (summed,)), ((), ())), preferred_element_type=f32)


def rows_folded(x):
    return jnp.sum(x.reshape(x.shape[0] // 8, 8, x.shape[1]), axis=0)


def whole_sum(x):
    return jnp.sum(jnp.sum(x, axis=0, keepdims=True), axis=1, keepdims=True)


def packed_sums(shape, sums):
    lane = lax.broadcasted_iota(jnp.int32, shape, 1)
    row = lax.broadcasted_iota(jnp.int32, shape, 0)
    packed = jnp.zeros(shape, f32)
    for place, value in enumerate(sums):
        packed = packed + jnp.where((lane == place) & (row == 0), value, 0.0)
    return packed


def read_sums(ref, count):
    total = jnp.sum(ref[...], axis=0, keepdims=True)
    return [total[:, k : k + 1] for k in range(count)]


def spread_mask(mask, chip, step):
    dates = mask.shape[1]
    date = lax.broadcasted_iota(jnp.int32, (dates, 2 * LANES), 0)
    lane = lax.broadcasted_iota(jnp.int32, (dates, 2 * LANES), 1)
    chunk = chip ^ (2 * step + lane // LANES)
    pick = (date == chunk * (LANES // BANDS) + lane % LANES // BANDS).astype(bf16)
    return jnp.dot(mask.astype(f32).astype(bf16), pick, preferred_element_type=f32)


SMEM = pl.BlockSpec(memory_space=pltpu.SMEM)
VMEM = pl.BlockSpec(memory_space=pltpu.VMEM)
ANY = pl.BlockSpec(memory_space=pl.ANY)


def call(kernel, in_specs, out_specs, out_shape, scratch, *args, grid=(), place=None, after=(), beside=()):
    inputs = len(in_specs)
    lead = 0 if place is None else 1

    def body(*refs):
        used = lead + inputs
        kernel(*refs[:used], *refs[used + len(after) + len(beside) :])

    results = pl.pallas_call(
        body,
        grid_spec=pltpu.PrefetchScalarGridSpec(
            num_scalar_prefetch=lead,
            grid=grid,
            in_specs=list(in_specs) + [ANY] * len(after) + [VMEM] * len(beside),
            out_specs=list(out_specs),
            scratch_shapes=scratch,
        ),
        out_shape=list(out_shape),
        compiler_params=pltpu.CompilerParams(vmem_limit_bytes=16 * 2**20),
    )(*([place] if lead else []), *args, *after, *[in_vmem(x) for x in beside])
    return list(results)


def plus_kernel(*refs):
    total = refs[0][...]
    for ref in refs[1:-1]:
        total = total + ref[...]
    refs[-1][...] = total


def plus(*arrays, after=()):
    (total,) = call(plus_kernel, [VMEM] * len(arrays), [VMEM], [shaped(*arrays[0].shape)], [], *arrays, after=after)
    return total


def in_vmem(array):
    return pltpu.with_memory_space_constraint(array, pltpu.VMEM)


def in_hbm(array):
    return pltpu.with_memory_space_constraint(array, pltpu.HBM)


def held_until(array, *after):
    def body(*refs):
        pass

    return pl.pallas_call(
        body,
        in_specs=[ANY] * (1 + len(after)),
        out_specs=ANY,
        out_shape=jax.ShapeDtypeStruct(array.shape, array.dtype),
        input_output_aliases={0: 0},
        compiler_params=pltpu.CompilerParams(vmem_limit_bytes=2**20),
    )(array, *after)


def shaped(*shape):
    return jax.ShapeDtypeStruct(shape, f32)


def tiles(ref):
    return [slice(start, start + 2 * LANES) for start in range(0, ref.shape[-1], 2 * LANES)]


def pack_strip(obs_ref, mask_ref, out_refs):
    columns = obs_ref.shape[1]
    start = 0
    for ref in out_refs:
        rows = slice(start, start + ref.shape[0])
        ref[:, :columns] = obs_ref[rows]
        ref[:, columns:] = mask_ref[rows].astype(f32)
        start += ref.shape[0]


def pack_kernel(which, obs_ref, mask_ref, *out_refs):
    pack_strip(obs_ref, mask_ref, out_refs)


def split_factor(refs, parts_ref):
    pixels = refs[0].shape[0]
    for part, ref in enumerate(refs):
        parts_ref[part * pixels : (part + 1) * pixels] = left_parts(ref[...], 1)


def chunk_starts(chip, step):
    return [pl.multiple_of((chip ^ (2 * step + b)) * LANES, LANES) for b in range(2)]


def own_kernel(place, obs_ref, mask_ref, v_ref, u_ref, *refs):
    vt_ref, res_ref, weight_ref, sum_ref = refs[-4:]
    pack_strip(obs_ref, mask_ref, refs[:-4])
    u = left_parts(u_ref[...], 1)
    spread = 0.0
    for step, cols in enumerate(tiles(vt_ref)):
        starts = chunk_starts(place[1], step)
        vt = jnp.concatenate([v_ref[pl.ds(start, LANES)].T for start in starts], axis=1)
        vt_ref[:, cols] = vt
        weight = spread_mask(mask_ref[...], place[1], step)
        obs = jnp.concatenate([obs_ref[:, pl.ds(start, LANES)] for start in starts], axis=1)
        res = weight * (obs - product(u, right_parts(vt, 0)))
        weight_ref[:, cols] = weight
        res_ref[:, cols] = res
        spread = spread + rows_folded(res * res)
    sum_ref[...] = spread


def residual_of_pieces(pieces, chip, step, low_rank):
    half = pieces[0].shape[1] // (BANDS + 1) * BANDS
    start = 0
    for piece in pieces:
        rows = slice(start, start + piece.shape[0])
        weight = spread_mask(piece[:, half:], chip, step)
        obs = jnp.concatenate([piece[:, pl.ds(first, LANES)] for first in chunk_starts(chip, step)], axis=1)
        yield rows, weight * (obs - low_rank[rows]), weight
        start += piece.shape[0]


def other_kernel(place, *refs):
    pieces = refs[:-8]
    u_ref, vt_ref, own_res, own_weight, own_sum, res_ref, weight_ref, sums_ref = refs[-8:]
    pixels = own_res.shape[0]
    res_ref[:pixels] = own_res[...]
    weight_ref[:pixels] = own_weight[...]
    u = left_parts(u_ref[...], 1)
    spread = own_sum[...]
    for step, cols in enumerate(tiles(vt_ref)):
        low_rank = product(u, right_parts(vt_ref[:, cols], 0))
        for rows, res, weight in residual_of_pieces(pieces, place[1], step, low_rank):
            below = slice(pixels + rows.start, pixels + rows.stop)
            weight_ref[below, cols] = weight
            res_ref[below, cols] = res
            spread = spread + rows_folded(res * res)
    sums_ref[...] = packed_sums(sums_ref.shape, [whole_sum(spread)])


def level_from(spread, total):
    return threshold_scale * jnp.sqrt(jnp.maximum(spread, 0.0) / total + 1e-06)


def store_parts(grad, own_ref, other_ref):
    pixels = own_ref.shape[0]
    own_ref[...] = grad[:pixels]
    other_ref[...] = grad[pixels:]


def first_grad_kernel(total, sums_ref, res_ref, vt_ref, own_ref, other_ref):
    (spread,) = read_sums(sums_ref, 1)
    level = level_from(spread, total)
    grad = None
    for cols in tiles(res_ref):
        misfit = -jnp.clip(res_ref[:, cols], -level, level)
        part = product(left_parts(misfit, 1), right_parts(vt_ref[:, cols], 1), 1)
        grad = part if grad is None else grad + part
    store_parts(grad, own_ref, other_ref)


def column_sums(sums):
    top, curve, cross, before = sums
    step = top / curve
    return step, before + 2.0 * step * cross + step * step * curve


def next_grad_kernel(total, sums_ref, res_ref, shift_ref, vt_ref, step_ref,
                     res_out, vt_out, own_ref, other_ref):
    size, spread = column_sums(read_sums(sums_ref, 4))
    level = level_from(spread, total)
    grad = None
    for cols in tiles(res_ref):
        vt = vt_ref[:, cols] - size * step_ref[:, cols]
        vt_out[:, cols] = vt
        res = res_ref[:, cols] + size * shift_ref[:, cols]
        res_out[:, cols] = res
        misfit = -jnp.clip(res, -level, level)
        part = product(left_parts(misfit, 1), right_parts(vt, 1), 1)
        grad = part if grad is None else grad + part
    store_parts(grad, own_ref, other_ref)


def change_kernel(col_count, own_grad, other_grad, vt_ref, weight_ref, change_ref, sums_ref, g_parts):
    split_factor((own_grad, other_grad), g_parts)
    curve = 0.0
    for cols in tiles(vt_ref):
        change = weight_ref[:, cols] * product(g_parts[...], right_parts(vt_ref[:, cols], 0))
        change_ref[:, cols] = change
        curve = curve + rows_folded(change * change)
    top = whole_sum(own_grad[...] * own_grad[...]) / col_count
    sums_ref[...] = packed_sums(sums_ref.shape, [top, whole_sum(curve)])


def pix_step_kernel(total, first, level_sums, sums_ref, own_u, other_u, own_grad, other_grad, res_ref,
                    change_ref, own_out, other_out, res_out, copy_ref, even_ref, odd_ref, ut_parts):
    pixels = own_grad.shape[0]
    top, curve = read_sums(sums_ref, 2)
    size = top / curve
    if first:
        (spread,) = read_sums(level_sums, 1)
    else:
        _, spread = column_sums(read_sums(level_sums, 4))
    level = level_from(spread, total)
    strips = ((own_u, own_grad, own_out), (other_u, other_grad, other_out))
    for part, (old, grad, out) in enumerate(strips):
        u = old[...] - size * grad[...]
        out[...] = u
        if part == 0:
            copy_ref[...] = u
        high, low = halves(u.T)
        for k, value in enumerate((high, high, low)):
            first_col = (2 * k + part) * pixels
            ut_parts[:, first_col : first_col + pixels] = value
    for k, cols in enumerate(tiles(res_ref)):
        res = res_ref[:, cols]
        moved = size * change_ref[:, cols]
        res_out[:, cols] = res + moved
        misfit = -(jnp.clip(res, -level, level) + moved)
        grad = product(ut_parts[...], right_parts(misfit, 0))
        even_ref[k] = grad[:, :LANES]
        odd_ref[k] = grad[:, LANES:]


def shift_kernel(chips, own_u, other_u, weight_ref, res_ref, *refs):
    chunk_refs = refs[:GROUP]
    shift_ref, grad_ref, sums_ref, u_parts = refs[GROUP:]
    split_factor((own_u, other_u), u_parts)
    top = curve = cross = spread = 0.0
    for k, cols in enumerate(tiles(res_ref)):
        grad = jnp.concatenate([chunk_refs[2 * k][...], chunk_refs[2 * k + 1][...]], axis=1)
        grad_ref[:, cols] = grad
        top = top + rows_folded(grad * grad)
        shift = weight_ref[:, cols] * product(u_parts[...], right_parts(grad, 0))
        shift_ref[:, cols] = shift
        res = res_ref[:, cols]
        curve = curve + rows_folded(shift * shift)
        cross = cross + rows_folded(shift * res)
        spread = spread + rows_folded(res * res)
    sums = [whole_sum(top) / chips, whole_sum(curve), whole_sum(cross), whole_sum(spread)]
    sums_ref[...] = packed_sums(sums_ref.shape, sums)


def rim_kernel(place, *refs):
    packs = [refs[3 * k : 3 * k + 3] for k in range(4)]
    factors = refs[12:16]
    vt_ref, res_ref, weight_ref, u_parts = refs[16:]
    pixels = factors[0].shape[0]
    split_factor(factors, u_parts)
    for step, cols in enumerate(tiles(vt_ref)):
        low_rank = product(u_parts[...], right_parts(vt_ref[:, cols], 0))
        for part, pieces in enumerate(packs):
            strip = low_rank[part * pixels : (part + 1) * pixels]
            for rows, res, weight in residual_of_pieces(pieces, place[1], step, strip):
                weight_ref[part, rows, cols] = weight
                res_ref[part, rows, cols] = res


def add_kernel(kept_ref, from_ref, *out_refs):
    for k, ref in enumerate(out_refs):
        ref[...] = kept_ref[k] + from_ref[k]


def flux_of(diff):
    below = 1.0 + diff * diff
    return diff * pl.reciprocal(below, approx=True)


PAD = 8
SPAN = 64


def smooth_rows(source, target, keep_north, keep_south, north_edge, south_edge):
    count = source.shape[0]
    for start in range(0, WIDTH, SPAN):
        row = lax.broadcasted_iota(jnp.int32, (SPAN + 2 * PAD, LANES), 0) + (start - PAD)
        edge = start == 0 or start + SPAN == WIDTH
        around = slice(start, start + SPAN + 2 * PAD)
        middle = slice(PAD, PAD + SPAN)
        before = None
        here = source[0, around]
        for k in range(count - 1):
            after = source[k + 1, around]
            cross = flux_of(after[middle] - here[middle])
            if k == north_edge:
                cross = cross * keep_north
            if k == south_edge:
                cross = cross * keep_south
            if k > 0:
                east = flux_of(pltpu.roll(here, SPAN + 2 * PAD - 1, 0) - here)
                if edge:
                    east = jnp.where((row >= 0) & (row < WIDTH - 1), east, 0.0)
                west = pltpu.roll(east, 1, 0)
                along = east[middle] - west[middle]
                target(k - 1, start, here[middle] + diffusion * ((cross - before) + along))
            before = cross
            here = after


def smooth_kernel(total, chips, place, sums_ref, res_ref, shift_ref, rim_ref, rim_weight, *refs):
    factors = refs[:4]
    own_vt, other_vt, own_grad, other_grad = refs[4:8]
    own_ref, other_ref, v_ref, u_parts, rim_shift, layer, once = refs[8:]
    step = pl.program_id(0)
    core, chip = place[0], place[2]
    pixels = own_ref.shape[0]

    @pl.when(step == 0)
    def _():
        split_factor(factors, u_parts)

    size, spread = column_sums(read_sums(sums_ref, 4))
    level = level_from(spread, total)
    inverse = 1.0 / level
    both_chunks = pl.ds(pl.multiple_of(step * 2 * LANES, 2 * LANES), 2 * LANES)
    moved = product(u_parts[...], right_parts(own_grad[:, both_chunks], 0))
    rim_shift[...] = moved.reshape(rim_shift.shape)

    def cut(res):
        return (res - jnp.clip(res, -level, level)) * inverse

    south = 2 * (chip % 2)
    beyond_own = jnp.where(core == 0, 2 - south, south)
    beyond_other = 2 - beyond_own
    keep_north = jnp.where(chip > 0, 1.0, 0.0).astype(f32)
    keep_south = jnp.where(chip < chips - 1, 1.0, 0.0).astype(f32)
    keep_own = jnp.where(core == 0, keep_north, keep_south)
    keep_other = jnp.where(core == 0, keep_south, keep_north)
    inner = slice(PAD, PAD + pixels)
    for b in range(2):
        cols = pl.ds(pl.multiple_of((2 * step + b) * LANES, LANES), LANES)
        here = slice(b * LANES, (b + 1) * LANES)
        there = pl.ds(pl.multiple_of((chip % 2 ^ b) * LANES, LANES), LANES)
        v_ref[core, there] = (own_vt[:, cols] - size * own_grad[:, cols]).T
        v_ref[1 - core, there] = (other_vt[:, cols] - size * other_grad[:, cols]).T
        for k in range(2):
            layer[2 + k, inner] = cut(res_ref[k, :, cols] + size * shift_ref[k, :, cols])
            for first, base in ((0, beyond_own), (4, beyond_other)):
                rim = base + k
                moved = size * (rim_weight[rim, :, cols] * rim_shift[rim, :, here])
                layer[first + k, inner] = cut(rim_ref[rim, :, cols] + moved)

        def to_once(strip, start, value):
            once[strip, PAD + start : PAD + start + SPAN] = value

        def to_cloud(strip, start, value):
            ref = other_ref if strip else own_ref
            ref[start : start + SPAN, there] = level * value

        smooth_rows(layer, to_once, keep_own, keep_other, 1, 3)
        smooth_rows(once, to_cloud, keep_own, keep_other, 0, 2)


def summed_over_chips(even, odd, meanwhile):
    chips = lax.axis_size("pix") // 2
    count, rank, lanes = even.shape
    from_odd = along_pix(odd, 2)
    kept = call(add_kernel, [VMEM] * 2, [VMEM] * count, [shaped(rank, lanes)] * count, [], even, from_odd)
    before_sum, before_end = meanwhile(from_odd)
    mine = plus(kept[0], *[along_pix(kept[k], 4 * k) for k in (1, 2, 3)], after=before_sum)
    distance = GROUP
    while distance < chips:
        mine = plus(mine, along_pix(mine, 2 * distance))
        distance *= 2
    parts = [mine] + [along_pix(mine, 4 * k) for k in (1, 2, 3)]
    parts[3] = held_until(parts[3], *before_end)
    summed = []
    for part in parts:
        summed += [part, along_pix(part, 2)]
    return summed


def per_device(observed, valid_mask, pix_factor, col_factor):
    pix_count = lax.axis_size("pix")
    col_count = lax.axis_size("col")
    chips = pix_count // 2
    pixels, columns = observed.shape
    rank = pix_factor.shape[1]
    half = columns // 2
    dates = valid_mask.shape[1] // 2
    total = float(pixels * columns * pix_count * col_count)
    assert pixels == WIDTH and half == GROUP * LANES and chips % GROUP == 0 and PASSES == 2
    index = lax.axis_index("pix")
    core = index % 2
    chip = index // 2
    place = jnp.stack([core, chip % GROUP, chip]).astype(jnp.int32)

    both = 2 * pixels
    wide = 2 * LANES
    steps = half // wide
    sums_shape = shaped(8, LANES)
    pix_shape = shaped(pixels, rank)
    half_shape = shaped(steps, rank, LANES)
    vt_shape = pltpu.VMEM((rank, half), f32)
    local = pltpu.VMEM((both, half), f32)
    strip = pltpu.VMEM((pixels, half), f32)
    factor_scratch = [pltpu.VMEM((both, 3 * rank), bf16)]

    unit = pixels // 32
    own_rows, other_rows = [13 * unit, 13 * unit, 6 * unit], [7 * unit, 12 * unit, 13 * unit]

    def pieces(rows):
        return [pltpu.VMEM((n, half + dates), f32) for n in rows]

    half_in = [pl.BlockSpec((pixels, half), lambda t, s: (0, s[0])), pl.BlockSpec((pixels, dates), lambda t, s: (0, s[0]))]
    other_pieces = call(
        pack_kernel, half_in, [VMEM] * 3, pieces(other_rows), [], in_hbm(observed), in_hbm(valid_mask),
        grid=(1,), place=jnp.reshape(1 - core, (1,)).astype(jnp.int32),
    )
    received = [along_pix(piece, 1) for piece in other_pieces]
    own_u, other_u = pix_factor, along_pix(pix_factor, 1)
    *own_pieces, vt, own_res, own_weight, own_sum = call(
        own_kernel, half_in + [pl.BlockSpec((half, rank), lambda t, s: (s[0], 0)), VMEM], [VMEM] * 7,
        pieces(own_rows) + [vt_shape, strip, strip, shaped(8, wide)], [],
        in_hbm(observed), in_hbm(valid_mask), in_hbm(col_factor), own_u, grid=(1,), place=place, after=[other_u],
    )
    near_own, near_other, far_own, far_other = [None] * 3, [None] * 3, [None] * 3, [None] * 3
    near_own[0] = to_near(held_until(own_pieces[0], *received), 0)
    residual, weight, sums = call(
        other_kernel, [SMEM] + [VMEM] * 8, [VMEM] * 3, [local, local, sums_shape], [],
        place, *received, other_u, in_vmem(vt), in_vmem(own_res), in_vmem(own_weight), own_sum,
    )
    level_sums = everywhere(sums, late=True)

    for iteration in range(ITERS):
        first = iteration == 0
        if first:
            near_own[1] = to_near(held_until(own_pieces[1], level_sums), 0)
            near_own[0] = held_until(near_own[0], level_sums)
            far_own[0] = to_far(near_own[0])
            passed = [near_own[1], far_own[0]]
            own_part, other_part = call(
                functools.partial(first_grad_kernel, total), [VMEM] * 3, [VMEM] * 2, [pix_shape] * 2, [],
                level_sums, in_vmem(residual), in_vmem(vt), after=near_own[:1],
            )
        else:
            near_other[2] = to_near(held_until(other_pieces[2], level_sums), 1)
            near_other[1] = held_until(near_other[1], level_sums)
            far_other[1] = to_far(near_other[1])
            passed = [near_other[2], far_other[1]]
            residual, vt, own_part, other_part = call(
                functools.partial(next_grad_kernel, total), [VMEM] * 5, [VMEM] * 4,
                [local, vt_shape, pix_shape, pix_shape], [],
                level_sums, in_vmem(residual), in_vmem(shift), in_vmem(vt), in_vmem(grad), after=[far_own[2], far_other[0]],
            )
        own_grad = summed_over_col(plus(own_part, along_pix(other_part, 1)))
        other_grad = along_pix(own_grad, 1)
        change, sums = call(
            functools.partial(change_kernel, col_count), [VMEM] * 4, [VMEM] * 2,
            [local, sums_shape], factor_scratch, own_grad, other_grad, in_vmem(vt), in_vmem(weight),
            beside=[residual],
        )
        pix_sums = everywhere(sums)
        u_next, other_u, residual, own_u, even, odd = call(
            functools.partial(pix_step_kernel, total, first), [VMEM] * 8, [VMEM] * 6,
            [pix_shape, pix_shape, local, pix_shape, half_shape, half_shape], [pltpu.VMEM((rank, 3 * both), bf16)],
            level_sums, pix_sums, own_u, other_u, own_grad, other_grad, in_vmem(residual),
            in_vmem(change), after=passed, beside=[vt, weight],
        )
        if first:
            near_own[1] = held_until(near_own[1], odd)
            far_own[1] = to_far(near_own[1])

            def meanwhile(moved):
                near_own[2] = to_near(held_until(own_pieces[2], moved), 0)
                near_other[0] = to_near(held_until(other_pieces[0], moved), 1)
                near_other[1] = to_near(held_until(other_pieces[1], moved), 1)
                return [], [far_own[1], near_own[2], near_other[0]]

        else:
            near_other[2] = held_until(near_other[2], odd)
            far_other[2] = to_far(near_other[2])
            sent = []

            def meanwhile(moved):
                sent.append(held_until(own_u, moved))
                sent.append(to_near(sent[0], 0))
                return [], [far_other[2], sent[1]]

            other_vt = along_pix(vt, 1)
        summed = summed_over_chips(even, odd, meanwhile)
        if first:
            near_own[2] = held_until(near_own[2], summed[6])
            near_other[0] = held_until(near_other[0], summed[6])
            far_own[2] = to_far(near_own[2])
            far_other[0] = to_far(near_other[0])
            passed = near_other[1:2]
        else:
            own_u = sent[0]
            near_u = held_until(sent[1], summed[6])
            far_u = to_far(near_u)
            passed = [far_u]
        shift, grad, sums = call(
            functools.partial(shift_kernel, chips), [VMEM] * (4 + GROUP), [VMEM] * 3,
            [local, vt_shape, sums_shape], factor_scratch, own_u, other_u, in_vmem(weight), in_vmem(residual),
            *summed, after=passed, beside=[vt],
        )
        if first:
            level_sums = everywhere(sums)

    near_other_u = along_pix(near_u, 1)
    rim_scratch = [pltpu.VMEM((2 * both, 3 * rank), bf16)]
    rim_shape = pltpu.VMEM((4, pixels, half), f32)

    def rim(group_sums):
        far = held_until(far_u, group_sums)
        factors = [near_u, near_other_u, far, along_pix(far, 1)]
        other_grad = along_pix(held_until(grad, group_sums), 1)
        return factors, other_grad, *call(
            rim_kernel, [SMEM] + [VMEM] * 17, [VMEM] * 2, [rim_shape] * 2, rim_scratch,
            place, *near_own, *near_other, *far_own, *far_other, *factors, in_vmem(vt), after=[group_sums],
        )

    level_sums, (factors, other_grad, rim_res, rim_weight) = everywhere(sums, beside=rim)
    pair = lambda s, t: s[1] // 2 ^ t
    own_cloud, other_cloud, v = call(
        functools.partial(smooth_kernel, total, chips), [VMEM] * 13,
        [
            pl.BlockSpec((pixels, wide), lambda t, s: (0, s[0] * steps + pair(s, t))),
            pl.BlockSpec((pixels, wide), lambda t, s: (0, pair(s, t))),
            pl.BlockSpec((2, wide, rank), lambda t, s: (0, pair(s, t), 0)),
        ],
        [shaped(pixels, columns), shaped(pixels, half), shaped(2, half, rank)],
        rim_scratch + [
            pltpu.VMEM((4, pixels, wide), f32),
            pltpu.VMEM((6, pixels + 2 * PAD, LANES), f32),
            pltpu.VMEM((4, pixels + 2 * PAD, LANES), f32),
        ],
        level_sums, in_vmem(residual.reshape(2, pixels, half)), in_vmem(shift.reshape(2, pixels, half)),
        in_vmem(rim_res), in_vmem(rim_weight), *factors, in_vmem(vt), other_vt, in_vmem(grad),
        other_grad, grid=(steps,), place=place,
    )
    from_other = along_pix(other_cloud, 1)
    cloud = lax.dynamic_update_slice(own_cloud, from_other, (0, (1 - core) * half))
    return u_next, v.reshape(columns, rank), cloud


def solution(mesh):
    in_specs = (P("pix", "col"), P("pix", "col"), P("pix", None), P("col", None))
    out_specs = (P("pix", None), P("col", None), P("pix", "col"))
    return jax.shard_map(
        per_device, mesh=mesh, in_specs=in_specs, out_specs=out_specs, check_vma=False
    )
```
